512 devices in a mesh: dp: 16 (over x, z_hi, core), fsdp: 32 (over y, z_lo).
Axes of the slice: x: 4, y: 4, z: 16 (z_hi: 2, z_lo: 8; z = z_hi * 8 + z_lo), core: 2. Of those that a mesh axis runs over, the one named last changes fastest.
Arguments:
- hidden_in: bfloat16 [131072, 4096], P(('dp', 'fsdp')), may hold values from -400 to 400, as said below
- key_grad: bfloat16 [131072, 512], P(('dp', 'fsdp')), may hold values from -6 to 6
- key_weight: bfloat16 [4096, 512], P('fsdp'), may hold values from -0.25 to 0.25
- norm_gain: float32 [4096], replicated, may hold values from 0.5 to 1.5
- head_order: int32 [512], replicated, may hold values from 0 to 511, each once
Outputs:
- fisher_served: bfloat16 [4096, 512], P(('dp', 'fsdp'))
- input_grad: bfloat16 [131072, 4096], P(('dp', 'fsdp'))
The draws below stay inside these ranges and needn't reach their ends.
Inputs may be any that keep to these rules, and one draw needn't show every extreme that they name: `hidden_in`: each row's magnitude and each feature's magnitude vary over about a factor of ten. `head_order`: a permutation of the key projection's output columns.
All inputs are finite; a program needn't handle non-finite values.
Results may differ from the reference program's by a relative error of at most 0.0095.
Values may be sent and summed in bfloat16 or wider, within the bound.
No kernel may reach another device: no remote copies, remote signals or barrier semaphores. Data moves between devices by JAX's collectives and lax.ppermute only.
A program may use at most 64 MiB of HBM per device.

```python
import math
import jax
import jax.numpy as jnp
from jax import lax

D = 4096
KVH = 4
HEAD = 128
SEQ_LEN = 256
TOKENS = 131072
N_DP = 16
N_FSDP = 32


def draw_hidden_in(key, part):
    key = jax.random.fold_in(key, 11)
    key_cols, key_rows, key_base = jax.random.split(key, 3)
    col_scale = jnp.exp(jax.random.uniform(key_cols, (1, D), jnp.float32) * math.log(10.0))
    row_scale = jnp.exp(jax.random.uniform(key_rows, (TOKENS, 1), jnp.float32) * math.log(10.0))
    base = jax.random.truncated_normal(key_base, -4.0, 4.0, (TOKENS, D), jnp.float32)
    return (base * col_scale * row_scale).astype(jnp.bfloat16)


def levels(key, extent, cuts, smallest, largest):
    def one(dim, shards_of):
        draws = jax.random.uniform(jax.random.fold_in(jax.random.fold_in(key, 6), dim), (shards_of,), jnp.float32, smallest / len(cuts), largest / len(cuts))
        return jnp.repeat(jnp.exp(draws), extent[dim] // shards_of).reshape((-1,) + (1,) * (len(extent) - dim - 1))

    gain = one(*cuts[0])
    for cut in cuts[1:]:
        gain = gain * one(*cut)
    return gain


def gaussian(stream_key, dims, width, reach, cuts=(), dtype=jnp.bfloat16):
    drawn = width * jax.random.normal(stream_key, dims, jnp.float32)
    if cuts:
        drawn = drawn * levels(stream_key, dims, cuts, -0.22, 0.18)
    return jnp.clip(drawn, -reach, reach).astype(dtype)


def setup_inputs(seed: int = 0) -> dict:
    key_of = jax.random.split(jax.random.key(seed), 6)
    return {
        "hidden_in": draw_hidden_in(jax.random.fold_in(key_of[5], 71), 0),
        "key_grad": gaussian(key_of[1], (TOKENS, KVH * HEAD), 1.0, 6.0, ((0, 512),)),
        "key_weight": gaussian(key_of[2], (D, KVH * HEAD), (KVH * HEAD) ** -0.5, 0.25, ((0, 32),)),
        "norm_gain": jnp.clip(1.0 + 0.1 * jax.random.normal(key_of[3], (D,), jnp.float32), 0.5, 1.5),
        "head_order": jax.random.permutation(key_of[4], KVH * HEAD).astype(jnp.int32),
    }


def reference(hidden_in, key_grad, key_weight, norm_gain, head_order):
    values = hidden_in.astype(jnp.float32)
    square_mean = lax.optimization_barrier(jnp.mean(values * values, axis=-1, keepdims=True))
    inverse_rms = lax.rsqrt(square_mean + 1e-06)
    unit_rows = values * inverse_rms
    normed = (unit_rows * norm_gain).astype(jnp.bfloat16)
    scale_factor = 1.0 / TOKENS
    width_out = KVH * HEAD
    normed_groups = normed.reshape(N_DP, N_FSDP, SEQ_LEN, D)
    grad_groups = key_grad.reshape(N_DP, N_FSDP, SEQ_LEN, width_out)

    def per_group(total, pair):
        normed_part, grad_part = pair
        gradient = jnp.einsum('stc,stk->sck', normed_part.astype(jnp.float32), grad_part.astype(jnp.float32))
        seq_terms = (gradient * gradient * scale_factor).astype(jnp.bfloat16)
        seq_terms = lax.optimization_barrier(seq_terms)
        group_fisher = lax.optimization_barrier(jnp.sum(seq_terms.astype(jnp.float32), axis=0)).astype(jnp.bfloat16)
        return (total + group_fisher.astype(jnp.float32), None)
    total, unused = lax.scan(per_group, jnp.zeros((D, width_out), jnp.float32), (normed_groups, grad_groups))
    fisher = total.astype(jnp.bfloat16)
    fisher_served = fisher[:, head_order.astype(jnp.int32)]
    back = jnp.dot(key_grad, key_weight.T, preferred_element_type=jnp.float32)
    grad_unit = back * norm_gain
    input_grad = inverse_rms * (grad_unit - unit_rows * lax.optimization_barrier(jnp.mean(grad_unit * unit_rows, axis=-1, keepdims=True)))
    return (fisher_served, input_grad.astype(jnp.bfloat16))
```

```python
import jax
import jax.numpy as jnp
from jax import lax
from jax.experimental import pallas as pl
from jax.experimental.pallas import tpu as pltpu
from jax.sharding import PartitionSpec as P

AXES = ("dp", "fsdp")
NX, NZH, NC, NY, NZL = 4, 2, 2, 4, 8
D, K = 4096, 512
SEQ = 256
TOKENS = SEQ * NX * NZH * NC * NY * NZL
COLS = 256
GRAD_ROWS = 1024
PIECE = 32
BLOCK = NZL * PIECE
ROWS = GRAD_ROWS + BLOCK
BF16, F32 = jnp.bfloat16, jnp.float32


def device(x, zh, c, y, zl):
    return (((x * NZH + zh) * NC + c) * NY + y) * NZL + zl


def ring_groups(first):
    groups = []
    for zh in range(NZH):
        for zl in range(NZL):
            groups += [[device(x, zh, first, y, zl) for x in range(NX)] for y in range(NY)]
            groups += [[device(x, zh, 1 - first, y, zl) for y in range(NY)] for x in range(NX)]
    return groups


Z_LINES = [
    [device(x, zh, c, y, zl) for zl in range(NZL)]
    for x in range(NX)
    for zh in range(NZH)
    for c in range(NC)
    for y in range(NY)
]
Z_RINGS = [
    [device(x, zh, c, y, zl) for zh in range(NZH) for zl in range(NZL)]
    for x in range(NX)
    for c in range(NC)
    for y in range(NY)
]
CORE_SWAP = [
    (device(x, zh, c, y, zl), device(x, zh, 1 - c, y, zl))
    for x in range(NX)
    for zh in range(NZH)
    for c in range(NC)
    for y in range(NY)
    for zl in range(NZL)
]


def exchange(value, groups):
    return lax.all_to_all(
        value, AXES, split_axis=0, concat_axis=0, axis_index_groups=groups, tiled=True
    )


def call(kernel, outs, *args, grid=None, in_specs=None, out_specs=None, scratch=(), mib=24):
    whole = pl.BlockSpec(memory_space=pltpu.VMEM)
    kwargs = {}
    if grid is not None:
        kwargs["grid"] = grid
    return pl.pallas_call(
        kernel,
        out_shape=outs,
        in_specs=in_specs or [pl.BlockSpec(memory_space=pltpu.SMEM)] + [whole] * (len(args) - 1),
        out_specs=out_specs or jax.tree.map(lambda _: whole, outs),
        scratch_shapes=list(scratch),
        compiler_params=pltpu.CompilerParams(vmem_limit_bytes=mib * 2**20),
        **kwargs,
    )(*args)


def shape(dims, dtype=BF16):
    return jax.ShapeDtypeStruct(dims, dtype)


def norm_kernel(core_ref, hidden_ref, key_ref, gain_ref, own_ref, send_ref, inv_ref):
    core = core_ref[0]
    step = 16

    def rows_of(i, carry):
        rows = pl.ds(pl.multiple_of(i * step, step), step)
        values = hidden_ref[rows, :].astype(F32)
        inv = lax.rsqrt(jnp.sum(values * values, axis=-1, keepdims=True) * (1.0 / D) + 1e-06)
        inv_ref[rows, :] = jnp.broadcast_to(inv, (step, 128))
        for ref, part in ((own_ref, core), (send_ref, 1 - core)):
            for k in range(NX * NZH):
                cols = pl.ds(pl.multiple_of((2 * k + part) * COLS, COLS), COLS)
                unit = hidden_ref[rows, cols].astype(F32) * inv
                ref[k, rows, :] = (unit * gain_ref[:, cols]).astype(BF16)
        return carry

    lax.fori_loop(0, hidden_ref.shape[0] // step, rows_of, 0)
    for half in range(2):
        send_ref[NX * NZH + half] = key_ref[:, half * COLS : (half + 1) * COLS]


def square_kernel(core_ref, own_ref, other_ref, key_ref, weight_ref, out_ref):
    core = core_ref[0]
    over_tokens = (((0,), (0,)), ((), ()))

    def block(k, carry):
        x, zh = k // NZH, k % NZH
        outer = jnp.where(core == 0, x, 0)
        for half in range(2):
            cols = slice(half * COLS, (half + 1) * COLS)
            g0 = lax.dot_general(
                own_ref[k], key_ref[:, cols], over_tokens, preferred_element_type=F32
            )
            g1 = lax.dot_general(
                other_ref[k], other_ref[NX * NZH + half], over_tokens, preferred_element_type=F32
            )
            total = ((g0 * g0 + g1 * g1) * (1.0 / TOKENS)).astype(BF16)
            for y in range(NY):
                chunk = jnp.where(core == 0, outer, y)
                inner = jnp.where(core == 0, y, x)
                start = inner * 256 + zh * 128 + half * 64
                out_ref[chunk, pl.ds(pl.multiple_of(start, 64), 64), :] = total[
                    y * 64 : (y + 1) * 64
                ]
        return carry

    lax.fori_loop(0, NX * NZH, block, 0)
    for chunk in range(4):
        out_ref[chunk, GRAD_ROWS:, :] = weight_ref[...]


def middle_kernel(in_ref, out_ref):
    for b in range(4):
        rows = slice(b * 256, (b + 1) * 256)
        total = in_ref[0, rows, :].astype(F32)
        for j in range(1, 4):
            total += in_ref[j, rows, :].astype(F32)
        out_ref[b, 0:256, :] = total.astype(BF16)
        for j in range(4):
            out_ref[b, 256 + j * BLOCK : 256 + (j + 1) * BLOCK, :] = in_ref[j, GRAD_ROWS:, :]


def split_kernel(in_ref, out_ref):
    total = in_ref[0, 0:256, :].astype(F32)
    for j in range(1, 4):
        total += in_ref[j, 0:256, :].astype(F32)
    total = total.reshape(NZH, 2, NZL, 8, COLS)
    for zh in range(NZH):
        for zl in range(NZL):
            rows = jnp.concatenate([total[zh, 0, zl], total[zh, 1, zl]], axis=0)
            out_ref[zh * NZL + zl] = rows.astype(BF16)


def serve_kernel(order_ref, in_ref, out_ref):
    total = in_ref[0].astype(F32)
    for z in range(1, NZH * NZL):
        total += in_ref[z].astype(F32)
    fisher = jnp.concatenate([total[0:8], total[8:16]], axis=1).astype(BF16)
    column = lax.broadcasted_iota(jnp.int32, (K, K), 0)
    pick = jnp.where(column == order_ref[...], 1.0, 0.0).astype(BF16)
    out_ref[...] = jnp.dot(fisher, pick, preferred_element_type=F32).astype(BF16)


def input_kernel(
    core_ref, hidden_ref, key_ref, gain_ref, inv_ref, own_ref, other_ref, out_ref, du_ref
):
    core = core_ref[0]
    key_own = key_ref[:, pl.ds(pl.multiple_of(core * COLS, COLS), COLS)]
    key_other = key_ref[:, pl.ds(pl.multiple_of((1 - core) * COLS, COLS), COLS)]
    inv = inv_ref[:, 0:1]
    over_cols = (((1,), (1,)), ((), ()))

    def rows_of(ref, y, zl, x, along_y):
        a = jnp.where(along_y, y, x)
        b = jnp.where(along_y, x, y)
        start = pl.multiple_of(256 + b * BLOCK + zl * PIECE, PIECE)
        return ref[a, pl.ds(start, PIECE), :]

    def forward(t, acc):
        y, pair = t // 4, t % 4
        places = [(2 * pair + i, x) for i in range(2) for x in range(NX)]
        own = jnp.concatenate([rows_of(own_ref, y, zl, x, core == 0) for zl, x in places], axis=0)
        other = jnp.concatenate(
            [rows_of(other_ref, y, zl, x, core != 0) for zl, x in places], axis=0
        )
        back = lax.dot_general(key_own, own, over_cols, preferred_element_type=F32)
        back += lax.dot_general(key_other, other, over_cols, preferred_element_type=F32)
        cols = pl.ds(pl.multiple_of(t * 256, 256), 256)
        du = back * gain_ref[:, cols]
        du_ref[:, cols] = du
        both = du * (hidden_ref[:, cols].astype(F32) * inv)
        return acc + both[:, :128] + both[:, 128:]

    acc = lax.fori_loop(0, D // 256, forward, jnp.zeros((SEQ, 128), F32))
    mean = jnp.sum(acc, axis=-1, keepdims=True) * (1.0 / D)

    def finish(t, carry):
        cols = pl.ds(pl.multiple_of(t * 256, 256), 256)
        unit = hidden_ref[:, cols].astype(F32) * inv
        out_ref[:, cols] = (inv * (du_ref[:, cols] - unit * mean)).astype(BF16)
        return carry

    lax.fori_loop(0, D // 256, finish, 0)


def body(hidden_in, key_grad, key_weight, norm_gain, head_order):
    dp = lax.axis_index("dp")
    x, core = lax.div(dp, NZH * NC), lax.rem(dp, NC)
    core_id = core.reshape(1).astype(jnp.int32)
    gain = norm_gain.reshape(1, D)

    with jax.named_scope("norm"):
        rows = 64
        blocks = NX * NZH
        own, send, inv = call(
            norm_kernel,
            (shape((blocks, SEQ, COLS)), shape((blocks + 2, SEQ, COLS)), shape((SEQ, 128), F32)),
            core_id,
            hidden_in,
            key_grad,
            gain,
            grid=(SEQ // rows,),
            in_specs=[
                pl.BlockSpec(memory_space=pltpu.SMEM),
                pl.BlockSpec((rows, D), lambda i: (i, 0)),
                pl.BlockSpec((rows, K), lambda i: (i, 0)),
                pl.BlockSpec((1, D), lambda i: (0, 0)),
            ],
            out_specs=(
                pl.BlockSpec((blocks, rows, COLS), lambda i: (0, i, 0)),
                pl.BlockSpec((blocks + 2, rows, COLS), lambda i: (0, i, 0)),
                pl.BlockSpec((rows, 128), lambda i: (i, 0)),
            ),
        )
    with jax.named_scope("weight_z"):
        piece = lax.dynamic_slice(key_weight, (x * PIECE, core * COLS), (PIECE, COLS))
        piece, send = lax.optimization_barrier((piece, send))
        other = lax.ppermute(send, AXES, CORE_SWAP)
        gathered = exchange(jnp.broadcast_to(piece, (NZL, PIECE, COLS)), Z_LINES)
    with jax.named_scope("squares"):
        chunks = call(
            square_kernel,
            shape((4, ROWS, COLS)),
            core_id,
            own,
            other,
            key_grad,
            gathered.reshape(BLOCK, COLS),
        )
    with jax.named_scope("ring_a"):
        first = exchange(chunks, ring_groups(0))
    with jax.named_scope("middle"):
        whole = pl.BlockSpec(memory_space=pltpu.VMEM)
        chunks = call(middle_kernel, shape((4, ROWS, COLS)), first, in_specs=[whole])
    with jax.named_scope("ring_b"):
        second = exchange(chunks, ring_groups(1))
    with jax.named_scope("weight_swap"):
        swapped = lax.ppermute(second, AXES, CORE_SWAP)
    with jax.named_scope("ring_z"):
        parts = call(split_kernel, shape((NZH * NZL, 16, COLS)), second, in_specs=[whole])
        parts = exchange(parts, Z_RINGS)
    with jax.named_scope("serve"):
        served = call(
            serve_kernel,
            shape((8, K)),
            head_order.reshape(1, K),
            parts,
            in_specs=[whole, whole],
        )
    with jax.named_scope("input_grad"):
        input_grad = call(
            input_kernel,
            shape((SEQ, D)),
            core_id,
            hidden_in,
            key_grad,
            gain,
            inv,
            second,
            swapped,
            scratch=[pltpu.VMEM((SEQ, D), F32)],
            mib=32,
        )
    return served, input_grad


def solution(mesh):
    in_specs = (P(AXES, None), P(AXES, None), P("fsdp", None), P(), P())
    out_specs = (P(AXES, None), P(AXES, None))
    return jax.shard_map(body, mesh=mesh, in_specs=in_specs, out_specs=out_specs, check_vma=False)
```

```python
import jax
import jax.numpy as jnp
from jax import lax
from jax.experimental import pallas as pl
from jax.experimental.pallas import tpu as pltpu
from jax.sharding import PartitionSpec as P

AXES = ("dp", "fsdp")
NX, NZH, NC, NY, NZL = 4, 2, 2, 4, 8
D, K = 4096, 512
SEQ = 256
TOKENS = SEQ * NX * NZH * NC * NY * NZL
COLS = 256
BF16, F32 = jnp.bfloat16, jnp.float32


def device(x, zh, c, y, zl):
    return (((x * NZH + zh) * NC + c) * NY + y) * NZL + zl


def places():
    return [
        (x, zh, c, y, zl)
        for x in range(NX)
        for zh in range(NZH)
        for c in range(NC)
        for y in range(NY)
        for zl in range(NZL)
    ]


def ring_groups(first):
    groups = []
    for zh in range(NZH):
        for zl in range(NZL):
            groups += [[device(x, zh, first, y, zl) for x in range(NX)] for y in range(NY)]
            groups += [[device(x, zh, 1 - first, y, zl) for y in range(NY)] for x in range(NX)]
    return groups


def from_z(distance):
    pairs = []
    for x, zh, c, y, zl in places():
        z = (zh * NZL + zl + (distance if c == 0 else -distance)) % (NZH * NZL)
        pairs.append((device(x, z // NZL, c, y, z % NZL), device(x, zh, c, y, zl)))
    return pairs


Y_RINGS = [
    [device(x, zh, c, y, zl) for y in range(NY)]
    for x in range(NX)
    for zh in range(NZH)
    for c in range(NC)
    for zl in range(NZL)
]
Z_RINGS = [
    [device(x, zh, c, y, zl) for zh in range(NZH) for zl in range(NZL)]
    for x in range(NX)
    for c in range(NC)
    for y in range(NY)
]
CORE_SWAP = [(device(x, zh, c, y, zl), device(x, zh, 1 - c, y, zl)) for x, zh, c, y, zl in places()]


def exchange(value, groups):
    return lax.all_to_all(
        value, AXES, split_axis=0, concat_axis=0, axis_index_groups=groups, tiled=True
    )


def call(kernel, outs, ins, in_spaces, out_spaces, scratch=(), mib=24):
    return pl.pallas_call(
        kernel,
        out_shape=outs,
        in_specs=[pl.BlockSpec(memory_space=space) for space in in_spaces],
        out_specs=jax.tree.map(lambda space: pl.BlockSpec(memory_space=space), out_spaces),
        scratch_shapes=list(scratch),
        compiler_params=pltpu.CompilerParams(vmem_limit_bytes=mib * 2**20),
    )(*ins)


def my_core():
    return lax.rem(lax.axis_index("dp"), NC)


def shape(dims, dtype=BF16):
    return jax.ShapeDtypeStruct(dims, dtype)


def norm_kernel(
    hidden_hbm, key_hbm, gain_hbm, own_ref, send_ref, inv_ref, hidden_ref, gain_ref, sems
):
    core = my_core()
    step, parts = 16, 4
    rows_each = SEQ // parts
    gain_copy = pltpu.make_async_copy(gain_hbm, gain_ref, sems.at[0])
    gain_copy.start()
    copies = []
    for i in range(parts):
        rows = pl.ds(i * rows_each, rows_each)
        copies.append(
            pltpu.make_async_copy(hidden_hbm.at[rows], hidden_ref.at[rows], sems.at[1 + i])
        )
        copies[-1].start()
    key_copies = []
    for half in range(2):
        source = key_hbm.at[:, pl.ds(half * COLS, COLS)]
        target = send_ref.at[NX * NZH + half]
        key_copies.append(pltpu.make_async_copy(source, target, sems.at[1 + parts + half]))
        key_copies[-1].start()

    def rows_of(i, carry):
        rows = pl.ds(pl.multiple_of(i * step, step), step)
        squares = jnp.zeros((step, 512), F32)
        for t in range(0, D, 512):
            values = hidden_ref[rows, t : t + 512].astype(F32)
            squares += values * values
        inv = lax.rsqrt(jnp.sum(squares, axis=-1, keepdims=True) * (1.0 / D) + 1e-06)
        inv_ref[rows, :] = jnp.broadcast_to(inv, (step, 128))
        for ref, part in ((own_ref, core), (send_ref, 1 - core)):
            for k in range(NX * NZH):
                cols = pl.ds(pl.multiple_of((2 * k + part) * COLS, COLS), COLS)
                unit = hidden_ref[rows, cols].astype(F32) * inv
                ref[k, rows, :] = (unit * gain_ref[:, cols]).astype(BF16)
        return carry

    gain_copy.wait()
    for i in range(parts):
        copies[i].wait()
        lax.fori_loop(i * rows_each // step, (i + 1) * rows_each // step, rows_of, 0)
    for copy in key_copies:
        copy.wait()


def piece_kernel(own_ref, far_ref, out_ref):
    cols = pl.ds(pl.multiple_of(my_core() * COLS, COLS), COLS)
    for y in range(NY):
        out_ref[y, 0:128, :] = own_ref[:, cols]
        out_ref[y, 128:256, :] = far_ref[:, cols]


def square_kernel(own_ref, other_ref, key_ref, out_ref):
    core = my_core()
    over_tokens = (((0,), (0,)), ((), ()))
    key_other = jnp.concatenate([other_ref[NX * NZH], other_ref[NX * NZH + 1]], axis=1)

    def block(k, carry):
        x, zh = k // NZH, k % NZH
        g0 = lax.dot_general(own_ref[k], key_ref[...], over_tokens, preferred_element_type=F32)
        g1 = lax.dot_general(other_ref[k], key_other, over_tokens, preferred_element_type=F32)
        total = ((g0 * g0 + g1 * g1) * (1.0 / TOKENS)).astype(BF16)
        for y in range(NY):
            chunk = jnp.where(core == 0, x, y)
            inner = jnp.where(core == 0, y, x)
            for half in range(2):
                start = pl.multiple_of(inner * 256 + zh * 128 + half * 64, 64)
                out_ref[chunk, pl.ds(start, 64), :] = total[
                    y * 64 : (y + 1) * 64, half * COLS : (half + 1) * COLS
                ]
        return carry

    lax.fori_loop(0, NX * NZH, block, 0)


def middle_kernel(in_ref, near_ref, far_ref, out_ref, weight_ref):
    for b in range(4):
        rows = slice(b * 256, (b + 1) * 256)
        total = in_ref[0, rows, :].astype(F32)
        for j in range(1, 4):
            total += in_ref[j, rows, :].astype(F32)
        out_ref[b] = total.astype(BF16)
        weight_ref[b] = near_ref[b]
        weight_ref[4 + b] = far_ref[b]


def split_kernel(in_ref, near_ref, far_ref, out_ref, weight_ref):
    total = in_ref[0].astype(F32)
    for j in range(1, 4):
        total += in_ref[j].astype(F32)
    total = total.reshape(NZH, 2, NZL, 8, COLS)
    for zh in range(NZH):
        for zl in range(NZL):
            rows = jnp.concatenate([total[zh, 0, zl], total[zh, 1, zl]], axis=0)
            out_ref[zh * NZL + zl] = rows.astype(BF16)
    for b in range(8):
        weight_ref[b] = near_ref[b]
        weight_ref[8 + b] = far_ref[b]


def serve_kernel(order_ref, in_ref, out_ref):
    total = in_ref[0].astype(F32)
    for z in range(1, NZH * NZL):
        total += in_ref[z].astype(F32)
    fisher = jnp.concatenate([total[0:8], total[8:16]], axis=1).astype(BF16)
    column = lax.broadcasted_iota(jnp.int32, (K, K), 0)
    pick = jnp.where(column == order_ref[...], 1.0, 0.0).astype(BF16)
    out_ref[...] = jnp.dot(fisher, pick, preferred_element_type=F32).astype(BF16)


def input_kernel(
    hidden_ref, key_ref, gain_ref, inv_ref, own_ref, other_ref, out_hbm, back_ref, out_ref, sems
):
    core = my_core()
    z_here = lax.rem(lax.axis_index("fsdp"), NZL)
    own_cols = pl.ds(pl.multiple_of(core * COLS, COLS), COLS)
    other_cols = pl.ds(pl.multiple_of((1 - core) * COLS, COLS), COLS)
    keys = jnp.concatenate([key_ref[:, own_cols], key_ref[:, other_cols]], axis=1)
    sign = 1 - 2 * core

    def shard(ref, y, zl, sign):
        away = (sign * (zl - z_here)) & (NZL - 1)
        index = (away & 1) * 8 + ((away >> 1) & 1) * 4 + y
        return ref[index, pl.ds(pl.multiple_of((away >> 2) * 128, 128), 128), :]

    def tile(t, carry):
        y, pair = t // 4, t % 4
        weight = jnp.concatenate(
            [
                jnp.concatenate(
                    [shard(own_ref, y, 2 * pair + i, sign), shard(other_ref, y, 2 * pair + i, -sign)],
                    axis=1,
                )
                for i in range(2)
            ],
            axis=0,
        )
        cols = pl.ds(pl.multiple_of(t * 256, 256), 256)
        back_ref[:, cols] = lax.dot_general(
            keys, weight, (((1,), (1,)), ((), ())), preferred_element_type=F32
        )
        return carry

    lax.fori_loop(0, D // 256, tile, 0)

    step, parts, width = 16, 4, 512

    def rows_of(i, carry):
        rows = pl.ds(pl.multiple_of(i * step, step), step)
        inv = inv_ref[rows, 0:1]
        total = jnp.zeros((step, width), F32)
        for t in range(0, D, width):
            cols = slice(t, t + width)
            du = back_ref[rows, cols] * gain_ref[:, cols]
            total += du * hidden_ref[rows, cols].astype(F32)
        mean = inv * jnp.sum(total, axis=-1, keepdims=True) * (1.0 / D)
        factor = inv * inv * mean
        for t in range(0, D, width):
            cols = slice(t, t + width)
            du = back_ref[rows, cols] * gain_ref[:, cols]
            out = du * inv - hidden_ref[rows, cols].astype(F32) * factor
            out_ref[rows, cols] = out.astype(BF16)
        return carry

    rows_each = SEQ // parts
    copies = []
    for i in range(parts):
        lax.fori_loop(i * rows_each // step, (i + 1) * rows_each // step, rows_of, 0)
        rows = pl.ds(i * rows_each, rows_each)
        copies.append(pltpu.make_async_copy(out_ref.at[rows], out_hbm.at[rows], sems.at[i]))
        copies[-1].start()
    for copy in copies:
        copy.wait()


def body(hidden_in, key_grad, key_weight, norm_gain, head_order):
    gain = norm_gain.reshape(1, D)
    vmem, hbm = pltpu.VMEM, pltpu.HBM

    with jax.named_scope("weight_z4"):
        far = lax.ppermute(key_weight, AXES, from_z(4))
    with jax.named_scope("norm"):
        blocks = NX * NZH
        own, send, inv = call(
            norm_kernel,
            (shape((blocks, SEQ, COLS)), shape((blocks + 2, SEQ, COLS)), shape((SEQ, 128), F32)),
            (hidden_in, key_grad, gain),
            (hbm, hbm, hbm),
            (vmem, vmem, vmem),
            [pltpu.VMEM((SEQ, D), BF16), pltpu.VMEM((1, D), F32), pltpu.SemaphoreType.DMA((7,))],
        )
        far, send = lax.optimization_barrier((far, send))
        other = lax.ppermute(send, AXES, CORE_SWAP)
    with jax.named_scope("weight_y"):
        pieces = call(
            piece_kernel, shape((NY, 256, COLS)), (key_weight, far), (vmem, vmem), vmem
        )
        near = exchange(pieces, Y_RINGS)
    with jax.named_scope("weight_z2"):
        far = lax.ppermute(near, AXES, from_z(2))
    with jax.named_scope("squares"):
        chunks = call(
            square_kernel, shape((4, 1024, COLS)), (own, other, key_grad), (vmem,) * 3, vmem
        )
    with jax.named_scope("ring_a"):
        chunks = exchange(chunks, ring_groups(0))
    with jax.named_scope("middle"):
        chunks, near = call(
            middle_kernel,
            (shape((4, 256, COLS)), shape((8, 256, COLS))),
            (chunks, near, far),
            (vmem,) * 3,
            (vmem, vmem),
        )
    with jax.named_scope("weight_z1"):
        far = lax.ppermute(near, AXES, from_z(1))
    with jax.named_scope("ring_b"):
        chunks = exchange(chunks, ring_groups(1))
    with jax.named_scope("split"):
        parts, weight_own = call(
            split_kernel,
            (shape((NZH * NZL, 16, COLS)), shape((16, 256, COLS))),
            (chunks, near, far),
            (vmem,) * 3,
            (vmem, vmem),
        )
    with jax.named_scope("weight_swap"):
        weight_other = lax.ppermute(weight_own, AXES, CORE_SWAP)
    with jax.named_scope("ring_z"):
        parts = exchange(parts, Z_RINGS)
    with jax.named_scope("serve"):
        served = call(
            serve_kernel, shape((8, K)), (head_order.reshape(1, K), parts), (vmem, vmem), vmem
        )
    with jax.named_scope("input_grad"):
        input_grad = call(
            input_kernel,
            shape((SEQ, D)),
            (hidden_in, key_grad, gain, inv, weight_own, weight_other),
            (vmem,) * 6,
            hbm,
            [
                pltpu.VMEM((SEQ, D), F32),
                pltpu.VMEM((SEQ, D), BF16),
                pltpu.SemaphoreType.DMA((4,)),
            ],
            mib=32,
        )
    return served, input_grad


def solution(mesh):
    in_specs = (P(AXES, None), P(AXES, None), P("fsdp", None), P(), P())
    out_specs = (P(AXES, None), P(AXES, None))
    return jax.shard_map(body, mesh=mesh, in_specs=in_specs, out_specs=out_specs, check_vma=False)
```

```python
import jax
import jax.numpy as jnp
from jax import lax
from jax.experimental import pallas as pl
from jax.experimental.pallas import tpu as pltpu
from jax.sharding import PartitionSpec as P

AXES = ("dp", "fsdp")
NX, NZH, NC, NY, NZL = 4, 2, 2, 4, 8
D, K = 4096, 512
SEQ = 256
TOKENS = SEQ * NX * NZH * NC * NY * NZL
COLS = 256
BF16, F32 = jnp.bfloat16, jnp.float32


def device(x, zh, c, y, zl):
    return (((x * NZH + zh) * NC + c) * NY + y) * NZL + zl


def places():
    return [
        (x, zh, c, y, zl)
        for x in range(NX)
        for zh in range(NZH)
        for c in range(NC)
        for y in range(NY)
        for zl in range(NZL)
    ]


def ring_groups(first):
    groups = []
    for zh in range(NZH):
        for zl in range(NZL):
            groups += [[device(x, zh, first, y, zl) for x in range(NX)] for y in range(NY)]
            groups += [[device(x, zh, 1 - first, y, zl) for y in range(NY)] for x in range(NX)]
    return groups


def from_z(distance):
    pairs = []
    for x, zh, c, y, zl in places():
        z = (zh * NZL + zl + (distance if c == 0 else -distance)) % (NZH * NZL)
        pairs.append((device(x, z // NZL, c, y, z % NZL), device(x, zh, c, y, zl)))
    return pairs


Y_RINGS = [
    [device(x, zh, c, y, zl) for y in range(NY)]
    for x in range(NX)
    for zh in range(NZH)
    for c in range(NC)
    for zl in range(NZL)
]
Z_RINGS = [
    [device(x, zh, c, y, zl) for zh in range(NZH) for zl in range(NZL)]
    for x in range(NX)
    for c in range(NC)
    for y in range(NY)
]
CORE_SWAP = [(device(x, zh, c, y, zl), device(x, zh, 1 - c, y, zl)) for x, zh, c, y, zl in places()]


def exchange(value, groups):
    return lax.all_to_all(
        value, AXES, split_axis=0, concat_axis=0, axis_index_groups=groups, tiled=True
    )


def call(kernel, outs, ins, in_spaces, out_spaces, scratch=(), mib=24, us=1.0):
    return pl.pallas_call(
        kernel,
        out_shape=outs,
        in_specs=[pl.BlockSpec(memory_space=space) for space in in_spaces],
        out_specs=jax.tree.map(lambda space: pl.BlockSpec(memory_space=space), out_spaces),
        scratch_shapes=list(scratch),
        compiler_params=pltpu.CompilerParams(vmem_limit_bytes=mib and mib * 2**20),
        cost_estimate=pl.CostEstimate(
            flops=0, bytes_accessed=int(us * 3.0e6), transcendentals=0
        ),
    )(*ins)


def my_core():
    return lax.rem(lax.axis_index("dp"), NC)


def shape(dims, dtype=BF16):
    return jax.ShapeDtypeStruct(dims, dtype)


def start(source, target, sem):
    copy = pltpu.make_async_copy(source, target, sem)
    copy.start()
    return copy


def norm_kernel(
    hidden_hbm, key_hbm, gain_hbm, own_hbm, send_hbm, inv_hbm,
    hidden_ref, key_ref, gain_ref, own_ref, send_ref, inv_ref, in_sems, out_sems,
):
    core = my_core()
    step, parts, blocks = 16, 4, NX * NZH
    rows_each = SEQ // parts
    pieces = [pl.ds(i * rows_each, rows_each) for i in range(parts)]
    gain_copy = start(gain_hbm, gain_ref, in_sems.at[parts])
    copies = [
        start(hidden_hbm.at[rows], hidden_ref.at[rows], in_sems.at[i])
        for i, rows in enumerate(pieces)
    ]
    key_copy = start(key_hbm, key_ref, in_sems.at[parts + 1])

    def rows_of(i, carry):
        rows = pl.ds(pl.multiple_of(i * step, step), step)
        squares = jnp.zeros((step, 512), F32)
        for t in range(0, D, 512):
            values = hidden_ref[rows, t : t + 512].astype(F32)
            squares += values * values
        inv = lax.rsqrt(jnp.sum(squares, axis=-1, keepdims=True) * (1.0 / D) + 1e-06)
        inv_ref[rows, :] = jnp.broadcast_to(inv, (step, 128))
        for ref, part in ((own_ref, core), (send_ref, 1 - core)):
            for k in range(blocks):
                cols = pl.ds(pl.multiple_of((2 * k + part) * COLS, COLS), COLS)
                unit = hidden_ref[rows, cols].astype(F32) * inv
                ref[k, rows, :] = (unit * gain_ref[:, cols]).astype(BF16)
        return carry

    gain_copy.wait()
    out_copies = []
    for i, rows in enumerate(pieces):
        copies[i].wait()
        lax.fori_loop(i * rows_each // step, (i + 1) * rows_each // step, rows_of, 0)
        out_copies += [
            start(send_ref.at[:, rows], send_hbm.at[pl.ds(0, blocks), rows], out_sems.at[2 * i]),
            start(own_ref.at[:, rows], own_hbm.at[:, rows], out_sems.at[2 * i + 1]),
        ]
    key_copy.wait()
    for half in range(2):
        source = key_ref.at[:, pl.ds(half * COLS, COLS)]
        out_copies.append(start(source, send_hbm.at[blocks + half], out_sems.at[2 * parts + half]))
    out_copies.append(start(inv_ref, inv_hbm, out_sems.at[2 * parts + 2]))
    for copy in out_copies:
        copy.wait()


def piece_kernel(own_hbm, far_hbm, out_hbm, sems):
    cols = pl.ds(pl.multiple_of(my_core() * COLS, COLS), COLS)
    copies = []
    for y in range(NY):
        for i, source in enumerate((own_hbm, far_hbm)):
            target = out_hbm.at[y, pl.ds(i * 128, 128)]
            copies.append(start(source.at[:, cols], target, sems.at[2 * y + i]))
    for copy in copies:
        copy.wait()


def square_kernel(
    own_hbm, other_hbm, key_hbm, out_hbm, own_ref, other_ref, key_ref, out_ref, in_sems, out_sems
):
    core = my_core()
    blocks = NX * NZH
    over_tokens = (((0,), (0,)), ((), ()))
    keys = [
        start(key_hbm, key_ref, in_sems.at[0]),
        start(other_hbm.at[pl.ds(blocks, 2)], other_ref.at[pl.ds(blocks, 2)], in_sems.at[1]),
    ]
    copies = []
    for part in range(4):
        some = pl.ds(2 * part, 2)
        copies += [
            start(own_hbm.at[some], own_ref.at[some], in_sems.at[2 + 2 * part]),
            start(other_hbm.at[some], other_ref.at[some], in_sems.at[3 + 2 * part]),
        ]
    for copy in keys:
        copy.wait()
    key_other = jnp.concatenate([other_ref[blocks], other_ref[blocks + 1]], axis=1)

    out_copies = []
    for k in range(blocks):
        x, zh = k // NZH, k % NZH
        if zh == 0:
            copies[2 * x].wait()
            copies[2 * x + 1].wait()
        g0 = lax.dot_general(own_ref[k], key_ref[...], over_tokens, preferred_element_type=F32)
        g1 = lax.dot_general(other_ref[k], key_other, over_tokens, preferred_element_type=F32)
        total = ((g0 * g0 + g1 * g1) * (1.0 / TOKENS)).astype(BF16)
        for y in range(NY):
            rows = slice(y * 64, (y + 1) * 64)
            out_ref[k, y, 0:64, :] = total[rows, 0:COLS]
            out_ref[k, y, 64:128, :] = total[rows, COLS:K]
            chunk = jnp.where(core == 0, x, y)
            place = pl.multiple_of(jnp.where(core == 0, y, x) * 256 + zh * 128, 128)
            target = out_hbm.at[chunk, pl.ds(place, 128)]
            out_copies.append(start(out_ref.at[k, y], target, out_sems.at[k, y]))
    for copy in out_copies:
        copy.wait()


def middle_kernel(in_ref, out_ref):
    for b in range(4):
        rows = slice(b * 256, (b + 1) * 256)
        total = in_ref[0, rows, :].astype(F32)
        for j in range(1, 4):
            total += in_ref[j, rows, :].astype(F32)
        out_ref[b] = total.astype(BF16)


def join_kernel(near_hbm, far_hbm, out_hbm, sems):
    copies = [
        start(near_hbm, out_hbm.at[pl.ds(0, 4)], sems.at[0]),
        start(far_hbm, out_hbm.at[pl.ds(4, 4)], sems.at[1]),
    ]
    for copy in copies:
        copy.wait()


def split_kernel(in_ref, out_ref):
    total = in_ref[0].astype(F32)
    for j in range(1, 4):
        total += in_ref[j].astype(F32)
    total = total.reshape(NZH, 2, NZL, 8, COLS)
    for zh in range(NZH):
        for zl in range(NZL):
            rows = jnp.concatenate([total[zh, 0, zl], total[zh, 1, zl]], axis=0)
            out_ref[zh * NZL + zl] = rows.astype(BF16)


def serve_kernel(order_hbm, in_ref, out_ref, order_ref, sem):
    copy = start(order_hbm, order_ref, sem)
    total = in_ref[0].astype(F32)
    for z in range(1, NZH * NZL):
        total += in_ref[z].astype(F32)
    fisher = jnp.concatenate([total[0:8], total[8:16]], axis=1).astype(BF16)
    copy.wait()
    column = lax.broadcasted_iota(jnp.int32, (K, K), 0)
    pick = jnp.where(column == order_ref[...], 1.0, 0.0).astype(BF16)
    out_ref[...] = jnp.dot(fisher, pick, preferred_element_type=F32).astype(BF16)


def input_kernel(
    hidden_hbm, key_hbm, gain_hbm, inv_hbm, own_a, own_b, other_a, other_b, out_hbm,
    hidden_ref, key_ref, gain_ref, inv_ref, own_ref, other_ref, back_ref, out_ref,
    in_sems, out_sems,
):
    first = [
        start(key_hbm, key_ref, in_sems.at[0]),
        start(own_a, own_ref.at[pl.ds(0, 8)], in_sems.at[1]),
        start(other_a, other_ref.at[pl.ds(0, 8)], in_sems.at[2]),
        start(own_b, own_ref.at[pl.ds(8, 8)], in_sems.at[3]),
        start(other_b, other_ref.at[pl.ds(8, 8)], in_sems.at[4]),
    ]
    second = [
        start(gain_hbm, gain_ref, in_sems.at[5]),
        start(inv_hbm, inv_ref, in_sems.at[6]),
        start(hidden_hbm, hidden_ref, in_sems.at[7]),
    ]
    for copy in first:
        copy.wait()
    core = my_core()
    z_here = lax.rem(lax.axis_index("fsdp"), NZL)
    own_cols = pl.ds(pl.multiple_of(core * COLS, COLS), COLS)
    other_cols = pl.ds(pl.multiple_of((1 - core) * COLS, COLS), COLS)
    keys = jnp.concatenate([key_ref[:, own_cols], key_ref[:, other_cols]], axis=1)
    sign = 1 - 2 * core

    def shard(ref, y, zl, sign):
        away = (sign * (zl - z_here)) & (NZL - 1)
        index = (away & 1) * 8 + ((away >> 1) & 1) * 4 + y
        return ref[index, pl.ds(pl.multiple_of((away >> 2) * 128, 128), 128), :]

    def tile(t, carry):
        y, pair = t // 4, t % 4
        weight = jnp.concatenate(
            [
                jnp.concatenate(
                    [shard(own_ref, y, 2 * pair + i, sign), shard(other_ref, y, 2 * pair + i, -sign)],
                    axis=1,
                )
                for i in range(2)
            ],
            axis=0,
        )
        cols = pl.ds(pl.multiple_of(t * 256, 256), 256)
        back_ref[:, cols] = lax.dot_general(
            keys, weight, (((1,), (1,)), ((), ())), preferred_element_type=F32
        )
        return carry

    lax.fori_loop(0, D // 256, tile, 0)
    for copy in second:
        copy.wait()

    step, parts, width = 16, 4, 512

    def rows_of(i, carry):
        rows = pl.ds(pl.multiple_of(i * step, step), step)
        inv = inv_ref[rows, 0:1]
        total = jnp.zeros((step, width), F32)
        for t in range(0, D, width):
            cols = slice(t, t + width)
            du = back_ref[rows, cols] * gain_ref[:, cols]
            total += du * hidden_ref[rows, cols].astype(F32)
        mean = inv * jnp.sum(total, axis=-1, keepdims=True) * (1.0 / D)
        factor = inv * inv * mean
        for t in range(0, D, width):
            cols = slice(t, t + width)
            du = back_ref[rows, cols] * gain_ref[:, cols]
            out = du * inv - hidden_ref[rows, cols].astype(F32) * factor
            out_ref[rows, cols] = out.astype(BF16)
        return carry

    rows_each = SEQ // parts
    copies = []
    for i in range(parts):
        lax.fori_loop(i * rows_each // step, (i + 1) * rows_each // step, rows_of, 0)
        rows = pl.ds(i * rows_each, rows_each)
        copies.append(start(out_ref.at[rows], out_hbm.at[rows], out_sems.at[i]))
    for copy in copies:
        copy.wait()


def body(hidden_in, key_grad, key_weight, norm_gain, head_order):
    gain = norm_gain.reshape(1, D)
    vmem, hbm, any_ = pltpu.VMEM, pltpu.HBM, pl.ANY
    dma = pltpu.SemaphoreType.DMA
    blocks = NX * NZH
    barrier = lax.optimization_barrier

    with jax.named_scope("weight_z4"):
        far = lax.ppermute(key_weight, AXES, from_z(4))
    with jax.named_scope("norm"):
        own, send, inv = call(
            norm_kernel,
            (shape((blocks, SEQ, COLS)), shape((blocks + 2, SEQ, COLS)), shape((SEQ, 128), F32)),
            (hidden_in, key_grad, gain),
            (any_,) * 3,
            (hbm, hbm, hbm),
            [
                pltpu.VMEM((SEQ, D), BF16),
                pltpu.VMEM((SEQ, K), BF16),
                pltpu.VMEM((1, D), F32),
                pltpu.VMEM((blocks, SEQ, COLS), BF16),
                pltpu.VMEM((blocks, SEQ, COLS), BF16),
                pltpu.VMEM((SEQ, 128), F32),
                dma((6,)),
                dma((11,)),
            ],
            mib=None,
            us=3.5,
        )
        far, send = barrier((far, send))
        other = lax.ppermute(send, AXES, CORE_SWAP)
    with jax.named_scope("weight_y"):
        pieces = call(
            piece_kernel, shape((NY, 256, COLS)), (key_weight, far), (any_, any_), hbm, [dma((8,))]
        )
        near = exchange(pieces, Y_RINGS)
    with jax.named_scope("squares"):
        chunks = call(
            square_kernel,
            shape((4, 1024, COLS)),
            (own, other, key_grad),
            (any_,) * 3,
            hbm,
            [
                pltpu.VMEM((blocks, SEQ, COLS), BF16),
                pltpu.VMEM((blocks + 2, SEQ, COLS), BF16),
                pltpu.VMEM((SEQ, K), BF16),
                pltpu.VMEM((blocks, NY, 128, COLS), BF16),
                dma((10,)),
                dma((blocks, NY)),
            ],
            mib=51,
            us=3.0,
        )
    with jax.named_scope("weight_z2"):
        far = lax.ppermute(near, AXES, from_z(2))
    with jax.named_scope("ring_a"):
        chunks = exchange(chunks, ring_groups(0))
    with jax.named_scope("middle"):
        chunks = call(middle_kernel, shape((4, 256, COLS)), (chunks,), (vmem,), vmem, us=0.3)
        chunks, far = barrier((chunks, far))
    with jax.named_scope("ring_b"):
        chunks = exchange(chunks, ring_groups(1))
    with jax.named_scope("weight_z1"):
        own_a = call(
            join_kernel, shape((8, 256, COLS)), (near, far), (any_, any_), hbm, [dma((2,))], mib=52
        )
        own_b = lax.ppermute(own_a, AXES, from_z(1))
        other_a = lax.ppermute(own_a, AXES, CORE_SWAP)
    with jax.named_scope("split"):
        parts = call(
            split_kernel, shape((NZH * NZL, 16, COLS)), (chunks,), (vmem,), vmem, us=0.3
        )
        parts, own_b = barrier((parts, own_b))
    with jax.named_scope("ring_z"):
        parts = exchange(parts, Z_RINGS)
    with jax.named_scope("weight_swap"):
        other_b = lax.ppermute(own_b, AXES, CORE_SWAP)
    with jax.named_scope("input_grad"):
        input_grad = call(
            input_kernel,
            shape((SEQ, D)),
            (hidden_in, key_grad, gain, inv, own_a, own_b, other_a, other_b),
            (any_,) * 8,
            hbm,
            [
                pltpu.VMEM((SEQ, D), BF16),
                pltpu.VMEM((SEQ, K), BF16),
                pltpu.VMEM((1, D), F32),
                pltpu.VMEM((SEQ, 128), F32),
                pltpu.VMEM((16, 256, COLS), BF16),
                pltpu.VMEM((16, 256, COLS), BF16),
                pltpu.VMEM((SEQ, D), F32),
                pltpu.VMEM((SEQ, D), BF16),
                dma((8,)),
                dma((4,)),
            ],
            mib=60,
            us=6.0,
        )
        parts, input_grad = barrier((parts, input_grad))
    with jax.named_scope("serve"):
        served = call(
            serve_kernel,
            shape((8, K)),
            (head_order.reshape(1, K), parts),
            (any_, vmem),
            vmem,
            [pltpu.VMEM((1, K), jnp.int32), dma],
            us=0.8,
        )
    return served, input_grad


def solution(mesh):
    in_specs = (P(AXES, None), P(AXES, None), P("fsdp", None), P(), P())
    out_specs = (P(AXES, None), P(AXES, None))
    return jax.shard_map(body, mesh=mesh, in_specs=in_specs, out_specs=out_specs, check_vma=False)
```

```python
import jax
import jax.numpy as jnp
from jax import lax
from jax.experimental import pallas as pl
from jax.experimental.pallas import tpu as pltpu
from jax.sharding import PartitionSpec as P

AXES = ("dp", "fsdp")
NX, NZH, NC, NY, NZL = 4, 2, 2, 4, 8
D, K = 4096, 512
SEQ = 256
TOKENS = SEQ * NX * NZH * NC * NY * NZL
COLS = 256
BF16, F32 = jnp.bfloat16, jnp.float32


def device(x, zh, c, y, zl):
    return (((x * NZH + zh) * NC + c) * NY + y) * NZL + zl


def places():
    return [
        (x, zh, c, y, zl)
        for x in range(NX)
        for zh in range(NZH)
        for c in range(NC)
        for y in range(NY)
        for zl in range(NZL)
    ]


def from_z(above_0, above_1):
    pairs = []
    for x, zh, c, y, zl in places():
        z = (zh * NZL + zl + (above_0, above_1)[c]) % (NZH * NZL)
        pairs.append((device(x, z // NZL, c, y, z % NZL), device(x, zh, c, y, zl)))
    return pairs


Y_RINGS = [
    [device(x, zh, c, y, zl) for y in range(NY)]
    for x in range(NX)
    for zh in range(NZH)
    for c in range(NC)
    for zl in range(NZL)
]
PLANES = [
    [device(x, zh, c, y, zl) for x in range(NX) for y in range(NY)]
    for zh in range(NZH)
    for c in range(NC)
    for zl in range(NZL)
]
Z_RINGS = [
    [device(x, zh, c, y, zl) for zh in range(NZH) for zl in range(NZL)]
    for x in range(NX)
    for c in range(NC)
    for y in range(NY)
]
CORE_SWAP = [(device(x, zh, c, y, zl), device(x, zh, 1 - c, y, zl)) for x, zh, c, y, zl in places()]


def exchange(value, groups):
    return lax.all_to_all(
        value, AXES, split_axis=0, concat_axis=0, axis_index_groups=groups, tiled=True
    )


def call(kernel, outs, ins, in_spaces, out_spaces, scratch=(), mib=24, us=0.05):
    return pl.pallas_call(
        kernel,
        out_shape=outs,
        in_specs=[pl.BlockSpec(memory_space=space) for space in in_spaces],
        out_specs=jax.tree.map(lambda space: pl.BlockSpec(memory_space=space), out_spaces),
        scratch_shapes=list(scratch),
        compiler_params=pltpu.CompilerParams(vmem_limit_bytes=mib and mib * 2**20),
        cost_estimate=pl.CostEstimate(
            flops=0, bytes_accessed=int(us * 3.0e6), transcendentals=0
        ),
    )(*ins)


def my_core():
    return lax.rem(lax.axis_index("dp"), NC)


def shape(dims, dtype=BF16):
    return jax.ShapeDtypeStruct(dims, dtype)


def start(source, target, sem):
    copy = pltpu.make_async_copy(source, target, sem)
    copy.start()
    return copy


def norm_kernel(
    hidden_hbm, key_hbm, gain_hbm, own_hbm, send_hbm, inv_hbm,
    hidden_ref, key_ref, gain_ref, own_ref, send_ref, inv_ref, in_sems, out_sems,
):
    core = my_core()
    step, parts, blocks = 16, 4, NX * NZH
    rows_each = SEQ // parts
    pieces = [pl.ds(i * rows_each, rows_each) for i in range(parts)]
    gain_copy = start(gain_hbm, gain_ref, in_sems.at[parts])
    copies = [
        start(hidden_hbm.at[rows], hidden_ref.at[rows], in_sems.at[i])
        for i, rows in enumerate(pieces)
    ]
    key_copy = start(key_hbm, key_ref, in_sems.at[parts + 1])

    def rows_of(i, carry):
        rows = pl.ds(pl.multiple_of(i * step, step), step)
        squares = jnp.zeros((step, 512), F32)
        for t in range(0, D, 512):
            values = hidden_ref[rows, t : t + 512].astype(F32)
            squares += values * values
        inv = lax.rsqrt(jnp.sum(squares, axis=-1, keepdims=True) * (1.0 / D) + 1e-06)
        inv_ref[rows, :] = jnp.broadcast_to(inv, (step, 128))
        for ref, part in ((own_ref, core), (send_ref, 1 - core)):
            for k in range(blocks):
                cols = pl.ds(pl.multiple_of((2 * k + part) * COLS, COLS), COLS)
                unit = hidden_ref[rows, cols].astype(F32) * inv
                ref[k, rows, :] = (unit * gain_ref[:, cols]).astype(BF16)
        return carry

    gain_copy.wait()
    out_copies = []
    for i, rows in enumerate(pieces):
        copies[i].wait()
        lax.fori_loop(i * rows_each // step, (i + 1) * rows_each // step, rows_of, 0)
        out_copies += [
            start(send_ref.at[:, rows], send_hbm.at[pl.ds(0, blocks), rows], out_sems.at[2 * i]),
            start(own_ref.at[:, rows], own_hbm.at[:, rows], out_sems.at[2 * i + 1]),
        ]
    key_copy.wait()
    for half in range(2):
        source = key_ref.at[:, pl.ds(half * COLS, COLS)]
        out_copies.append(start(source, send_hbm.at[blocks + half], out_sems.at[2 * parts + half]))
    out_copies.append(start(inv_ref, inv_hbm, out_sems.at[2 * parts + 2]))
    for copy in out_copies:
        copy.wait()


def piece_kernel(own_hbm, far_hbm, out_hbm, sems):
    cols = pl.ds(pl.multiple_of(my_core() * COLS, COLS), COLS)
    copies = []
    for y in range(NY):
        for i, source in enumerate((own_hbm, far_hbm)):
            target = out_hbm.at[y, pl.ds(i * 128, 128)]
            copies.append(start(source.at[:, cols], target, sems.at[2 * y + i]))
    for copy in copies:
        copy.wait()


def square_kernel(
    own_hbm, other_hbm, key_hbm, out_hbm, own_ref, other_ref, key_ref, out_ref, in_sems, out_sems
):
    blocks = NX * NZH
    over_tokens = (((0,), (0,)), ((), ()))
    keys = [
        start(key_hbm, key_ref, in_sems.at[0]),
        start(other_hbm.at[pl.ds(blocks, 2)], other_ref.at[pl.ds(blocks, 2)], in_sems.at[1]),
    ]
    copies = []
    for part in range(4):
        some = pl.ds(2 * part, 2)
        copies += [
            start(own_hbm.at[some], own_ref.at[some], in_sems.at[2 + 2 * part]),
            start(other_hbm.at[some], other_ref.at[some], in_sems.at[3 + 2 * part]),
        ]
    for copy in keys:
        copy.wait()
    key_other = jnp.concatenate([other_ref[blocks], other_ref[blocks + 1]], axis=1)

    out_copies = []
    for k in range(blocks):
        x, zh = k // NZH, k % NZH
        if zh == 0:
            copies[2 * x].wait()
            copies[2 * x + 1].wait()
        g0 = lax.dot_general(own_ref[k], key_ref[...], over_tokens, preferred_element_type=F32)
        g1 = lax.dot_general(other_ref[k], key_other, over_tokens, preferred_element_type=F32)
        total = ((g0 * g0 + g1 * g1) * (1.0 / TOKENS)).astype(BF16)
        for y in range(NY):
            rows = slice(y * 64, (y + 1) * 64)
            out_ref[k, y, 0:64, :] = total[rows, 0:COLS]
            out_ref[k, y, 64:128, :] = total[rows, COLS:K]
            target = out_hbm.at[x * NY + y, pl.ds(zh * 128, 128)]
            out_copies.append(start(out_ref.at[k, y], target, out_sems.at[k, y]))
    for copy in out_copies:
        copy.wait()


def split_kernel(in_ref, out_ref):
    for zh in range(NZH):
        rows = slice(zh * 128, (zh + 1) * 128)
        total = in_ref[0, rows, :].astype(F32)
        for j in range(1, NX * NY):
            total += in_ref[j, rows, :].astype(F32)
        total = total.reshape(2, NZL, 8, COLS)
        for zl in range(NZL):
            both = jnp.concatenate([total[0, zl], total[1, zl]], axis=0)
            out_ref[zh * NZL + zl] = both.astype(BF16)


def serve_kernel(order_hbm, in_ref, out_ref, order_ref, sem):
    copy = start(order_hbm, order_ref, sem)
    total = in_ref[0].astype(F32)
    for z in range(1, NZH * NZL):
        total += in_ref[z].astype(F32)
    fisher = jnp.concatenate([total[0:8], total[8:16]], axis=1).astype(BF16)
    copy.wait()
    column = lax.broadcasted_iota(jnp.int32, (K, K), 0)
    pick = jnp.where(column == order_ref[...], 1.0, 0.0).astype(BF16)
    out_ref[...] = jnp.dot(fisher, pick, preferred_element_type=F32).astype(BF16)


def input_kernel(
    hidden_hbm, key_hbm, gain_hbm, inv_hbm, own_0, own_1, own_2a, own_2b, own_3,
    other_0, other_1, other_2a, other_2b, other_3, out_hbm,
    hidden_ref, key_ref, gain_ref, inv_ref, own_ref, other_ref, back_ref, out_ref,
    in_sems, out_sems,
):
    first = [start(key_hbm, key_ref, in_sems.at[0])]
    for ref, parts in (
        (own_ref, (own_0, own_1, own_2a, own_2b, own_3)),
        (other_ref, (other_0, other_1, other_2a, other_2b, other_3)),
    ):
        for part, (place, size) in zip(parts, ((0, 4), (4, 4), (8, 2), (10, 2), (12, 4))):
            first.append(start(part, ref.at[pl.ds(place, size)], in_sems.at[len(first)]))
    second = [
        start(gain_hbm, gain_ref, in_sems.at[11]),
        start(inv_hbm, inv_ref, in_sems.at[12]),
        start(hidden_hbm, hidden_ref, in_sems.at[13]),
    ]
    for copy in first:
        copy.wait()
    core = my_core()
    z_here = lax.rem(lax.axis_index("fsdp"), NZL)
    own_cols = pl.ds(pl.multiple_of(core * COLS, COLS), COLS)
    other_cols = pl.ds(pl.multiple_of((1 - core) * COLS, COLS), COLS)
    keys = jnp.concatenate([key_ref[:, own_cols], key_ref[:, other_cols]], axis=1)

    def shard(ref, y, zl):
        away = (zl - z_here) & (NZL - 1)
        step = away & 3
        from_below = (step == 3) | ((step == 2) & (y >= 2))
        second = jnp.where(from_below, 1 - (away >> 2), away >> 2)
        return ref[step * 4 + y, pl.ds(pl.multiple_of(second * 128, 128), 128), :]

    def tile(t, carry):
        y, pair = t // 4, t % 4
        weight = jnp.concatenate(
            [
                jnp.concatenate(
                    [shard(own_ref, y, 2 * pair + i), shard(other_ref, y, 2 * pair + i)], axis=1
                )
                for i in range(2)
            ],
            axis=0,
        )
        cols = pl.ds(pl.multiple_of(t * 256, 256), 256)
        back_ref[:, cols] = lax.dot_general(
            keys, weight, (((1,), (1,)), ((), ())), preferred_element_type=F32
        )
        return carry

    lax.fori_loop(0, D // 256, tile, 0)
    for copy in second:
        copy.wait()

    step, parts, width = 16, 4, 512

    def rows_of(i, carry):
        rows = pl.ds(pl.multiple_of(i * step, step), step)
        inv = inv_ref[rows, 0:1]
        total = jnp.zeros((step, width), F32)
        for t in range(0, D, width):
            cols = slice(t, t + width)
            du = back_ref[rows, cols] * gain_ref[:, cols]
            total += du * hidden_ref[rows, cols].astype(F32)
        mean = inv * jnp.sum(total, axis=-1, keepdims=True) * (1.0 / D)
        factor = inv * inv * mean
        for t in range(0, D, width):
            cols = slice(t, t + width)
            du = back_ref[rows, cols] * gain_ref[:, cols]
            out = du * inv - hidden_ref[rows, cols].astype(F32) * factor
            out_ref[rows, cols] = out.astype(BF16)
        return carry

    rows_each = SEQ // parts
    copies = []
    for i in range(parts):
        lax.fori_loop(i * rows_each // step, (i + 1) * rows_each // step, rows_of, 0)
        rows = pl.ds(i * rows_each, rows_each)
        copies.append(start(out_ref.at[rows], out_hbm.at[rows], out_sems.at[i]))
    for copy in copies:
        copy.wait()


def body(hidden_in, key_grad, key_weight, norm_gain, head_order):
    gain = norm_gain.reshape(1, D)
    vmem, hbm, any_ = pltpu.VMEM, pltpu.HBM, pl.ANY
    dma = pltpu.SemaphoreType.DMA
    blocks = NX * NZH
    barrier = lax.optimization_barrier

    with jax.named_scope("weight_z4"):
        far = lax.ppermute(key_weight, AXES, from_z(4, -4))
    with jax.named_scope("norm"):
        own, send, inv = call(
            norm_kernel,
            (shape((blocks, SEQ, COLS)), shape((blocks + 2, SEQ, COLS)), shape((SEQ, 128), F32)),
            (hidden_in, key_grad, gain),
            (any_,) * 3,
            (hbm, hbm, hbm),
            [
                pltpu.VMEM((SEQ, D), BF16),
                pltpu.VMEM((SEQ, K), BF16),
                pltpu.VMEM((1, D), F32),
                pltpu.VMEM((blocks, SEQ, COLS), BF16),
                pltpu.VMEM((blocks, SEQ, COLS), BF16),
                pltpu.VMEM((SEQ, 128), F32),
                dma((6,)),
                dma((11,)),
            ],
            mib=None,
        )
        other = lax.ppermute(send, AXES, CORE_SWAP)
        far, send = barrier((far, send))
    with jax.named_scope("weight_y"):
        pieces = call(
            piece_kernel, shape((NY, 256, COLS)), (key_weight, far), (any_, any_), hbm, [dma((8,))]
        )
        near = exchange(pieces, Y_RINGS)
    with jax.named_scope("squares"):
        chunks = call(
            square_kernel,
            shape((NX * NY, 256, COLS)),
            (own, other, key_grad),
            (any_,) * 3,
            hbm,
            [
                pltpu.VMEM((blocks, SEQ, COLS), BF16),
                pltpu.VMEM((blocks + 2, SEQ, COLS), BF16),
                pltpu.VMEM((SEQ, K), BF16),
                pltpu.VMEM((blocks, NY, 128, COLS), BF16),
                dma((10,)),
                dma((blocks, NY)),
            ],
            mib=51,
        )
    with jax.named_scope("plane"):
        chunks = exchange(chunks, PLANES)
    with jax.named_scope("weight_z1"):
        up = lax.ppermute(near, AXES, from_z(1, 1))
        down = lax.ppermute(near, AXES, from_z(-1, -1))
    with jax.named_scope("weight_z2"):
        far_up = lax.ppermute(up[:2], AXES, from_z(1, 1))
        far_down = lax.ppermute(down[2:], AXES, from_z(-1, -1))
    with jax.named_scope("split"):
        parts = call(split_kernel, shape((NZH * NZL, 16, COLS)), (chunks,), (vmem,), vmem)
    with jax.named_scope("ring_z"):
        parts = exchange(parts, Z_RINGS)
    with jax.named_scope("weight_swap"):
        weights = (near, up, far_up, far_down, down)
        swapped = tuple(lax.ppermute(part, AXES, CORE_SWAP) for part in weights)
    with jax.named_scope("input_grad"):
        input_grad = call(
            input_kernel,
            shape((SEQ, D)),
            (hidden_in, key_grad, gain, inv, *weights, *swapped),
            (any_,) * 14,
            hbm,
            [
                pltpu.VMEM((SEQ, D), BF16),
                pltpu.VMEM((SEQ, K), BF16),
                pltpu.VMEM((1, D), F32),
                pltpu.VMEM((SEQ, 128), F32),
                pltpu.VMEM((16, 256, COLS), BF16),
                pltpu.VMEM((16, 256, COLS), BF16),
                pltpu.VMEM((SEQ, D), F32),
                pltpu.VMEM((SEQ, D), BF16),
                dma((14,)),
                dma((4,)),
            ],
            mib=60,
        )
        parts, input_grad = barrier((parts, input_grad))
    with jax.named_scope("serve"):
        served = call(
            serve_kernel,
            shape((8, K)),
            (head_order.reshape(1, K), parts),
            (any_, vmem),
            vmem,
            [pltpu.VMEM((1, K), jnp.int32), dma],
        )
    return served, input_grad


def solution(mesh):
    in_specs = (P(AXES, None), P(AXES, None), P("fsdp", None), P(), P())
    out_specs = (P(AXES, None), P(AXES, None))
    return jax.shard_map(body, mesh=mesh, in_specs=in_specs, out_specs=out_specs, check_vma=False)
```

```python
import jax
import jax.numpy as jnp
from jax import lax
from jax.experimental import pallas as pl
from jax.experimental.pallas import tpu as pltpu
from jax.sharding import PartitionSpec as P

AXES = ("dp", "fsdp")
NX, NZH, NC, NY, NZL = 4, 2, 2, 4, 8
D, K = 4096, 512
SEQ = 256
TOKENS = SEQ * NX * NZH * NC * NY * NZL
COLS = 256
NORM_PARTS = 4
BF16, F32 = jnp.bfloat16, jnp.float32


def device(x, zh, c, y, zl):
    return (((x * NZH + zh) * NC + c) * NY + y) * NZL + zl


def places():
    return [
        (x, zh, c, y, zl)
        for x in range(NX)
        for zh in range(NZH)
        for c in range(NC)
        for y in range(NY)
        for zl in range(NZL)
    ]


def from_z(above_0, above_1):
    pairs = []
    for x, zh, c, y, zl in places():
        z = (zh * NZL + zl + (above_0, above_1)[c]) % (NZH * NZL)
        pairs.append((device(x, z // NZL, c, y, z % NZL), device(x, zh, c, y, zl)))
    return pairs


Y_RINGS = [
    [device(x, zh, c, y, zl) for y in range(NY)]
    for x in range(NX)
    for zh in range(NZH)
    for c in range(NC)
    for zl in range(NZL)
]
PLANES = [
    [device(x, zh, c, y, zl) for x in range(NX) for y in range(NY)]
    for zh in range(NZH)
    for c in range(NC)
    for zl in range(NZL)
]
Z_RINGS = [
    [device(x, zh, c, y, zl) for zh in range(NZH) for zl in range(NZL)]
    for x in range(NX)
    for c in range(NC)
    for y in range(NY)
]
CORE_SWAP = [(device(x, zh, c, y, zl), device(x, zh, 1 - c, y, zl)) for x, zh, c, y, zl in places()]


def exchange(value, groups):
    return lax.all_to_all(
        value, AXES, split_axis=0, concat_axis=0, axis_index_groups=groups, tiled=True
    )


def call(kernel, outs, ins, in_spaces, out_spaces, scratch=(), mib=24, us=0.05):
    return pl.pallas_call(
        kernel,
        out_shape=outs,
        in_specs=[pl.BlockSpec(memory_space=space) for space in in_spaces],
        out_specs=jax.tree.map(lambda space: pl.BlockSpec(memory_space=space), out_spaces),
        scratch_shapes=list(scratch),
        compiler_params=pltpu.CompilerParams(vmem_limit_bytes=mib and mib * 2**20),
        cost_estimate=pl.CostEstimate(
            flops=0, bytes_accessed=int(us * 3.0e6), transcendentals=0
        ),
    )(*ins)


def my_core():
    return lax.rem(lax.axis_index("dp"), NC)


def shape(dims, dtype=BF16):
    return jax.ShapeDtypeStruct(dims, dtype)


def start(source, target, sem):
    copy = pltpu.make_async_copy(source, target, sem)
    copy.start()
    return copy


def norm_kernel(
    hidden_hbm, key_hbm, gain_hbm, own_hbm, send_hbm, inv_hbm,
    hidden_ref, key_ref, gain_ref, own_ref, send_ref, inv_ref, in_sems, out_sems,
):
    core = my_core()
    step, parts, blocks = 16, NORM_PARTS, NX * NZH
    rows_each = SEQ // parts
    pieces = [pl.ds(i * rows_each, rows_each) for i in range(parts)]
    gain_copy = start(gain_hbm, gain_ref, in_sems.at[parts])
    copies = [
        start(hidden_hbm.at[rows], hidden_ref.at[rows], in_sems.at[i])
        for i, rows in enumerate(pieces)
    ]
    key_copy = start(key_hbm, key_ref, in_sems.at[parts + 1])

    def rows_of(i, carry):
        rows = pl.ds(pl.multiple_of(i * step, step), step)
        squares = jnp.zeros((step, 512), F32)
        for t in range(0, D, 512):
            values = hidden_ref[rows, t : t + 512].astype(F32)
            squares += values * values
        inv = lax.rsqrt(jnp.sum(squares, axis=-1, keepdims=True) * (1.0 / D) + 1e-06)
        inv_ref[rows, :] = jnp.broadcast_to(inv, (step, 128))
        for ref, part in ((own_ref, core), (send_ref, 1 - core)):
            for k in range(blocks):
                cols = pl.ds(pl.multiple_of((2 * k + part) * COLS, COLS), COLS)
                unit = hidden_ref[rows, cols].astype(F32) * inv
                ref[k, rows, :] = (unit * gain_ref[:, cols]).astype(BF16)
        return carry

    gain_copy.wait()
    out_copies = []
    for i, rows in enumerate(pieces):
        copies[i].wait()
        lax.fori_loop(i * rows_each // step, (i + 1) * rows_each // step, rows_of, 0, unroll=4)
        out_copies += [
            start(send_ref.at[:, rows], send_hbm.at[pl.ds(0, blocks), rows], out_sems.at[2 * i]),
            start(own_ref.at[:, rows], own_hbm.at[:, rows], out_sems.at[2 * i + 1]),
        ]
    key_copy.wait()
    for half in range(2):
        source = key_ref.at[:, pl.ds(half * COLS, COLS)]
        out_copies.append(start(source, send_hbm.at[blocks + half], out_sems.at[2 * parts + half]))
    out_copies.append(start(inv_ref, inv_hbm, out_sems.at[2 * parts + 2]))
    for copy in out_copies:
        copy.wait()


def piece_kernel(own_hbm, far_hbm, out_hbm, sems):
    cols = pl.ds(pl.multiple_of(my_core() * COLS, COLS), COLS)
    copies = []
    for y in range(NY):
        for i, source in enumerate((own_hbm, far_hbm)):
            target = out_hbm.at[y, pl.ds(i * 128, 128)]
            copies.append(start(source.at[:, cols], target, sems.at[2 * y + i]))
    for copy in copies:
        copy.wait()


def square_kernel(
    own_hbm, other_hbm, key_hbm, out_hbm, own_ref, other_ref, key_ref, out_ref, in_sems, out_sems
):
    blocks = NX * NZH
    over_tokens = (((0,), (0,)), ((), ()))
    keys = [
        start(key_hbm, key_ref, in_sems.at[0]),
        start(other_hbm.at[pl.ds(blocks, 2)], other_ref.at[pl.ds(blocks, 2)], in_sems.at[1]),
    ]
    copies = []
    for part in range(4):
        some = pl.ds(2 * part, 2)
        copies += [
            start(own_hbm.at[some], own_ref.at[some], in_sems.at[2 + 2 * part]),
            start(other_hbm.at[some], other_ref.at[some], in_sems.at[3 + 2 * part]),
        ]
    for copy in keys:
        copy.wait()
    key_other = jnp.concatenate([other_ref[blocks], other_ref[blocks + 1]], axis=1)

    out_copies = []
    for k in range(blocks):
        x, zh = k // NZH, k % NZH
        if zh == 0:
            copies[2 * x].wait()
            copies[2 * x + 1].wait()
        g0 = lax.dot_general(own_ref[k], key_ref[...], over_tokens, preferred_element_type=F32)
        g1 = lax.dot_general(other_ref[k], key_other, over_tokens, preferred_element_type=F32)
        total = ((g0 * g0 + g1 * g1) * (1.0 / TOKENS)).astype(BF16)
        for y in range(NY):
            rows = slice(y * 64, (y + 1) * 64)
            out_ref[k, y, 0:64, :] = total[rows, 0:COLS]
            out_ref[k, y, 64:128, :] = total[rows, COLS:K]
            target = out_hbm.at[x * NY + y, pl.ds(zh * 128, 128)]
            out_copies.append(start(out_ref.at[k, y], target, out_sems.at[k, y]))
    for copy in out_copies:
        copy.wait()


def halves_kernel(up_hbm, down_hbm, up_half, down_half, sems):
    copies = [
        start(up_hbm.at[pl.ds(0, 2)], up_half, sems.at[0]),
        start(down_hbm.at[pl.ds(2, 2)], down_half, sems.at[1]),
    ]
    for copy in copies:
        copy.wait()


def split_kernel(in_ref, out_ref):
    for zh in range(NZH):
        rows = slice(zh * 128, (zh + 1) * 128)
        total = in_ref[0, rows, :].astype(F32)
        for j in range(1, NX * NY):
            total += in_ref[j, rows, :].astype(F32)
        total = total.reshape(2, NZL, 8, COLS)
        for zl in range(NZL):
            both = jnp.concatenate([total[0, zl], total[1, zl]], axis=0)
            out_ref[zh * NZL + zl] = both.astype(BF16)


def serve_kernel(order_hbm, in_ref, out_ref, order_ref, sem):
    copy = start(order_hbm, order_ref, sem)
    total = in_ref[0].astype(F32)
    for z in range(1, NZH * NZL):
        total += in_ref[z].astype(F32)
    fisher = jnp.concatenate([total[0:8], total[8:16]], axis=1).astype(BF16)
    copy.wait()
    column = lax.broadcasted_iota(jnp.int32, (K, K), 0)
    pick = jnp.where(column == order_ref[...], 1.0, 0.0).astype(BF16)
    out_ref[...] = jnp.dot(fisher, pick, preferred_element_type=F32).astype(BF16)


def input_kernel(
    hidden_hbm, key_hbm, gain_hbm, inv_hbm, own_0, own_1, own_2a, own_2b, own_3,
    other_0, other_1, other_2a, other_2b, other_3, out_hbm,
    hidden_ref, key_ref, gain_ref, inv_ref, own_ref, other_ref, back_ref, out_ref,
    in_sems, out_sems,
):
    key_copy = start(key_hbm, key_ref, in_sems.at[0])
    places = {0: (0, 4), 1: (4, 4), 3: (12, 4), 2: (8, 2), 4: (10, 2)}
    sources = {
        0: (own_0, other_0),
        1: (own_1, other_1),
        3: (own_3, other_3),
        2: (own_2a, other_2a),
        4: (own_2b, other_2b),
    }
    weights = {}
    for i, (part, (place, size)) in enumerate(places.items()):
        weights[part] = [
            start(source, ref.at[pl.ds(place, size)], in_sems.at[1 + 2 * i + j])
            for j, (source, ref) in enumerate(zip(sources[part], (own_ref, other_ref)))
        ]
    second = [
        start(gain_hbm, gain_ref, in_sems.at[11]),
        start(inv_hbm, inv_ref, in_sems.at[12]),
        start(hidden_hbm, hidden_ref, in_sems.at[13]),
    ]
    core = my_core()
    z_here = lax.rem(lax.axis_index("fsdp"), NZL)
    own_cols = pl.ds(pl.multiple_of(core * COLS, COLS), COLS)
    other_cols = pl.ds(pl.multiple_of((1 - core) * COLS, COLS), COLS)
    key_copy.wait()
    keys = jnp.concatenate([key_ref[:, own_cols], key_ref[:, other_cols]], axis=1)

    for part, (place, size) in places.items():
        for copy in weights[part]:
            copy.wait()
        for i in range(size):
            y = (place + i) % NY
            away = (0, 1, 2, 7, 6)[part]
            weight = jnp.concatenate([own_ref[place + i], other_ref[place + i]], axis=1)
            back = lax.dot_general(
                keys, weight, (((1,), (1,)), ((), ())), preferred_element_type=F32
            )
            for half in range(2):
                shard = (z_here + away + 4 * half) & (NZL - 1)
                cols = pl.ds(pl.multiple_of((y * NZL + shard) * 128, 128), 128)
                back_ref[:, cols] = back[:, half * 128 : (half + 1) * 128]
    for copy in second:
        copy.wait()

    step, parts, width = 16, 4, 512

    def rows_of(i, carry):
        rows = pl.ds(pl.multiple_of(i * step, step), step)
        inv = inv_ref[rows, 0:1]
        total = jnp.zeros((step, width), F32)
        for t in range(0, D, width):
            cols = slice(t, t + width)
            du = back_ref[rows, cols] * gain_ref[:, cols]
            total += du * hidden_ref[rows, cols].astype(F32)
        mean = inv * jnp.sum(total, axis=-1, keepdims=True) * (1.0 / D)
        factor = inv * inv * mean
        for t in range(0, D, width):
            cols = slice(t, t + width)
            du = back_ref[rows, cols] * gain_ref[:, cols]
            out = du * inv - hidden_ref[rows, cols].astype(F32) * factor
            out_ref[rows, cols] = out.astype(BF16)
        return carry

    rows_each = SEQ // parts
    copies = []
    for i in range(parts):
        lax.fori_loop(i * rows_each // step, (i + 1) * rows_each // step, rows_of, 0, unroll=4)
        rows = pl.ds(i * rows_each, rows_each)
        copies.append(start(out_ref.at[rows], out_hbm.at[rows], out_sems.at[i]))
    for copy in copies:
        copy.wait()


def body(hidden_in, key_grad, key_weight, norm_gain, head_order):
    gain = norm_gain.reshape(1, D)
    vmem, hbm, any_ = pltpu.VMEM, pltpu.HBM, pl.ANY
    dma = pltpu.SemaphoreType.DMA
    blocks = NX * NZH
    barrier = lax.optimization_barrier

    with jax.named_scope("weight_z4"):
        far = lax.ppermute(key_weight, AXES, from_z(4, -4))
    with jax.named_scope("norm"):
        own, send, inv = call(
            norm_kernel,
            (shape((blocks, SEQ, COLS)), shape((blocks + 2, SEQ, COLS)), shape((SEQ, 128), F32)),
            (hidden_in, key_grad, gain),
            (any_,) * 3,
            (hbm, hbm, hbm),
            [
                pltpu.VMEM((SEQ, D), BF16),
                pltpu.VMEM((SEQ, K), BF16),
                pltpu.VMEM((1, D), F32),
                pltpu.VMEM((blocks, SEQ, COLS), BF16),
                pltpu.VMEM((blocks, SEQ, COLS), BF16),
                pltpu.VMEM((SEQ, 128), F32),
                dma((NORM_PARTS + 2,)),
                dma((2 * NORM_PARTS + 3,)),
            ],
            mib=None,
        )
        far, send = barrier((far, send))
        other = lax.ppermute(send, AXES, CORE_SWAP)
    with jax.named_scope("weight_y"):
        pieces = call(
            piece_kernel, shape((NY, 256, COLS)), (key_weight, far), (any_, any_), hbm, [dma((8,))]
        )
        near = exchange(pieces, Y_RINGS)
    with jax.named_scope("squares"):
        chunks = call(
            square_kernel,
            shape((NX * NY, 256, COLS)),
            (own, other, key_grad),
            (any_,) * 3,
            hbm,
            [
                pltpu.VMEM((blocks, SEQ, COLS), BF16),
                pltpu.VMEM((blocks + 2, SEQ, COLS), BF16),
                pltpu.VMEM((SEQ, K), BF16),
                pltpu.VMEM((blocks, NY, 128, COLS), BF16),
                dma((10,)),
                dma((blocks, NY)),
            ],
            mib=51,
        )
    with jax.named_scope("plane"):
        chunks = exchange(chunks, PLANES)
    with jax.named_scope("weight_z1"):
        up = lax.ppermute(near, AXES, from_z(1, 1))
        down = lax.ppermute(near, AXES, from_z(-1, -1))
    with jax.named_scope("weight_z2"):
        half = shape((2, 256, COLS))
        up_half, down_half = call(
            halves_kernel, (half, half), (up, down), (any_, any_), (hbm, hbm), [dma((2,))], mib=52
        )
        far_up = lax.ppermute(up_half, AXES, from_z(1, 1))
        far_down = lax.ppermute(down_half, AXES, from_z(-1, -1))
    with jax.named_scope("split"):
        parts = call(split_kernel, shape((NZH * NZL, 16, COLS)), (chunks,), (vmem,), vmem)
    with jax.named_scope("ring_z"):
        parts = exchange(parts, Z_RINGS)
    with jax.named_scope("weight_swap"):
        weights = (near, up, far_up, far_down, down)
        swapped = tuple(lax.ppermute(part, AXES, CORE_SWAP) for part in weights)
    with jax.named_scope("input_grad"):
        input_grad = call(
            input_kernel,
            shape((SEQ, D)),
            (hidden_in, key_grad, gain, inv, *weights, *swapped),
            (any_,) * 14,
            hbm,
            [
                pltpu.VMEM((SEQ, D), BF16),
                pltpu.VMEM((SEQ, K), BF16),
                pltpu.VMEM((1, D), F32),
                pltpu.VMEM((SEQ, 128), F32),
                pltpu.VMEM((16, 256, COLS), BF16),
                pltpu.VMEM((16, 256, COLS), BF16),
                pltpu.VMEM((SEQ, D), F32),
                pltpu.VMEM((SEQ, D), BF16),
                dma((14,)),
                dma((4,)),
            ],
            mib=60,
        )
        parts, input_grad = barrier((parts, input_grad))
    with jax.named_scope("serve"):
        served = call(
            serve_kernel,
            shape((8, K)),
            (head_order.reshape(1, K), parts),
            (any_, vmem),
            vmem,
            [pltpu.VMEM((1, K), jnp.int32), dma],
        )
    return served, input_grad


def solution(mesh):
    in_specs = (P(AXES, None), P(AXES, None), P("fsdp", None), P(), P())
    out_specs = (P(AXES, None), P(AXES, None))
    return jax.shard_map(body, mesh=mesh, in_specs=in_specs, out_specs=out_specs, check_vma=False)
```

```python
import jax
import jax.numpy as jnp
from jax import lax
from jax.experimental import pallas as pl
from jax.experimental.pallas import tpu as pltpu
from jax.sharding import PartitionSpec as P

AXES = ("dp", "fsdp")
NX, NZH, NC, NY, NZL = 4, 2, 2, 4, 8
D, K = 4096, 512
SEQ = 256
TOKENS = SEQ * NX * NZH * NC * NY * NZL
COLS = 256
NORM_PARTS = 4
BF16, F32 = jnp.bfloat16, jnp.float32


def device(x, zh, c, y, zl):
    return (((x * NZH + zh) * NC + c) * NY + y) * NZL + zl


def places():
    return [
        (x, zh, c, y, zl)
        for x in range(NX)
        for zh in range(NZH)
        for c in range(NC)
        for y in range(NY)
        for zl in range(NZL)
    ]


def from_z(distance):
    pairs = []
    for x, zh, c, y, zl in places():
        z = (zh * NZL + zl + distance) % (NZH * NZL)
        pairs.append((device(x, z // NZL, c, y, z % NZL), device(x, zh, c, y, zl)))
    return pairs


def from_y(ahead):
    return [
        (device(x, zh, c, (y + ahead) % NY, zl), device(x, zh, c, y, zl))
        for x, zh, c, y, zl in places()
    ]


def origins():
    pairs = []
    for x, zh, c, y, zl in places():
        z = (zh * NZL + zl + c * (4 if zl % 2 == 0 else -4)) % (NZH * NZL)
        pairs.append((device(x, z // NZL, c, y, z % NZL), device(x, zh, c, y, zl)))
    return pairs


PLANES = [
    [device(x, zh, c, y, zl) for x in range(NX) for y in range(NY)]
    for zh in range(NZH)
    for c in range(NC)
    for zl in range(NZL)
]
Z_RINGS = [
    [device(x, zh, c, y, zl) for zh in range(NZH) for zl in range(NZL)]
    for x in range(NX)
    for c in range(NC)
    for y in range(NY)
]
CORE_SWAP = [(device(x, zh, c, y, zl), device(x, zh, 1 - c, y, zl)) for x, zh, c, y, zl in places()]


def exchange(value, groups):
    return lax.all_to_all(
        value, AXES, split_axis=0, concat_axis=0, axis_index_groups=groups, tiled=True
    )


def call(kernel, outs, ins, in_spaces, out_spaces, scratch=(), mib=24, us=0.05):
    return pl.pallas_call(
        kernel,
        out_shape=outs,
        in_specs=[pl.BlockSpec(memory_space=space) for space in in_spaces],
        out_specs=jax.tree.map(lambda space: pl.BlockSpec(memory_space=space), out_spaces),
        scratch_shapes=list(scratch),
        compiler_params=pltpu.CompilerParams(vmem_limit_bytes=mib and mib * 2**20),
        cost_estimate=pl.CostEstimate(
            flops=0, bytes_accessed=int(us * 3.0e6), transcendentals=0
        ),
    )(*ins)


def my_core():
    return lax.rem(lax.axis_index("dp"), NC)


def shape(dims, dtype=BF16):
    return jax.ShapeDtypeStruct(dims, dtype)


def start(source, target, sem):
    copy = pltpu.make_async_copy(source, target, sem)
    copy.start()
    return copy


def norm_kernel(
    hidden_hbm, key_hbm, gain_hbm, own_hbm, send_hbm, inv_hbm,
    hidden_ref, key_ref, gain_ref, own_ref, send_ref, inv_ref, in_sems, out_sems,
):
    core = my_core()
    step, parts, blocks = 16, NORM_PARTS, NX * NZH
    rows_each = SEQ // parts
    pieces = [pl.ds(i * rows_each, rows_each) for i in range(parts)]
    gain_copy = start(gain_hbm, gain_ref, in_sems.at[parts])
    copies = [
        start(hidden_hbm.at[rows], hidden_ref.at[rows], in_sems.at[i])
        for i, rows in enumerate(pieces)
    ]
    key_copy = start(key_hbm, key_ref, in_sems.at[parts + 1])

    def rows_of(i, carry):
        rows = pl.ds(pl.multiple_of(i * step, step), step)
        squares = jnp.zeros((step, 512), F32)
        for t in range(0, D, 512):
            values = hidden_ref[rows, t : t + 512].astype(F32)
            squares += values * values
        inv = lax.rsqrt(jnp.sum(squares, axis=-1, keepdims=True) * (1.0 / D) + 1e-06)
        inv_ref[rows, :] = jnp.broadcast_to(inv, (step, 128))
        for ref, part in ((own_ref, core), (send_ref, 1 - core)):
            for k in range(blocks):
                cols = pl.ds(pl.multiple_of((2 * k + part) * COLS, COLS), COLS)
                unit = hidden_ref[rows, cols].astype(F32) * inv
                ref[k, rows, :] = (unit * gain_ref[:, cols]).astype(BF16)
        return carry

    gain_copy.wait()
    out_copies = []
    for i, rows in enumerate(pieces):
        copies[i].wait()
        lax.fori_loop(i * rows_each // step, (i + 1) * rows_each // step, rows_of, 0, unroll=4)
        out_copies += [
            start(send_ref.at[:, rows], send_hbm.at[pl.ds(0, blocks), rows], out_sems.at[2 * i]),
            start(own_ref.at[:, rows], own_hbm.at[:, rows], out_sems.at[2 * i + 1]),
        ]
    key_copy.wait()
    for half in range(2):
        source = key_ref.at[:, pl.ds(half * COLS, COLS)]
        out_copies.append(start(source, send_hbm.at[blocks + half], out_sems.at[2 * parts + half]))
    out_copies.append(start(inv_ref, inv_hbm, out_sems.at[2 * parts + 2]))
    for copy in out_copies:
        copy.wait()


def column_kernel(*refs):
    *blocks, out_hbm, sems = refs
    copies = [start(block, out_hbm.at[j], sems.at[j]) for j, block in enumerate(blocks)]
    for copy in copies:
        copy.wait()


def partner_kernel(key_hbm, after_hbm, *refs):
    del after_hbm
    *sources, out_hbm, key_ref, weight_ref, out_ref, in_sems, out_sems = refs
    key_copy = start(key_hbm.at[pl.ds(NX * NZH, 2)], key_ref, in_sems.at[0])
    copies, place = [], 0
    for i, source in enumerate(sources):
        size = source.shape[0]
        target = weight_ref.at[pl.ds(place, size)]
        copies.append((start(source, target, in_sems.at[1 + i]), place // 2, size // 2))
        place += size
    key_copy.wait()
    keys = jnp.concatenate([key_ref[0], key_ref[1]], axis=1)
    out_copies = []
    for copy, first, size in copies:
        copy.wait()
        for block in range(first, first + size):
            weight = weight_ref[2 * block : 2 * block + 2].reshape(256, K)
            back = lax.dot_general(
                keys, weight, (((1,), (1,)), ((), ())), preferred_element_type=F32
            )
            out_ref[block] = back.astype(BF16)
            out_copies.append(start(out_ref.at[block], out_hbm.at[block], out_sems.at[block]))
    for copy in out_copies:
        copy.wait()


def partner(other, after, *sources):
    size = sum(source.shape[0] for source in sources)
    dma = pltpu.SemaphoreType.DMA
    return call(
        partner_kernel,
        shape((size // 2, SEQ, COLS)),
        (other, after, *sources),
        (pl.ANY,) * (2 + len(sources)),
        pltpu.HBM,
        [
            pltpu.VMEM((2, SEQ, COLS), BF16),
            pltpu.VMEM((size, 128, K), BF16),
            pltpu.VMEM((size // 2, SEQ, COLS), BF16),
            dma((1 + len(sources),)),
            dma((size // 2,)),
        ],
        mib=52,
    )


def square_kernel(
    own_hbm, other_hbm, key_hbm, out_hbm, own_ref, other_ref, key_ref, out_ref, in_sems, out_sems
):
    blocks = NX * NZH
    over_tokens = (((0,), (0,)), ((), ()))
    keys = [
        start(key_hbm, key_ref, in_sems.at[0]),
        start(other_hbm.at[pl.ds(blocks, 2)], other_ref.at[pl.ds(blocks, 2)], in_sems.at[1]),
    ]
    copies = []
    for part in range(4):
        some = pl.ds(2 * part, 2)
        copies += [
            start(own_hbm.at[some], own_ref.at[some], in_sems.at[2 + 2 * part]),
            start(other_hbm.at[some], other_ref.at[some], in_sems.at[3 + 2 * part]),
        ]
    for copy in keys:
        copy.wait()
    key_other = jnp.concatenate([other_ref[blocks], other_ref[blocks + 1]], axis=1)

    out_copies = []
    for k in range(blocks):
        x, zh = k // NZH, k % NZH
        if zh == 0:
            copies[2 * x].wait()
            copies[2 * x + 1].wait()
        g0 = lax.dot_general(own_ref[k], key_ref[...], over_tokens, preferred_element_type=F32)
        g1 = lax.dot_general(other_ref[k], key_other, over_tokens, preferred_element_type=F32)
        total = ((g0 * g0 + g1 * g1) * (1.0 / TOKENS)).astype(BF16)
        for y in range(NY):
            rows = slice(y * 64, (y + 1) * 64)
            out_ref[k, y, 0:64, :] = total[rows, 0:COLS]
            out_ref[k, y, 64:128, :] = total[rows, COLS:K]
            target = out_hbm.at[x * NY + y, pl.ds(zh * 128, 128)]
            out_copies.append(start(out_ref.at[k, y], target, out_sems.at[k, y]))
    for copy in out_copies:
        copy.wait()


def halves_kernel(up_hbm, down_hbm, up_half, down_half, sems):
    copies = [
        start(up_hbm.at[pl.ds(0, 2)], up_half, sems.at[0]),
        start(down_hbm.at[pl.ds(2, 2)], down_half, sems.at[1]),
    ]
    for copy in copies:
        copy.wait()


def split_kernel(in_ref, out_ref):
    for zh in range(NZH):
        rows = slice(zh * 128, (zh + 1) * 128)
        total = in_ref[0, rows, :].astype(F32)
        for j in range(1, NX * NY):
            total += in_ref[j, rows, :].astype(F32)
        total = total.reshape(2, NZL, 8, COLS)
        for zl in range(NZL):
            both = jnp.concatenate([total[0, zl], total[1, zl]], axis=0)
            out_ref[zh * NZL + zl] = both.astype(BF16)


def serve_kernel(order_hbm, in_ref, out_ref, order_ref, sem):
    copy = start(order_hbm, order_ref, sem)
    total = in_ref[0].astype(F32)
    for z in range(1, NZH * NZL):
        total += in_ref[z].astype(F32)
    fisher = jnp.concatenate([total[0:8], total[8:16]], axis=1).astype(BF16)
    copy.wait()
    column = lax.broadcasted_iota(jnp.int32, (K, K), 0)
    pick = jnp.where(column == order_ref[...], 1.0, 0.0).astype(BF16)
    out_ref[...] = jnp.dot(fisher, pick, preferred_element_type=F32).astype(BF16)


def input_kernel(
    hidden_hbm, key_hbm, gain_hbm, inv_hbm, weight_0, weight_1, weight_3, weight_2a, weight_2b,
    early_hbm, late_hbm, out_hbm,
    hidden_ref, key_ref, gain_ref, inv_ref, weight_ref, early_ref, late_ref, back_ref, out_ref,
    in_sems, out_sems,
):
    key_copy = start(key_hbm, key_ref, in_sems.at[0])
    groups = (
        (weight_0, 0, 0),
        (weight_1, 1, 0),
        (weight_3, 7, 0),
        (weight_2a, 2, 0),
        (weight_2b, 6, 2),
    )
    copies, blocks = [], []
    for i, (source, away, row) in enumerate(groups):
        size = source.shape[0]
        target = weight_ref.at[pl.ds(2 * len(blocks), size)]
        copies.append(start(source, target, in_sems.at[1 + i]))
        blocks += [(i, away, row + j) for j in range(0, size, 2)]
    second = [
        start(early_hbm, early_ref, in_sems.at[6]),
        start(late_hbm, late_ref, in_sems.at[7]),
        start(gain_hbm, gain_ref, in_sems.at[8]),
        start(inv_hbm, inv_ref, in_sems.at[9]),
        start(hidden_hbm, hidden_ref, in_sems.at[10]),
    ]
    core = my_core()
    z_here = lax.rem(lax.axis_index("fsdp"), NZL)
    y_here = lax.div(lax.axis_index("fsdp"), NZL)

    def put(back, origin, away, row):
        zl = (z_here + origin + away) & (NZL - 1)
        for half in range(2):
            y = (y_here + row + half) & (NY - 1)
            cols = pl.ds(pl.multiple_of((y * NZL + zl) * 128, 128), 128)
            back_ref[:, cols] = back[:, half * 128 : (half + 1) * 128]

    key_copy.wait()
    keys = key_ref[...]
    waited = 0
    for block, (group, away, row) in enumerate(blocks):
        if waited == group:
            copies[group].wait()
            waited += 1
        weight = weight_ref[2 * block : 2 * block + 2].reshape(256, K)
        back = lax.dot_general(keys, weight, (((1,), (1,)), ((), ())), preferred_element_type=F32)
        put(back, 4 * core, away, row)
    second[0].wait()
    second[1].wait()
    early = early_ref.shape[0]
    for block, (_, away, row) in enumerate(blocks):
        back = early_ref[block] if block < early else late_ref[block - early]
        put(back.astype(F32), 4 * (1 - core), away, row)
    for copy in second[2:]:
        copy.wait()

    step, parts, width = 16, 4, 512

    def rows_of(i, carry):
        rows = pl.ds(pl.multiple_of(i * step, step), step)
        inv = inv_ref[rows, 0:1]
        total = jnp.zeros((step, width), F32)
        for t in range(0, D, width):
            cols = slice(t, t + width)
            du = back_ref[rows, cols] * gain_ref[:, cols]
            total += du * hidden_ref[rows, cols].astype(F32)
        mean = inv * jnp.sum(total, axis=-1, keepdims=True) * (1.0 / D)
        factor = inv * inv * mean
        for t in range(0, D, width):
            cols = slice(t, t + width)
            du = back_ref[rows, cols] * gain_ref[:, cols]
            out = du * inv - hidden_ref[rows, cols].astype(F32) * factor
            out_ref[rows, cols] = out.astype(BF16)
        return carry

    rows_each = SEQ // parts
    copies = []
    for i in range(parts):
        lax.fori_loop(i * rows_each // step, (i + 1) * rows_each // step, rows_of, 0, unroll=4)
        rows = pl.ds(i * rows_each, rows_each)
        copies.append(start(out_ref.at[rows], out_hbm.at[rows], out_sems.at[i]))
    for copy in copies:
        copy.wait()


def body(hidden_in, key_grad, key_weight, norm_gain, head_order):
    gain = norm_gain.reshape(1, D)
    vmem, hbm, any_ = pltpu.VMEM, pltpu.HBM, pl.ANY
    dma = pltpu.SemaphoreType.DMA
    blocks = NX * NZH
    barrier = lax.optimization_barrier

    with jax.named_scope("weight_z4"):
        origin = lax.ppermute(key_weight, AXES, origins())
    with jax.named_scope("norm"):
        own, send, inv = call(
            norm_kernel,
            (shape((blocks, SEQ, COLS)), shape((blocks + 2, SEQ, COLS)), shape((SEQ, 128), F32)),
            (hidden_in, key_grad, gain),
            (any_,) * 3,
            (hbm, hbm, hbm),
            [
                pltpu.VMEM((SEQ, D), BF16),
                pltpu.VMEM((SEQ, K), BF16),
                pltpu.VMEM((1, D), F32),
                pltpu.VMEM((blocks, SEQ, COLS), BF16),
                pltpu.VMEM((blocks, SEQ, COLS), BF16),
                pltpu.VMEM((SEQ, 128), F32),
                dma((NORM_PARTS + 2,)),
                dma((2 * NORM_PARTS + 3,)),
            ],
            mib=None,
        )
        other = lax.ppermute(send, AXES, CORE_SWAP)
    with jax.named_scope("squares"):
        chunks = call(
            square_kernel,
            shape((NX * NY, 256, COLS)),
            (own, other, key_grad),
            (any_,) * 3,
            hbm,
            [
                pltpu.VMEM((blocks, SEQ, COLS), BF16),
                pltpu.VMEM((blocks + 2, SEQ, COLS), BF16),
                pltpu.VMEM((SEQ, K), BF16),
                pltpu.VMEM((blocks, NY, 128, COLS), BF16),
                dma((10,)),
                dma((blocks, NY)),
            ],
            mib=51,
        )
        chunks, origin = barrier((chunks, origin))
    with jax.named_scope("plane"):
        chunks = exchange(chunks, PLANES)
    with jax.named_scope("weight_y"):
        column = [origin] + [lax.ppermute(origin, AXES, from_y(ahead)) for ahead in (1, 2, 3)]
        near = call(
            column_kernel, shape((NY, 128, K)), column, (any_,) * NY, hbm, [dma((NY,))], mib=52
        )
    with jax.named_scope("weight_z1"):
        up = lax.ppermute(near, AXES, from_z(1))
        down = lax.ppermute(near, AXES, from_z(-1))
    with jax.named_scope("weight_z2"):
        half = shape((2, 128, K))
        up_half, down_half = call(
            halves_kernel, (half, half), (up, down), (any_, any_), (hbm, hbm), [dma((2,))], mib=52
        )
        far_up = lax.ppermute(up_half, AXES, from_z(1))
        far_down = lax.ppermute(down_half, AXES, from_z(-1))
    with jax.named_scope("back_early"):
        early = lax.ppermute(partner(other, up_half, near, up, down), AXES, CORE_SWAP)
    with jax.named_scope("split"):
        parts = call(split_kernel, shape((NZH * NZL, 16, COLS)), (chunks,), (vmem,), vmem)
    with jax.named_scope("ring_z"):
        parts = exchange(parts, Z_RINGS)
    with jax.named_scope("back_late"):
        late = lax.ppermute(partner(other, far_up, far_up, far_down), AXES, CORE_SWAP)
    with jax.named_scope("input_grad"):
        weights = (near, up, down, far_up, far_down)
        input_grad = call(
            input_kernel,
            shape((SEQ, D)),
            (hidden_in, key_grad, gain, inv, *weights, early, late),
            (any_,) * 11,
            hbm,
            [
                pltpu.VMEM((SEQ, D), BF16),
                pltpu.VMEM((SEQ, K), BF16),
                pltpu.VMEM((1, D), F32),
                pltpu.VMEM((SEQ, 128), F32),
                pltpu.VMEM((16, 128, K), BF16),
                pltpu.VMEM((6, SEQ, COLS), BF16),
                pltpu.VMEM((2, SEQ, COLS), BF16),
                pltpu.VMEM((SEQ, D), F32),
                pltpu.VMEM((SEQ, D), BF16),
                dma((11,)),
                dma((4,)),
            ],
            mib=60,
        )
        parts, input_grad = barrier((parts, input_grad))
    with jax.named_scope("serve"):
        served = call(
            serve_kernel,
            shape((8, K)),
            (head_order.reshape(1, K), parts),
            (any_, vmem),
            vmem,
            [pltpu.VMEM((1, K), jnp.int32), dma],
        )
    return served, input_grad


def solution(mesh):
    in_specs = (P(AXES, None), P(AXES, None), P("fsdp", None), P(), P())
    out_specs = (P(AXES, None), P(AXES, None))
    return jax.shard_map(body, mesh=mesh, in_specs=in_specs, out_specs=out_specs, check_vma=False)
```

```python
import jax
import jax.numpy as jnp
from jax import lax
from jax.experimental import pallas as pl
from jax.experimental.pallas import tpu as pltpu
from jax.sharding import PartitionSpec as P

AXES = ("dp", "fsdp")
NX, NZH, NC, NY, NZL = 4, 2, 2, 4, 8
D, K = 4096, 512
SEQ = 256
TOKENS = SEQ * NX * NZH * NC * NY * NZL
COLS = 256
NORM_PARTS = 4
BF16, F32 = jnp.bfloat16, jnp.float32


def device(x, zh, c, y, zl):
    return (((x * NZH + zh) * NC + c) * NY + y) * NZL + zl


def places():
    return [
        (x, zh, c, y, zl)
        for x in range(NX)
        for zh in range(NZH)
        for c in range(NC)
        for y in range(NY)
        for zl in range(NZL)
    ]


def from_z(distance):
    pairs = []
    for x, zh, c, y, zl in places():
        z = (zh * NZL + zl + distance) % (NZH * NZL)
        pairs.append((device(x, z // NZL, c, y, z % NZL), device(x, zh, c, y, zl)))
    return pairs


def from_y(ahead):
    return [
        (device(x, zh, c, (y + ahead) % NY, zl), device(x, zh, c, y, zl))
        for x, zh, c, y, zl in places()
    ]


def origins():
    pairs = []
    for x, zh, c, y, zl in places():
        z = (zh * NZL + zl + c * (4 if zl % 2 == 0 else -4)) % (NZH * NZL)
        pairs.append((device(x, z // NZL, c, y, z % NZL), device(x, zh, c, y, zl)))
    return pairs


PLANES = [
    [device(x, zh, c, y, zl) for x in range(NX) for y in range(NY)]
    for zh in range(NZH)
    for c in range(NC)
    for zl in range(NZL)
]
Z_RINGS = [
    [device(x, zh, c, y, zl) for zh in range(NZH) for zl in range(NZL)]
    for x in range(NX)
    for c in range(NC)
    for y in range(NY)
]
CORE_SWAP = [(device(x, zh, c, y, zl), device(x, zh, 1 - c, y, zl)) for x, zh, c, y, zl in places()]


def exchange(value, groups):
    return lax.all_to_all(
        value, AXES, split_axis=0, concat_axis=0, axis_index_groups=groups, tiled=True
    )


def call(kernel, outs, ins, in_spaces, out_spaces, scratch=(), mib=24, us=0.05):
    return pl.pallas_call(
        kernel,
        out_shape=outs,
        in_specs=[pl.BlockSpec(memory_space=space) for space in in_spaces],
        out_specs=jax.tree.map(lambda space: pl.BlockSpec(memory_space=space), out_spaces),
        scratch_shapes=list(scratch),
        compiler_params=pltpu.CompilerParams(vmem_limit_bytes=mib and mib * 2**20),
        cost_estimate=pl.CostEstimate(
            flops=0, bytes_accessed=int(us * 3.0e6), transcendentals=0
        ),
    )(*ins)


def my_core():
    return lax.rem(lax.axis_index("dp"), NC)


def shape(dims, dtype=BF16):
    return jax.ShapeDtypeStruct(dims, dtype)


def start(source, target, sem):
    copy = pltpu.make_async_copy(source, target, sem)
    copy.start()
    return copy


def norm_kernel(
    hidden_hbm, key_hbm, gain_hbm, own_hbm, send_hbm, inv_hbm,
    hidden_ref, key_ref, gain_ref, own_ref, send_ref, inv_ref, in_sems, out_sems,
):
    core = my_core()
    step, parts, blocks = 16, NORM_PARTS, NX * NZH
    rows_each = SEQ // parts
    pieces = [pl.ds(i * rows_each, rows_each) for i in range(parts)]
    gain_copy = start(gain_hbm, gain_ref, in_sems.at[parts])
    copies = [
        start(hidden_hbm.at[rows], hidden_ref.at[rows], in_sems.at[i])
        for i, rows in enumerate(pieces)
    ]
    key_copy = start(key_hbm, key_ref, in_sems.at[parts + 1])

    def rows_of(i, carry):
        rows = pl.ds(pl.multiple_of(i * step, step), step)
        squares = jnp.zeros((step, 512), F32)
        for t in range(0, D, 512):
            values = hidden_ref[rows, t : t + 512].astype(F32)
            squares += values * values
        inv = lax.rsqrt(jnp.sum(squares, axis=-1, keepdims=True) * (1.0 / D) + 1e-06)
        inv_ref[rows, :] = jnp.broadcast_to(inv, (step, 128))
        for ref, part in ((own_ref, core), (send_ref, 1 - core)):
            for k in range(blocks):
                cols = pl.ds(pl.multiple_of((2 * k + part) * COLS, COLS), COLS)
                unit = hidden_ref[rows, cols].astype(F32) * inv
                ref[k, rows, :] = (unit * gain_ref[:, cols]).astype(BF16)
        return carry

    gain_copy.wait()
    out_copies = []
    for i, rows in enumerate(pieces):
        copies[i].wait()
        lax.fori_loop(i * rows_each // step, (i + 1) * rows_each // step, rows_of, 0, unroll=4)
        out_copies += [
            start(send_ref.at[:, rows], send_hbm.at[pl.ds(0, blocks), rows], out_sems.at[2 * i]),
            start(own_ref.at[:, rows], own_hbm.at[:, rows], out_sems.at[2 * i + 1]),
        ]
    key_copy.wait()
    for half in range(2):
        source = key_ref.at[:, pl.ds(half * COLS, COLS)]
        out_copies.append(start(source, send_hbm.at[blocks + half], out_sems.at[2 * parts + half]))
    out_copies.append(start(inv_ref, inv_hbm, out_sems.at[2 * parts + 2]))
    for copy in out_copies:
        copy.wait()


def column_kernel(*refs):
    *blocks, out_hbm, sems = refs
    copies = [start(block, out_hbm.at[j], sems.at[j]) for j, block in enumerate(blocks)]
    for copy in copies:
        copy.wait()


def partner_kernel(key_hbm, after_hbm, *refs):
    del after_hbm
    *sources, out_hbm, key_ref, weight_ref, out_ref, in_sems, out_sems = refs
    key_copy = start(key_hbm.at[pl.ds(NX * NZH, 2)], key_ref, in_sems.at[0])
    copies, place = [], 0
    for i, source in enumerate(sources):
        size = source.shape[0]
        target = weight_ref.at[pl.ds(place, size)]
        copies.append((start(source, target, in_sems.at[1 + i]), place // 2, size // 2))
        place += size
    key_copy.wait()
    keys = jnp.concatenate([key_ref[0], key_ref[1]], axis=1)
    out_copies = []
    for copy, first, size in copies:
        copy.wait()
        for block in range(first, first + size):
            weight = weight_ref[2 * block : 2 * block + 2].reshape(256, K)
            back = lax.dot_general(
                keys, weight, (((1,), (1,)), ((), ())), preferred_element_type=F32
            )
            out_ref[block] = back.astype(BF16)
            out_copies.append(start(out_ref.at[block], out_hbm.at[block], out_sems.at[block]))
    for copy in out_copies:
        copy.wait()


def partner(other, after, *sources):
    size = sum(source.shape[0] for source in sources)
    dma = pltpu.SemaphoreType.DMA
    return call(
        partner_kernel,
        shape((size // 2, SEQ, COLS)),
        (other, after, *sources),
        (pl.ANY,) * (2 + len(sources)),
        pltpu.HBM,
        [
            pltpu.VMEM((2, SEQ, COLS), BF16),
            pltpu.VMEM((size, 128, K), BF16),
            pltpu.VMEM((size // 2, SEQ, COLS), BF16),
            dma((1 + len(sources),)),
            dma((size // 2,)),
        ],
        mib=52,
    )


def square_kernel(
    own_hbm, other_hbm, key_hbm, out_hbm, own_ref, other_ref, key_ref, out_ref, in_sems, out_sems
):
    blocks = NX * NZH
    over_tokens = (((0,), (0,)), ((), ()))
    keys = [
        start(key_hbm, key_ref, in_sems.at[0]),
        start(other_hbm.at[pl.ds(blocks, 2)], other_ref.at[pl.ds(blocks, 2)], in_sems.at[1]),
    ]
    copies = []
    for part in range(4):
        some = pl.ds(2 * part, 2)
        copies += [
            start(own_hbm.at[some], own_ref.at[some], in_sems.at[2 + 2 * part]),
            start(other_hbm.at[some], other_ref.at[some], in_sems.at[3 + 2 * part]),
        ]
    for copy in keys:
        copy.wait()
    key_other = jnp.concatenate([other_ref[blocks], other_ref[blocks + 1]], axis=1)

    out_copies = []
    for k in range(blocks):
        x, zh = k // NZH, k % NZH
        if zh == 0:
            copies[2 * x].wait()
            copies[2 * x + 1].wait()
        g0 = lax.dot_general(own_ref[k], key_ref[...], over_tokens, preferred_element_type=F32)
        g1 = lax.dot_general(other_ref[k], key_other, over_tokens, preferred_element_type=F32)
        total = ((g0 * g0 + g1 * g1) * (1.0 / TOKENS)).astype(BF16)
        for y in range(NY):
            rows = slice(y * 64, (y + 1) * 64)
            out_ref[k, y, 0:64, :] = total[rows, 0:COLS]
            out_ref[k, y, 64:128, :] = total[rows, COLS:K]
            target = out_hbm.at[x * NY + y, pl.ds(zh * 128, 128)]
            out_copies.append(start(out_ref.at[k, y], target, out_sems.at[k, y]))
    for copy in out_copies:
        copy.wait()


def halves_kernel(up_hbm, down_hbm, up_half, down_half, sems):
    copies = [
        start(up_hbm.at[pl.ds(0, 2)], up_half, sems.at[0]),
        start(down_hbm.at[pl.ds(2, 2)], down_half, sems.at[1]),
    ]
    for copy in copies:
        copy.wait()


def split_kernel(in_ref, out_ref):
    for zh in range(NZH):
        rows = slice(zh * 128, (zh + 1) * 128)
        total = in_ref[0, rows, :].astype(F32)
        for j in range(1, NX * NY):
            total += in_ref[j, rows, :].astype(F32)
        total = total.reshape(2, NZL, 8, COLS)
        for zl in range(NZL):
            both = jnp.concatenate([total[0, zl], total[1, zl]], axis=0)
            out_ref[zh * NZL + zl] = both.astype(BF16)


def serve_kernel(order_hbm, in_ref, out_ref, order_ref, sem):
    copy = start(order_hbm, order_ref, sem)
    total = in_ref[0].astype(F32)
    for z in range(1, NZH * NZL):
        total += in_ref[z].astype(F32)
    fisher = jnp.concatenate([total[0:8], total[8:16]], axis=1).astype(BF16)
    copy.wait()
    column = lax.broadcasted_iota(jnp.int32, (K, K), 0)
    pick = jnp.where(column == order_ref[...], 1.0, 0.0).astype(BF16)
    out_ref[...] = jnp.dot(fisher, pick, preferred_element_type=F32).astype(BF16)


def input_kernel(
    hidden_hbm, key_hbm, gain_hbm, inv_hbm, weight_0, weight_1, weight_3, weight_2a, weight_2b,
    early_hbm, late_hbm, out_hbm,
    hidden_ref, key_ref, gain_ref, inv_ref, weight_ref, early_ref, late_ref, back_ref, out_ref,
    in_sems, out_sems,
):
    key_copy = start(key_hbm, key_ref, in_sems.at[0])
    groups = (
        (weight_0, 0, 0),
        (weight_1, 1, 0),
        (weight_3, 7, 0),
        (weight_2a, 2, 0),
        (weight_2b, 6, 2),
    )
    copies, blocks = [], []
    for i, (source, away, row) in enumerate(groups):
        size = source.shape[0]
        target = weight_ref.at[pl.ds(2 * len(blocks), size)]
        copies.append(start(source, target, in_sems.at[1 + i]))
        blocks += [(i, away, row + j) for j in range(0, size, 2)]
    second = [
        start(early_hbm, early_ref, in_sems.at[6]),
        start(late_hbm, late_ref, in_sems.at[7]),
        start(gain_hbm, gain_ref, in_sems.at[8]),
        start(inv_hbm, inv_ref, in_sems.at[9]),
        start(hidden_hbm, hidden_ref, in_sems.at[10]),
    ]
    core = my_core()
    z_here = lax.rem(lax.axis_index("fsdp"), NZL)
    y_here = lax.div(lax.axis_index("fsdp"), NZL)

    def put(back, origin, away, row):
        zl = (z_here + origin + away) & (NZL - 1)
        for half in range(2):
            y = (y_here + row + half) & (NY - 1)
            cols = pl.ds(pl.multiple_of((y * NZL + zl) * 128, 128), 128)
            back_ref[:, cols] = back[:, half * 128 : (half + 1) * 128]

    key_copy.wait()
    keys = key_ref[...]
    waited = 0
    for block, (group, away, row) in enumerate(blocks):
        if waited == group:
            copies[group].wait()
            waited += 1
        weight = weight_ref[2 * block : 2 * block + 2].reshape(256, K)
        back = lax.dot_general(keys, weight, (((1,), (1,)), ((), ())), preferred_element_type=F32)
        put(back, 4 * core, away, row)
    second[0].wait()
    second[1].wait()
    early = early_ref.shape[0]
    for block, (_, away, row) in enumerate(blocks):
        back = early_ref[block] if block < early else late_ref[block - early]
        put(back.astype(F32), 4 * (1 - core), away, row)
    for copy in second[2:]:
        copy.wait()

    step, parts, width = 16, 4, 512

    def rows_of(i, carry):
        rows = pl.ds(pl.multiple_of(i * step, step), step)
        inv = inv_ref[rows, 0:1]
        total = jnp.zeros((step, width), F32)
        for t in range(0, D, width):
            cols = slice(t, t + width)
            du = back_ref[rows, cols] * gain_ref[:, cols]
            total += du * hidden_ref[rows, cols].astype(F32)
        mean = inv * jnp.sum(total, axis=-1, keepdims=True) * (1.0 / D)
        factor = inv * inv * mean
        for t in range(0, D, width):
            cols = slice(t, t + width)
            du = back_ref[rows, cols] * gain_ref[:, cols]
            out = du * inv - hidden_ref[rows, cols].astype(F32) * factor
            out_ref[rows, cols] = out.astype(BF16)
        return carry

    rows_each = SEQ // parts
    copies = []
    for i in range(parts):
        lax.fori_loop(i * rows_each // step, (i + 1) * rows_each // step, rows_of, 0, unroll=4)
        rows = pl.ds(i * rows_each, rows_each)
        copies.append(start(out_ref.at[rows], out_hbm.at[rows], out_sems.at[i]))
    for copy in copies:
        copy.wait()


def body(hidden_in, key_grad, key_weight, norm_gain, head_order):
    gain = norm_gain.reshape(1, D)
    vmem, hbm, any_ = pltpu.VMEM, pltpu.HBM, pl.ANY
    dma = pltpu.SemaphoreType.DMA
    blocks = NX * NZH
    barrier = lax.optimization_barrier

    with jax.named_scope("weight_z4"):
        origin = lax.ppermute(key_weight, AXES, origins())
    with jax.named_scope("norm"):
        own, send, inv = call(
            norm_kernel,
            (shape((blocks, SEQ, COLS)), shape((blocks + 2, SEQ, COLS)), shape((SEQ, 128), F32)),
            (hidden_in, key_grad, gain),
            (any_,) * 3,
            (hbm, hbm, hbm),
            [
                pltpu.VMEM((SEQ, D), BF16),
                pltpu.VMEM((SEQ, K), BF16),
                pltpu.VMEM((1, D), F32),
                pltpu.VMEM((blocks, SEQ, COLS), BF16),
                pltpu.VMEM((blocks, SEQ, COLS), BF16),
                pltpu.VMEM((SEQ, 128), F32),
                dma((NORM_PARTS + 2,)),
                dma((2 * NORM_PARTS + 3,)),
            ],
            mib=None,
        )
        origin, send = barrier((origin, send))
        other = lax.ppermute(send, AXES, CORE_SWAP)
    with jax.named_scope("squares"):
        chunks = call(
            square_kernel,
            shape((NX * NY, 256, COLS)),
            (own, other, key_grad),
            (any_,) * 3,
            hbm,
            [
                pltpu.VMEM((blocks, SEQ, COLS), BF16),
                pltpu.VMEM((blocks + 2, SEQ, COLS), BF16),
                pltpu.VMEM((SEQ, K), BF16),
                pltpu.VMEM((blocks, NY, 128, COLS), BF16),
                dma((10,)),
                dma((blocks, NY)),
            ],
            mib=60,
        )
    with jax.named_scope("weight_y"):
        column = [origin] + [lax.ppermute(origin, AXES, from_y(ahead)) for ahead in (1, 2, 3)]
        chunks, *column = barrier((chunks, *column))
    with jax.named_scope("plane"):
        chunks = exchange(chunks, PLANES)
    with jax.named_scope("weight_y"):
        near = call(
            column_kernel, shape((NY, 128, K)), column, (any_,) * NY, hbm, [dma((NY,))], mib=52
        )
    with jax.named_scope("weight_z1"):
        up = lax.ppermute(near, AXES, from_z(1))
        down = lax.ppermute(near, AXES, from_z(-1))
    with jax.named_scope("weight_z2"):
        half = shape((2, 128, K))
        up_half, down_half = call(
            halves_kernel, (half, half), (up, down), (any_, any_), (hbm, hbm), [dma((2,))], mib=52
        )
        far_up = lax.ppermute(up_half, AXES, from_z(1))
        far_down = lax.ppermute(down_half, AXES, from_z(-1))
    with jax.named_scope("back_early"):
        early = lax.ppermute(partner(other, up_half, near, up, down), AXES, CORE_SWAP)
    with jax.named_scope("split"):
        parts = call(split_kernel, shape((NZH * NZL, 16, COLS)), (chunks,), (vmem,), vmem)
    with jax.named_scope("ring_z"):
        parts = exchange(parts, Z_RINGS)
    with jax.named_scope("back_late"):
        late = lax.ppermute(partner(other, far_up, far_up, far_down), AXES, CORE_SWAP)
    with jax.named_scope("input_grad"):
        weights = (near, up, down, far_up, far_down)
        input_grad = call(
            input_kernel,
            shape((SEQ, D)),
            (hidden_in, key_grad, gain, inv, *weights, early, late),
            (any_,) * 11,
            hbm,
            [
                pltpu.VMEM((SEQ, D), BF16),
                pltpu.VMEM((SEQ, K), BF16),
                pltpu.VMEM((1, D), F32),
                pltpu.VMEM((SEQ, 128), F32),
                pltpu.VMEM((16, 128, K), BF16),
                pltpu.VMEM((6, SEQ, COLS), BF16),
                pltpu.VMEM((2, SEQ, COLS), BF16),
                pltpu.VMEM((SEQ, D), F32),
                pltpu.VMEM((SEQ, D), BF16),
                dma((11,)),
                dma((4,)),
            ],
            mib=60,
        )
        parts, input_grad = barrier((parts, input_grad))
    with jax.named_scope("serve"):
        served = call(
            serve_kernel,
            shape((8, K)),
            (head_order.reshape(1, K), parts),
            (any_, vmem),
            vmem,
            [pltpu.VMEM((1, K), jnp.int32), dma],
        )
    return served, input_grad


def solution(mesh):
    in_specs = (P(AXES, None), P(AXES, None), P("fsdp", None), P(), P())
    out_specs = (P(AXES, None), P(AXES, None))
    return jax.shard_map(body, mesh=mesh, in_specs=in_specs, out_specs=out_specs, check_vma=False)
```

```python
import jax
import jax.numpy as jnp
from jax import lax
from jax.experimental import pallas as pl
from jax.experimental.pallas import tpu as pltpu
from jax.sharding import PartitionSpec as P

AXES = ("dp", "fsdp")
NX, NZH, NC, NY, NZL = 4, 2, 2, 4, 8
D, K = 4096, 512
SEQ = 256
TOKENS = SEQ * NX * NZH * NC * NY * NZL
COLS = 256
NORM_PARTS = 4
BF16, F32 = jnp.bfloat16, jnp.float32


def device(x, zh, c, y, zl):
    return (((x * NZH + zh) * NC + c) * NY + y) * NZL + zl


def places():
    return [
        (x, zh, c, y, zl)
        for x in range(NX)
        for zh in range(NZH)
        for c in range(NC)
        for y in range(NY)
        for zl in range(NZL)
    ]


def from_z(distance):
    pairs = []
    for x, zh, c, y, zl in places():
        z = (zh * NZL + zl + distance) % (NZH * NZL)
        pairs.append((device(x, z // NZL, c, y, z % NZL), device(x, zh, c, y, zl)))
    return pairs


def two_away():
    pairs = []
    for x, zh, c, y, zl in places():
        z = (zh * NZL + zl + (2 if zl % 2 == 0 else -2)) % (NZH * NZL)
        pairs.append((device(x, z // NZL, c, y, z % NZL), device(x, zh, c, y, zl)))
    return pairs


def from_y(ahead):
    return [
        (device(x, zh, c, (y + ahead) % NY, zl), device(x, zh, c, y, zl))
        for x, zh, c, y, zl in places()
    ]


def origins():
    pairs = []
    for x, zh, c, y, zl in places():
        z = (zh * NZL + zl + c * (4 if zl % 2 == 0 else -4)) % (NZH * NZL)
        pairs.append((device(x, z // NZL, c, y, z % NZL), device(x, zh, c, y, zl)))
    return pairs


PLANES = [
    [device(x, zh, c, y, zl) for x in range(NX) for y in range(NY)]
    for zh in range(NZH)
    for c in range(NC)
    for zl in range(NZL)
]
Z_RINGS = [
    [device(x, zh, c, y, zl) for zh in range(NZH) for zl in range(NZL)]
    for x in range(NX)
    for c in range(NC)
    for y in range(NY)
]
CORE_SWAP = [(device(x, zh, c, y, zl), device(x, zh, 1 - c, y, zl)) for x, zh, c, y, zl in places()]


def exchange(value, groups):
    return lax.all_to_all(
        value, AXES, split_axis=0, concat_axis=0, axis_index_groups=groups, tiled=True
    )


def call(kernel, outs, ins, in_spaces, out_spaces, scratch=(), mib=24, us=0.05):
    return pl.pallas_call(
        kernel,
        out_shape=outs,
        in_specs=[pl.BlockSpec(memory_space=space) for space in in_spaces],
        out_specs=jax.tree.map(lambda space: pl.BlockSpec(memory_space=space), out_spaces),
        scratch_shapes=list(scratch),
        compiler_params=pltpu.CompilerParams(vmem_limit_bytes=mib and mib * 2**20),
        cost_estimate=pl.CostEstimate(
            flops=0, bytes_accessed=int(us * 3.0e6), transcendentals=0
        ),
    )(*ins)


def my_core():
    return lax.rem(lax.axis_index("dp"), NC)


def shape(dims, dtype=BF16):
    return jax.ShapeDtypeStruct(dims, dtype)


def start(source, target, sem):
    copy = pltpu.make_async_copy(source, target, sem)
    copy.start()
    return copy


def norm_kernel(
    hidden_hbm, key_hbm, gain_hbm, own_hbm, send_hbm, inv_hbm,
    hidden_ref, key_ref, gain_ref, own_ref, send_ref, inv_ref, in_sems, out_sems,
):
    core = my_core()
    step, parts, blocks = 16, NORM_PARTS, NX * NZH
    rows_each = SEQ // parts
    pieces = [pl.ds(i * rows_each, rows_each) for i in range(parts)]
    gain_copy = start(gain_hbm, gain_ref, in_sems.at[parts])
    copies = [
        start(hidden_hbm.at[rows], hidden_ref.at[rows], in_sems.at[i])
        for i, rows in enumerate(pieces)
    ]
    key_copy = start(key_hbm, key_ref, in_sems.at[parts + 1])

    def rows_of(i, carry):
        rows = pl.ds(pl.multiple_of(i * step, step), step)
        squares = jnp.zeros((step, 512), F32)
        for t in range(0, D, 512):
            values = hidden_ref[rows, t : t + 512].astype(F32)
            squares += values * values
        inv = lax.rsqrt(jnp.sum(squares, axis=-1, keepdims=True) * (1.0 / D) + 1e-06)
        inv_ref[rows, :] = jnp.broadcast_to(inv, (step, 128))
        for ref, part in ((own_ref, core), (send_ref, 1 - core)):
            for k in range(blocks):
                cols = pl.ds(pl.multiple_of((2 * k + part) * COLS, COLS), COLS)
                unit = hidden_ref[rows, cols].astype(F32) * inv
                ref[k, rows, :] = (unit * gain_ref[:, cols]).astype(BF16)
        return carry

    gain_copy.wait()
    out_copies = []
    for i, rows in enumerate(pieces):
        copies[i].wait()
        lax.fori_loop(i * rows_each // step, (i + 1) * rows_each // step, rows_of, 0, unroll=4)
        out_copies += [
            start(send_ref.at[:, rows], send_hbm.at[pl.ds(0, blocks), rows], out_sems.at[2 * i]),
            start(own_ref.at[:, rows], own_hbm.at[:, rows], out_sems.at[2 * i + 1]),
        ]
    key_copy.wait()
    for half in range(2):
        source = key_ref.at[:, pl.ds(half * COLS, COLS)]
        out_copies.append(start(source, send_hbm.at[blocks + half], out_sems.at[2 * parts + half]))
    out_copies.append(start(inv_ref, inv_hbm, out_sems.at[2 * parts + 2]))
    for copy in out_copies:
        copy.wait()


def column_kernel(*refs):
    *blocks, out_hbm, sems = refs
    copies = [start(block, out_hbm.at[j], sems.at[j]) for j, block in enumerate(blocks)]
    for copy in copies:
        copy.wait()


def partner_kernel(key_hbm, *refs):
    *sources, out_hbm, key_ref, weight_ref, out_ref, in_sems, out_sems = refs
    key_copy = start(key_hbm.at[pl.ds(NX * NZH, 2)], key_ref, in_sems.at[0])
    copies, place = [], 0
    for i, source in enumerate(sources):
        size = source.shape[0]
        target = weight_ref.at[pl.ds(place, size)]
        copies.append((start(source, target, in_sems.at[1 + i]), place // 2, size // 2))
        place += size
    key_copy.wait()
    keys = jnp.concatenate([key_ref[0], key_ref[1]], axis=1)
    out_copies = []
    for copy, first, size in copies:
        copy.wait()
        for block in range(first, first + size):
            weight = weight_ref[2 * block : 2 * block + 2].reshape(256, K)
            back = lax.dot_general(
                keys, weight, (((1,), (1,)), ((), ())), preferred_element_type=F32
            )
            out_ref[block] = back.astype(BF16)
            out_copies.append(start(out_ref.at[block], out_hbm.at[block], out_sems.at[block]))
    for copy in out_copies:
        copy.wait()


def partner(other, *sources):
    size = sum(source.shape[0] for source in sources)
    dma = pltpu.SemaphoreType.DMA
    return call(
        partner_kernel,
        shape((size // 2, SEQ, COLS)),
        (other, *sources),
        (pl.ANY,) * (1 + len(sources)),
        pltpu.HBM,
        [
            pltpu.VMEM((2, SEQ, COLS), BF16),
            pltpu.VMEM((size, 128, K), BF16),
            pltpu.VMEM((size // 2, SEQ, COLS), BF16),
            dma((1 + len(sources),)),
            dma((size // 2,)),
        ],
        mib=52,
    )


def square_kernel(
    own_hbm, other_hbm, key_hbm, out_hbm, own_ref, other_ref, key_ref, out_ref, in_sems, out_sems
):
    blocks = NX * NZH
    over_tokens = (((0,), (0,)), ((), ()))
    keys = [
        start(key_hbm, key_ref, in_sems.at[0]),
        start(other_hbm.at[pl.ds(blocks, 2)], other_ref.at[pl.ds(blocks, 2)], in_sems.at[1]),
    ]
    copies = []
    for part in range(4):
        some = pl.ds(2 * part, 2)
        copies += [
            start(own_hbm.at[some], own_ref.at[some], in_sems.at[2 + 2 * part]),
            start(other_hbm.at[some], other_ref.at[some], in_sems.at[3 + 2 * part]),
        ]
    for copy in keys:
        copy.wait()
    key_other = jnp.concatenate([other_ref[blocks], other_ref[blocks + 1]], axis=1)

    out_copies = []
    for k in range(blocks):
        x, zh = k // NZH, k % NZH
        if zh == 0:
            copies[2 * x].wait()
            copies[2 * x + 1].wait()
        g0 = lax.dot_general(own_ref[k], key_ref[...], over_tokens, preferred_element_type=F32)
        g1 = lax.dot_general(other_ref[k], key_other, over_tokens, preferred_element_type=F32)
        total = ((g0 * g0 + g1 * g1) * (1.0 / TOKENS)).astype(BF16)
        for y in range(NY):
            rows = slice(y * 64, (y + 1) * 64)
            out_ref[k, y, 0:64, :] = total[rows, 0:COLS]
            out_ref[k, y, 64:128, :] = total[rows, COLS:K]
            target = out_hbm.at[x * NY + y, pl.ds(zh * 128, 128)]
            out_copies.append(start(out_ref.at[k, y], target, out_sems.at[k, y]))
    for copy in out_copies:
        copy.wait()


def split_kernel(in_ref, out_ref):
    for zh in range(NZH):
        rows = slice(zh * 128, (zh + 1) * 128)
        total = in_ref[0, rows, :].astype(F32)
        for j in range(1, NX * NY):
            total += in_ref[j, rows, :].astype(F32)
        total = total.reshape(2, NZL, 8, COLS)
        for zl in range(NZL):
            both = jnp.concatenate([total[0, zl], total[1, zl]], axis=0)
            out_ref[zh * NZL + zl] = both.astype(BF16)


def serve_kernel(order_hbm, in_ref, out_ref, order_ref, sem):
    copy = start(order_hbm, order_ref, sem)
    total = in_ref[0].astype(F32)
    for z in range(1, NZH * NZL):
        total += in_ref[z].astype(F32)
    fisher = jnp.concatenate([total[0:8], total[8:16]], axis=1).astype(BF16)
    copy.wait()
    column = lax.broadcasted_iota(jnp.int32, (K, K), 0)
    pick = jnp.where(column == order_ref[...], 1.0, 0.0).astype(BF16)
    out_ref[...] = jnp.dot(fisher, pick, preferred_element_type=F32).astype(BF16)


def input_kernel(
    hidden_hbm, key_hbm, gain_hbm, inv_hbm, weight_0, weight_1, weight_3, weight_2,
    early_hbm, late_hbm, out_hbm,
    hidden_ref, key_ref, gain_ref, inv_ref, weight_ref, early_ref, late_ref, back_ref, out_ref,
    in_sems, out_sems,
):
    key_copy = start(key_hbm, key_ref, in_sems.at[0])
    core = my_core()
    z_here = lax.rem(lax.axis_index("fsdp"), NZL)
    y_here = lax.div(lax.axis_index("fsdp"), NZL)
    groups = (
        (weight_0, 0),
        (weight_1, 1),
        (weight_3, 7),
        (weight_2, jnp.where((z_here & 1) == 0, 2, 6)),
    )
    copies, blocks = [], []
    for i, (source, away) in enumerate(groups):
        size = source.shape[0]
        target = weight_ref.at[pl.ds(2 * len(blocks), size)]
        copies.append(start(source, target, in_sems.at[1 + i]))
        blocks += [(i, away, row) for row in range(0, size, 2)]
    second = [
        start(early_hbm, early_ref, in_sems.at[5]),
        start(late_hbm, late_ref, in_sems.at[6]),
        start(gain_hbm, gain_ref, in_sems.at[7]),
        start(inv_hbm, inv_ref, in_sems.at[8]),
        start(hidden_hbm, hidden_ref, in_sems.at[9]),
    ]

    def put(back, origin, away, row):
        zl = (z_here + origin + away) & (NZL - 1)
        for half in range(2):
            y = (y_here + row + half) & (NY - 1)
            cols = pl.ds(pl.multiple_of((y * NZL + zl) * 128, 128), 128)
            back_ref[:, cols] = back[:, half * 128 : (half + 1) * 128]

    key_copy.wait()
    keys = key_ref[...]
    waited = 0
    for block, (group, away, row) in enumerate(blocks):
        if waited == group:
            copies[group].wait()
            waited += 1
        weight = weight_ref[2 * block : 2 * block + 2].reshape(256, K)
        back = lax.dot_general(keys, weight, (((1,), (1,)), ((), ())), preferred_element_type=F32)
        put(back, 4 * core, away, row)
    second[0].wait()
    second[1].wait()
    early = early_ref.shape[0]
    for block, (_, away, row) in enumerate(blocks):
        back = early_ref[block] if block < early else late_ref[block - early]
        put(back.astype(F32), 4 * (1 - core), away, row)
    for copy in second[2:]:
        copy.wait()

    step, parts, width = 16, 4, 512

    def rows_of(i, carry):
        rows = pl.ds(pl.multiple_of(i * step, step), step)
        inv = inv_ref[rows, 0:1]
        total = jnp.zeros((step, width), F32)
        for t in range(0, D, width):
            cols = slice(t, t + width)
            du = back_ref[rows, cols] * gain_ref[:, cols]
            total += du * hidden_ref[rows, cols].astype(F32)
        mean = inv * jnp.sum(total, axis=-1, keepdims=True) * (1.0 / D)
        factor = inv * inv * mean
        for t in range(0, D, width):
            cols = slice(t, t + width)
            du = back_ref[rows, cols] * gain_ref[:, cols]
            out = du * inv - hidden_ref[rows, cols].astype(F32) * factor
            out_ref[rows, cols] = out.astype(BF16)
        return carry

    rows_each = SEQ // parts
    copies = []
    for i in range(parts):
        lax.fori_loop(i * rows_each // step, (i + 1) * rows_each // step, rows_of, 0, unroll=4)
        rows = pl.ds(i * rows_each, rows_each)
        copies.append(start(out_ref.at[rows], out_hbm.at[rows], out_sems.at[i]))
    for copy in copies:
        copy.wait()


def body(hidden_in, key_grad, key_weight, norm_gain, head_order):
    gain = norm_gain.reshape(1, D)
    vmem, hbm, any_ = pltpu.VMEM, pltpu.HBM, pl.ANY
    dma = pltpu.SemaphoreType.DMA
    blocks = NX * NZH
    barrier = lax.optimization_barrier

    with jax.named_scope("weight_z4"):
        origin = lax.ppermute(key_weight, AXES, origins())
    with jax.named_scope("norm"):
        own, send, inv = call(
            norm_kernel,
            (shape((blocks, SEQ, COLS)), shape((blocks + 2, SEQ, COLS)), shape((SEQ, 128), F32)),
            (hidden_in, key_grad, gain),
            (any_,) * 3,
            (hbm, hbm, hbm),
            [
                pltpu.VMEM((SEQ, D), BF16),
                pltpu.VMEM((SEQ, K), BF16),
                pltpu.VMEM((1, D), F32),
                pltpu.VMEM((blocks, SEQ, COLS), BF16),
                pltpu.VMEM((blocks, SEQ, COLS), BF16),
                pltpu.VMEM((SEQ, 128), F32),
                dma((NORM_PARTS + 2,)),
                dma((2 * NORM_PARTS + 3,)),
            ],
            mib=None,
        )
        origin, send = barrier((origin, send))
        other = lax.ppermute(send, AXES, CORE_SWAP)
    with jax.named_scope("squares"):
        chunks = call(
            square_kernel,
            shape((NX * NY, 256, COLS)),
            (own, other, key_grad),
            (any_,) * 3,
            hbm,
            [
                pltpu.VMEM((blocks, SEQ, COLS), BF16),
                pltpu.VMEM((blocks + 2, SEQ, COLS), BF16),
                pltpu.VMEM((SEQ, K), BF16),
                pltpu.VMEM((blocks, NY, 128, COLS), BF16),
                dma((10,)),
                dma((blocks, NY)),
            ],
            mib=60,
        )
    with jax.named_scope("weight_y"):
        column = [origin] + [lax.ppermute(origin, AXES, from_y(ahead)) for ahead in (1, 2, 3)]
        chunks, *column = barrier((chunks, *column))
    with jax.named_scope("plane"):
        chunks = exchange(chunks, PLANES)
    with jax.named_scope("weight_y"):
        near = call(
            column_kernel, shape((NY, 128, K)), column, (any_,) * NY, hbm, [dma((NY,))], mib=52
        )
    with jax.named_scope("weight_z1"):
        up = lax.ppermute(near, AXES, from_z(1))
        down = lax.ppermute(near, AXES, from_z(-1))
        far = lax.ppermute(near, AXES, two_away())
    with jax.named_scope("back_early"):
        early = lax.ppermute(partner(other, near, up, down), AXES, CORE_SWAP)
    with jax.named_scope("split"):
        parts = call(split_kernel, shape((NZH * NZL, 16, COLS)), (chunks,), (vmem,), vmem)
    with jax.named_scope("ring_z"):
        parts = exchange(parts, Z_RINGS)
    with jax.named_scope("back_late"):
        late = lax.ppermute(partner(other, far), AXES, CORE_SWAP)
    with jax.named_scope("input_grad"):
        weights = (near, up, down, far)
        input_grad = call(
            input_kernel,
            shape((SEQ, D)),
            (hidden_in, key_grad, gain, inv, *weights, early, late),
            (any_,) * 10,
            hbm,
            [
                pltpu.VMEM((SEQ, D), BF16),
                pltpu.VMEM((SEQ, K), BF16),
                pltpu.VMEM((1, D), F32),
                pltpu.VMEM((SEQ, 128), F32),
                pltpu.VMEM((16, 128, K), BF16),
                pltpu.VMEM((6, SEQ, COLS), BF16),
                pltpu.VMEM((2, SEQ, COLS), BF16),
                pltpu.VMEM((SEQ, D), F32),
                pltpu.VMEM((SEQ, D), BF16),
                dma((10,)),
                dma((4,)),
            ],
            mib=60,
        )
        parts, input_grad = barrier((parts, input_grad))
    with jax.named_scope("serve"):
        served = call(
            serve_kernel,
            shape((8, K)),
            (head_order.reshape(1, K), parts),
            (any_, vmem),
            vmem,
            [pltpu.VMEM((1, K), jnp.int32), dma],
        )
    return served, input_grad


def solution(mesh):
    in_specs = (P(AXES, None), P(AXES, None), P("fsdp", None), P(), P())
    out_specs = (P(AXES, None), P(AXES, None))
    return jax.shard_map(body, mesh=mesh, in_specs=in_specs, out_specs=out_specs, check_vma=False)
```

```python
import jax
import jax.numpy as jnp
from jax import lax
from jax.experimental import pallas as pl
from jax.experimental.pallas import tpu as pltpu
from jax.sharding import PartitionSpec as P

AXES = ("dp", "fsdp")
NX, NZH, NC, NY, NZL = 4, 2, 2, 4, 8
D, K = 4096, 512
SEQ = 256
TOKENS = SEQ * NX * NZH * NC * NY * NZL
COLS = 256
NORM_PARTS = 4
BF16, F32 = jnp.bfloat16, jnp.float32


def device(x, zh, c, y, zl):
    return (((x * NZH + zh) * NC + c) * NY + y) * NZL + zl


def places():
    return [
        (x, zh, c, y, zl)
        for x in range(NX)
        for zh in range(NZH)
        for c in range(NC)
        for y in range(NY)
        for zl in range(NZL)
    ]


def from_z(distance):
    pairs = []
    for x, zh, c, y, zl in places():
        z = (zh * NZL + zl + distance) % (NZH * NZL)
        pairs.append((device(x, z // NZL, c, y, z % NZL), device(x, zh, c, y, zl)))
    return pairs


def two_away():
    pairs = []
    for x, zh, c, y, zl in places():
        z = (zh * NZL + zl + (2 if zl % 2 == 0 else -2)) % (NZH * NZL)
        pairs.append((device(x, z // NZL, c, y, z % NZL), device(x, zh, c, y, zl)))
    return pairs


def origins():
    pairs = []
    for x, zh, c, y, zl in places():
        z = (zh * NZL + zl + c * (4 if zl % 2 == 0 else -4)) % (NZH * NZL)
        pairs.append((device(x, z // NZL, c, y, z % NZL), device(x, zh, c, y, zl)))
    return pairs


Y_RINGS = [
    [device(x, zh, c, y, zl) for y in range(NY)]
    for x in range(NX)
    for zh in range(NZH)
    for c in range(NC)
    for zl in range(NZL)
]
PLANES = [
    [device(x, zh, c, y, zl) for x in range(NX) for y in range(NY)]
    for zh in range(NZH)
    for c in range(NC)
    for zl in range(NZL)
]
Z_RINGS = [
    [device(x, zh, c, y, zl) for zh in range(NZH) for zl in range(NZL)]
    for x in range(NX)
    for c in range(NC)
    for y in range(NY)
]
CORE_SWAP = [(device(x, zh, c, y, zl), device(x, zh, 1 - c, y, zl)) for x, zh, c, y, zl in places()]


def exchange(value, groups):
    return lax.all_to_all(
        value, AXES, split_axis=0, concat_axis=0, axis_index_groups=groups, tiled=True
    )


def call(kernel, outs, ins, in_spaces, out_spaces, scratch=(), mib=24, us=0.05):
    return pl.pallas_call(
        kernel,
        out_shape=outs,
        in_specs=[pl.BlockSpec(memory_space=space) for space in in_spaces],
        out_specs=jax.tree.map(lambda space: pl.BlockSpec(memory_space=space), out_spaces),
        scratch_shapes=list(scratch),
        compiler_params=pltpu.CompilerParams(vmem_limit_bytes=mib and mib * 2**20),
        cost_estimate=pl.CostEstimate(
            flops=0, bytes_accessed=int(us * 3.0e6), transcendentals=0
        ),
    )(*ins)


def my_core():
    return lax.rem(lax.axis_index("dp"), NC)


def shape(dims, dtype=BF16):
    return jax.ShapeDtypeStruct(dims, dtype)


def start(source, target, sem):
    copy = pltpu.make_async_copy(source, target, sem)
    copy.start()
    return copy


def norm_kernel(
    hidden_hbm, key_hbm, gain_hbm, own_hbm, send_hbm, inv_hbm,
    hidden_ref, key_ref, gain_ref, own_ref, send_ref, inv_ref, in_sems, out_sems,
):
    core = my_core()
    step, parts, blocks = 16, NORM_PARTS, NX * NZH
    rows_each = SEQ // parts
    pieces = [pl.ds(i * rows_each, rows_each) for i in range(parts)]
    gain_copy = start(gain_hbm, gain_ref, in_sems.at[parts])
    copies = [
        start(hidden_hbm.at[rows], hidden_ref.at[rows], in_sems.at[i])
        for i, rows in enumerate(pieces)
    ]
    key_copy = start(key_hbm, key_ref, in_sems.at[parts + 1])

    def rows_of(i, carry):
        rows = pl.ds(pl.multiple_of(i * step, step), step)
        squares = jnp.zeros((step, 512), F32)
        for t in range(0, D, 512):
            values = hidden_ref[rows, t : t + 512].astype(F32)
            squares += values * values
        inv = lax.rsqrt(jnp.sum(squares, axis=-1, keepdims=True) * (1.0 / D) + 1e-06)
        inv_ref[rows, :] = jnp.broadcast_to(inv, (step, 128))
        for ref, part in ((own_ref, core), (send_ref, 1 - core)):
            for k in range(blocks):
                cols = pl.ds(pl.multiple_of((2 * k + part) * COLS, COLS), COLS)
                unit = hidden_ref[rows, cols].astype(F32) * inv
                ref[k, rows, :] = (unit * gain_ref[:, cols]).astype(BF16)
        return carry

    gain_copy.wait()
    out_copies = []
    for i, rows in enumerate(pieces):
        copies[i].wait()
        lax.fori_loop(i * rows_each // step, (i + 1) * rows_each // step, rows_of, 0, unroll=4)
        out_copies += [
            start(send_ref.at[:, rows], send_hbm.at[pl.ds(0, blocks), rows], out_sems.at[2 * i]),
            start(own_ref.at[:, rows], own_hbm.at[:, rows], out_sems.at[2 * i + 1]),
        ]
    key_copy.wait()
    for half in range(2):
        source = key_ref.at[:, pl.ds(half * COLS, COLS)]
        out_copies.append(start(source, send_hbm.at[blocks + half], out_sems.at[2 * parts + half]))
    out_copies.append(start(inv_ref, inv_hbm, out_sems.at[2 * parts + 2]))
    for copy in out_copies:
        copy.wait()


def partner_kernel(key_hbm, *refs):
    *sources, out_hbm, key_ref, weight_ref, out_ref, in_sems, out_sems = refs
    key_copy = start(key_hbm.at[pl.ds(NX * NZH, 2)], key_ref, in_sems.at[0])
    copies, place = [], 0
    for i, source in enumerate(sources):
        size = source.shape[0]
        target = weight_ref.at[pl.ds(place, size)]
        copies.append((start(source, target, in_sems.at[1 + i]), place // 2, size // 2))
        place += size
    key_copy.wait()
    keys = jnp.concatenate([key_ref[0], key_ref[1]], axis=1)
    out_copies = []
    for copy, first, size in copies:
        copy.wait()
        for block in range(first, first + size):
            weight = weight_ref[2 * block : 2 * block + 2].reshape(256, K)
            back = lax.dot_general(
                keys, weight, (((1,), (1,)), ((), ())), preferred_element_type=F32
            )
            out_ref[block] = back.astype(BF16)
            out_copies.append(start(out_ref.at[block], out_hbm.at[block], out_sems.at[block]))
    for copy in out_copies:
        copy.wait()


def partner(other, *sources):
    size = sum(source.shape[0] for source in sources)
    dma = pltpu.SemaphoreType.DMA
    return call(
        partner_kernel,
        shape((size // 2, SEQ, COLS)),
        (other, *sources),
        (pl.ANY,) * (1 + len(sources)),
        pltpu.HBM,
        [
            pltpu.VMEM((2, SEQ, COLS), BF16),
            pltpu.VMEM((size, 128, K), BF16),
            pltpu.VMEM((size // 2, SEQ, COLS), BF16),
            dma((1 + len(sources),)),
            dma((size // 2,)),
        ],
        mib=52,
    )


def square_kernel(
    own_hbm, other_hbm, key_hbm, out_hbm, own_ref, other_ref, key_ref, out_ref, in_sems, out_sems
):
    blocks = NX * NZH
    over_tokens = (((0,), (0,)), ((), ()))
    keys = [
        start(key_hbm, key_ref, in_sems.at[0]),
        start(other_hbm.at[pl.ds(blocks, 2)], other_ref.at[pl.ds(blocks, 2)], in_sems.at[1]),
    ]
    copies = []
    for part in range(4):
        some = pl.ds(2 * part, 2)
        copies += [
            start(own_hbm.at[some], own_ref.at[some], in_sems.at[2 + 2 * part]),
            start(other_hbm.at[some], other_ref.at[some], in_sems.at[3 + 2 * part]),
        ]
    for copy in keys:
        copy.wait()
    key_other = jnp.concatenate([other_ref[blocks], other_ref[blocks + 1]], axis=1)

    out_copies = []
    for k in range(blocks):
        x, zh = k // NZH, k % NZH
        if zh == 0:
            copies[2 * x].wait()
            copies[2 * x + 1].wait()
        g0 = lax.dot_general(own_ref[k], key_ref[...], over_tokens, preferred_element_type=F32)
        g1 = lax.dot_general(other_ref[k], key_other, over_tokens, preferred_element_type=F32)
        total = ((g0 * g0 + g1 * g1) * (1.0 / TOKENS)).astype(BF16)
        for y in range(NY):
            rows = slice(y * 64, (y + 1) * 64)
            out_ref[k, y, 0:64, :] = total[rows, 0:COLS]
            out_ref[k, y, 64:128, :] = total[rows, COLS:K]
            target = out_hbm.at[x * NY + y, pl.ds(zh * 128, 128)]
            out_copies.append(start(out_ref.at[k, y], target, out_sems.at[k, y]))
    for copy in out_copies:
        copy.wait()


def split_kernel(in_ref, out_ref):
    for zh in range(NZH):
        rows = slice(zh * 128, (zh + 1) * 128)
        total = in_ref[0, rows, :].astype(F32)
        for j in range(1, NX * NY):
            total += in_ref[j, rows, :].astype(F32)
        total = total.reshape(2, NZL, 8, COLS)
        for zl in range(NZL):
            both = jnp.concatenate([total[0, zl], total[1, zl]], axis=0)
            out_ref[zh * NZL + zl] = both.astype(BF16)


def serve_kernel(order_hbm, in_ref, out_ref, order_ref, sem):
    copy = start(order_hbm, order_ref, sem)
    total = in_ref[0].astype(F32)
    for z in range(1, NZH * NZL):
        total += in_ref[z].astype(F32)
    fisher = jnp.concatenate([total[0:8], total[8:16]], axis=1).astype(BF16)
    copy.wait()
    column = lax.broadcasted_iota(jnp.int32, (K, K), 0)
    pick = jnp.where(column == order_ref[...], 1.0, 0.0).astype(BF16)
    out_ref[...] = jnp.dot(fisher, pick, preferred_element_type=F32).astype(BF16)


def input_kernel(
    hidden_hbm, key_hbm, gain_hbm, inv_hbm, weight_0, weight_1, weight_3, weight_2,
    early_hbm, late_hbm, out_hbm,
    hidden_ref, key_ref, gain_ref, inv_ref, weight_ref, early_ref, late_ref, back_ref, out_ref,
    in_sems, out_sems,
):
    key_copy = start(key_hbm, key_ref, in_sems.at[0])
    core = my_core()
    z_here = lax.rem(lax.axis_index("fsdp"), NZL)
    groups = (
        (weight_0, 0),
        (weight_1, 1),
        (weight_3, 7),
        (weight_2, jnp.where((z_here & 1) == 0, 2, 6)),
    )
    copies, blocks = [], []
    for i, (source, away) in enumerate(groups):
        size = source.shape[0]
        target = weight_ref.at[pl.ds(2 * len(blocks), size)]
        copies.append(start(source, target, in_sems.at[1 + i]))
        blocks += [(i, away, row) for row in range(0, size, 2)]
    second = [
        start(early_hbm, early_ref, in_sems.at[5]),
        start(late_hbm, late_ref, in_sems.at[6]),
        start(gain_hbm, gain_ref, in_sems.at[7]),
        start(inv_hbm, inv_ref, in_sems.at[8]),
        start(hidden_hbm, hidden_ref, in_sems.at[9]),
    ]

    def put(back, origin, away, row):
        zl = (z_here + origin + away) & (NZL - 1)
        for half in range(2):
            cols = pl.ds(pl.multiple_of(((row + half) * NZL + zl) * 128, 128), 128)
            back_ref[:, cols] = back[:, half * 128 : (half + 1) * 128]

    key_copy.wait()
    keys = key_ref[...]
    waited = 0
    for block, (group, away, row) in enumerate(blocks):
        if waited == group:
            copies[group].wait()
            waited += 1
        weight = weight_ref[2 * block : 2 * block + 2].reshape(256, K)
        back = lax.dot_general(keys, weight, (((1,), (1,)), ((), ())), preferred_element_type=F32)
        put(back, 4 * core, away, row)
    second[0].wait()
    second[1].wait()
    early = early_ref.shape[0]
    for block, (_, away, row) in enumerate(blocks):
        back = early_ref[block] if block < early else late_ref[block - early]
        put(back.astype(F32), 4 * (1 - core), away, row)
    for copy in second[2:]:
        copy.wait()

    step, parts, width = 16, 4, 512

    def rows_of(i, carry):
        rows = pl.ds(pl.multiple_of(i * step, step), step)
        inv = inv_ref[rows, 0:1]
        total = jnp.zeros((step, width), F32)
        for t in range(0, D, width):
            cols = slice(t, t + width)
            du = back_ref[rows, cols] * gain_ref[:, cols]
            total += du * hidden_ref[rows, cols].astype(F32)
        mean = inv * jnp.sum(total, axis=-1, keepdims=True) * (1.0 / D)
        factor = inv * inv * mean
        for t in range(0, D, width):
            cols = slice(t, t + width)
            du = back_ref[rows, cols] * gain_ref[:, cols]
            out = du * inv - hidden_ref[rows, cols].astype(F32) * factor
            out_ref[rows, cols] = out.astype(BF16)
        return carry

    rows_each = SEQ // parts
    copies = []
    for i in range(parts):
        lax.fori_loop(i * rows_each // step, (i + 1) * rows_each // step, rows_of, 0, unroll=4)
        rows = pl.ds(i * rows_each, rows_each)
        copies.append(start(out_ref.at[rows], out_hbm.at[rows], out_sems.at[i]))
    for copy in copies:
        copy.wait()


def body(hidden_in, key_grad, key_weight, norm_gain, head_order):
    gain = norm_gain.reshape(1, D)
    vmem, hbm, any_ = pltpu.VMEM, pltpu.HBM, pl.ANY
    dma = pltpu.SemaphoreType.DMA
    blocks = NX * NZH
    barrier = lax.optimization_barrier

    with jax.named_scope("weight_z4"):
        origin = lax.ppermute(key_weight, AXES, origins())
    with jax.named_scope("norm"):
        own, send, inv = call(
            norm_kernel,
            (shape((blocks, SEQ, COLS)), shape((blocks + 2, SEQ, COLS)), shape((SEQ, 128), F32)),
            (hidden_in, key_grad, gain),
            (any_,) * 3,
            (hbm, hbm, hbm),
            [
                pltpu.VMEM((SEQ, D), BF16),
                pltpu.VMEM((SEQ, K), BF16),
                pltpu.VMEM((1, D), F32),
                pltpu.VMEM((blocks, SEQ, COLS), BF16),
                pltpu.VMEM((blocks, SEQ, COLS), BF16),
                pltpu.VMEM((SEQ, 128), F32),
                dma((NORM_PARTS + 2,)),
                dma((2 * NORM_PARTS + 3,)),
            ],
            mib=None,
        )
        origin, send = barrier((origin, send))
        other = lax.ppermute(send, AXES, CORE_SWAP)
    with jax.named_scope("weight_y"):
        near = lax.all_gather(origin, AXES, axis=0, tiled=True, axis_index_groups=Y_RINGS)
        near, other = barrier((near.reshape(NY, 128, K), other))
    with jax.named_scope("squares"):
        chunks = call(
            square_kernel,
            shape((NX * NY, 256, COLS)),
            (own, other, key_grad),
            (any_,) * 3,
            hbm,
            [
                pltpu.VMEM((blocks, SEQ, COLS), BF16),
                pltpu.VMEM((blocks + 2, SEQ, COLS), BF16),
                pltpu.VMEM((SEQ, K), BF16),
                pltpu.VMEM((blocks, NY, 128, COLS), BF16),
                dma((10,)),
                dma((blocks, NY)),
            ],
            mib=60,
        )
    with jax.named_scope("plane"):
        chunks = exchange(chunks, PLANES)
    with jax.named_scope("weight_z1"):
        up = lax.ppermute(near, AXES, from_z(1))
        down = lax.ppermute(near, AXES, from_z(-1))
        *now, up, down = barrier((near, up, down))
        far = lax.ppermute(now[0], AXES, two_away())
    with jax.named_scope("back_early"):
        early = lax.ppermute(partner(other, near, up, down), AXES, CORE_SWAP)
    with jax.named_scope("split"):
        parts = call(split_kernel, shape((NZH * NZL, 16, COLS)), (chunks,), (vmem,), vmem)
    with jax.named_scope("ring_z"):
        parts = exchange(parts, Z_RINGS)
    with jax.named_scope("back_late"):
        late = lax.ppermute(partner(other, far), AXES, CORE_SWAP)
    with jax.named_scope("input_grad"):
        weights = (near, up, down, far)
        input_grad = call(
            input_kernel,
            shape((SEQ, D)),
            (hidden_in, key_grad, gain, inv, *weights, early, late),
            (any_,) * 10,
            hbm,
            [
                pltpu.VMEM((SEQ, D), BF16),
                pltpu.VMEM((SEQ, K), BF16),
                pltpu.VMEM((1, D), F32),
                pltpu.VMEM((SEQ, 128), F32),
                pltpu.VMEM((16, 128, K), BF16),
                pltpu.VMEM((6, SEQ, COLS), BF16),
                pltpu.VMEM((2, SEQ, COLS), BF16),
                pltpu.VMEM((SEQ, D), F32),
                pltpu.VMEM((SEQ, D), BF16),
                dma((10,)),
                dma((4,)),
            ],
            mib=60,
        )
        parts, input_grad = barrier((parts, input_grad))
    with jax.named_scope("serve"):
        served = call(
            serve_kernel,
            shape((8, K)),
            (head_order.reshape(1, K), parts),
            (any_, vmem),
            vmem,
            [pltpu.VMEM((1, K), jnp.int32), dma],
        )
    return served, input_grad


def solution(mesh):
    in_specs = (P(AXES, None), P(AXES, None), P("fsdp", None), P(), P())
    out_specs = (P(AXES, None), P(AXES, None))
    return jax.shard_map(body, mesh=mesh, in_specs=in_specs, out_specs=out_specs, check_vma=False)
```

```python
import jax
import jax.numpy as jnp
from jax import lax
from jax.experimental import pallas as pl
from jax.experimental.pallas import tpu as pltpu
from jax.sharding import PartitionSpec as P

AXES = ("dp", "fsdp")
NX, NZH, NC, NY, NZL = 4, 2, 2, 4, 8
D, K = 4096, 512
SEQ = 256
TOKENS = SEQ * NX * NZH * NC * NY * NZL
COLS = 256
NORM_PARTS = 4
BF16, F32 = jnp.bfloat16, jnp.float32


def device(x, zh, c, y, zl):
    return (((x * NZH + zh) * NC + c) * NY + y) * NZL + zl


def places():
    return [
        (x, zh, c, y, zl)
        for x in range(NX)
        for zh in range(NZH)
        for c in range(NC)
        for y in range(NY)
        for zl in range(NZL)
    ]


def from_z(distance):
    pairs = []
    for x, zh, c, y, zl in places():
        z = (zh * NZL + zl + distance) % (NZH * NZL)
        pairs.append((device(x, z // NZL, c, y, z % NZL), device(x, zh, c, y, zl)))
    return pairs


def two_away():
    pairs = []
    for x, zh, c, y, zl in places():
        z = (zh * NZL + zl + (2 if zl % 2 == 0 else -2)) % (NZH * NZL)
        pairs.append((device(x, z // NZL, c, y, z % NZL), device(x, zh, c, y, zl)))
    return pairs


def from_y(ahead):
    return [
        (device(x, zh, c, (y + ahead) % NY, zl), device(x, zh, c, y, zl))
        for x, zh, c, y, zl in places()
    ]


def origins():
    pairs = []
    for x, zh, c, y, zl in places():
        z = (zh * NZL + zl + c * (4 if zl % 2 == 0 else -4)) % (NZH * NZL)
        pairs.append((device(x, z // NZL, c, y, z % NZL), device(x, zh, c, y, zl)))
    return pairs


PLANES = [
    [device(x, zh, c, y, zl) for x in range(NX) for y in range(NY)]
    for zh in range(NZH)
    for c in range(NC)
    for zl in range(NZL)
]
Z_RINGS = [
    [device(x, zh, c, y, zl) for zh in range(NZH) for zl in range(NZL)]
    for x in range(NX)
    for c in range(NC)
    for y in range(NY)
]
CORE_SWAP = [(device(x, zh, c, y, zl), device(x, zh, 1 - c, y, zl)) for x, zh, c, y, zl in places()]


def exchange(value, groups):
    return lax.all_to_all(
        value, AXES, split_axis=0, concat_axis=0, axis_index_groups=groups, tiled=True
    )


def call(kernel, outs, ins, in_spaces, out_spaces, scratch=(), mib=24, us=0.05):
    return pl.pallas_call(
        kernel,
        out_shape=outs,
        in_specs=[pl.BlockSpec(memory_space=space) for space in in_spaces],
        out_specs=jax.tree.map(lambda space: pl.BlockSpec(memory_space=space), out_spaces),
        scratch_shapes=list(scratch),
        compiler_params=pltpu.CompilerParams(vmem_limit_bytes=mib and mib * 2**20),
        cost_estimate=pl.CostEstimate(
            flops=0, bytes_accessed=int(us * 3.0e6), transcendentals=0
        ),
    )(*ins)


def my_core():
    return lax.rem(lax.axis_index("dp"), NC)


def shape(dims, dtype=BF16):
    return jax.ShapeDtypeStruct(dims, dtype)


def start(source, target, sem):
    copy = pltpu.make_async_copy(source, target, sem)
    copy.start()
    return copy


def norm_kernel(
    hidden_hbm, key_hbm, gain_hbm, own_hbm, send_hbm, inv_hbm,
    hidden_ref, key_ref, gain_ref, own_ref, send_ref, inv_ref, in_sems, out_sems,
):
    core = my_core()
    step, parts, blocks = 16, NORM_PARTS, NX * NZH
    rows_each = SEQ // parts
    pieces = [pl.ds(i * rows_each, rows_each) for i in range(parts)]
    gain_copy = start(gain_hbm, gain_ref, in_sems.at[parts])
    copies = [
        start(hidden_hbm.at[rows], hidden_ref.at[rows], in_sems.at[i])
        for i, rows in enumerate(pieces)
    ]
    key_copy = start(key_hbm, key_ref, in_sems.at[parts + 1])

    def rows_of(i, carry):
        rows = pl.ds(pl.multiple_of(i * step, step), step)
        squares = jnp.zeros((step, 512), F32)
        for t in range(0, D, 512):
            values = hidden_ref[rows, t : t + 512].astype(F32)
            squares += values * values
        inv = lax.rsqrt(jnp.sum(squares, axis=-1, keepdims=True) * (1.0 / D) + 1e-06)
        inv_ref[rows, :] = jnp.broadcast_to(inv, (step, 128))
        for ref, part in ((own_ref, core), (send_ref, 1 - core)):
            for k in range(blocks):
                cols = pl.ds(pl.multiple_of((2 * k + part) * COLS, COLS), COLS)
                unit = hidden_ref[rows, cols].astype(F32) * inv
                ref[k, rows, :] = (unit * gain_ref[:, cols]).astype(BF16)
        return carry

    gain_copy.wait()
    out_copies = []
    for i, rows in enumerate(pieces):
        copies[i].wait()
        lax.fori_loop(i * rows_each // step, (i + 1) * rows_each // step, rows_of, 0, unroll=4)
        out_copies += [
            start(send_ref.at[:, rows], send_hbm.at[pl.ds(0, blocks), rows], out_sems.at[2 * i]),
            start(own_ref.at[:, rows], own_hbm.at[:, rows], out_sems.at[2 * i + 1]),
        ]
    key_copy.wait()
    for half in range(2):
        source = key_ref.at[:, pl.ds(half * COLS, COLS)]
        out_copies.append(start(source, send_hbm.at[blocks + half], out_sems.at[2 * parts + half]))
    out_copies.append(start(inv_ref, inv_hbm, out_sems.at[2 * parts + 2]))
    for copy in out_copies:
        copy.wait()


def column_kernel(*refs):
    *blocks, out_hbm, sems = refs
    copies = [start(block, out_hbm.at[j], sems.at[j]) for j, block in enumerate(blocks)]
    for copy in copies:
        copy.wait()


def partner_kernel(key_hbm, *refs):
    *sources, out_hbm, key_ref, weight_ref, out_ref, in_sems, out_sems = refs
    key_copy = start(key_hbm.at[pl.ds(NX * NZH, 2)], key_ref, in_sems.at[0])
    copies, place = [], 0
    for i, source in enumerate(sources):
        size = source.shape[0]
        target = weight_ref.at[pl.ds(place, size)]
        copies.append((start(source, target, in_sems.at[1 + i]), place // 2, size // 2))
        place += size
    key_copy.wait()
    keys = jnp.concatenate([key_ref[0], key_ref[1]], axis=1)
    out_copies = []
    for copy, first, size in copies:
        copy.wait()
        for block in range(first, first + size):
            weight = weight_ref[2 * block : 2 * block + 2].reshape(256, K)
            back = lax.dot_general(
                keys, weight, (((1,), (1,)), ((), ())), preferred_element_type=F32
            )
            out_ref[block] = back.astype(BF16)
            out_copies.append(start(out_ref.at[block], out_hbm.at[block], out_sems.at[block]))
    for copy in out_copies:
        copy.wait()


def partner(other, *sources):
    size = sum(source.shape[0] for source in sources)
    dma = pltpu.SemaphoreType.DMA
    return call(
        partner_kernel,
        shape((size // 2, SEQ, COLS)),
        (other, *sources),
        (pl.ANY,) * (1 + len(sources)),
        pltpu.HBM,
        [
            pltpu.VMEM((2, SEQ, COLS), BF16),
            pltpu.VMEM((size, 128, K), BF16),
            pltpu.VMEM((size // 2, SEQ, COLS), BF16),
            dma((1 + len(sources),)),
            dma((size // 2,)),
        ],
        mib=52,
    )


def square_kernel(
    own_hbm, other_hbm, key_hbm, out_hbm, own_ref, other_ref, key_ref, out_ref, in_sems, out_sems
):
    blocks = NX * NZH
    over_tokens = (((0,), (0,)), ((), ()))
    keys = [
        start(key_hbm, key_ref, in_sems.at[0]),
        start(other_hbm.at[pl.ds(blocks, 2)], other_ref.at[pl.ds(blocks, 2)], in_sems.at[1]),
    ]
    copies = []
    for part in range(4):
        some = pl.ds(2 * part, 2)
        copies += [
            start(own_hbm.at[some], own_ref.at[some], in_sems.at[2 + 2 * part]),
            start(other_hbm.at[some], other_ref.at[some], in_sems.at[3 + 2 * part]),
        ]
    for copy in keys:
        copy.wait()
    key_other = jnp.concatenate([other_ref[blocks], other_ref[blocks + 1]], axis=1)

    out_copies = []
    for k in range(blocks):
        x, zh = k // NZH, k % NZH
        if zh == 0:
            copies[2 * x].wait()
            copies[2 * x + 1].wait()
        g0 = lax.dot_general(own_ref[k], key_ref[...], over_tokens, preferred_element_type=F32)
        g1 = lax.dot_general(other_ref[k], key_other, over_tokens, preferred_element_type=F32)
        total = ((g0 * g0 + g1 * g1) * (1.0 / TOKENS)).astype(BF16)
        for y in range(NY):
            rows = slice(y * 64, (y + 1) * 64)
            out_ref[k, y, 0:64, :] = total[rows, 0:COLS]
            out_ref[k, y, 64:128, :] = total[rows, COLS:K]
            target = out_hbm.at[x * NY + y, pl.ds(zh * 128, 128)]
            out_copies.append(start(out_ref.at[k, y], target, out_sems.at[k, y]))
    for copy in out_copies:
        copy.wait()


def split_kernel(in_ref, out_ref):
    for zh in range(NZH):
        rows = slice(zh * 128, (zh + 1) * 128)
        total = in_ref[0, rows, :].astype(F32)
        for j in range(1, NX * NY):
            total += in_ref[j, rows, :].astype(F32)
        total = total.reshape(2, NZL, 8, COLS)
        for zl in range(NZL):
            both = jnp.concatenate([total[0, zl], total[1, zl]], axis=0)
            out_ref[zh * NZL + zl] = both.astype(BF16)


def serve_kernel(order_hbm, in_ref, out_ref, order_ref, sem):
    copy = start(order_hbm, order_ref, sem)
    total = in_ref[0].astype(F32)
    for z in range(1, NZH * NZL):
        total += in_ref[z].astype(F32)
    fisher = jnp.concatenate([total[0:8], total[8:16]], axis=1).astype(BF16)
    copy.wait()
    column = lax.broadcasted_iota(jnp.int32, (K, K), 0)
    pick = jnp.where(column == order_ref[...], 1.0, 0.0).astype(BF16)
    out_ref[...] = jnp.dot(fisher, pick, preferred_element_type=F32).astype(BF16)


def input_kernel(
    hidden_hbm, key_hbm, gain_hbm, inv_hbm, weight_0, weight_1, weight_3, weight_2,
    early_hbm, late_hbm, out_hbm,
    hidden_ref, key_ref, gain_ref, inv_ref, weight_ref, early_ref, late_ref, back_ref, out_ref,
    in_sems, out_sems,
):
    key_copy = start(key_hbm, key_ref, in_sems.at[0])
    core = my_core()
    z_here = lax.rem(lax.axis_index("fsdp"), NZL)
    y_here = lax.div(lax.axis_index("fsdp"), NZL)
    groups = (
        (weight_0, 0),
        (weight_1, 1),
        (weight_3, 7),
        (weight_2, jnp.where((z_here & 1) == 0, 2, 6)),
    )
    copies, blocks = [], []
    for i, (source, away) in enumerate(groups):
        size = source.shape[0]
        target = weight_ref.at[pl.ds(2 * len(blocks), size)]
        copies.append(start(source, target, in_sems.at[1 + i]))
        blocks += [(i, away, row) for row in range(0, size, 2)]
    second = [
        start(early_hbm, early_ref, in_sems.at[5]),
        start(late_hbm, late_ref, in_sems.at[6]),
        start(gain_hbm, gain_ref, in_sems.at[7]),
        start(inv_hbm, inv_ref, in_sems.at[8]),
        start(hidden_hbm, hidden_ref, in_sems.at[9]),
    ]

    def put(back, origin, away, row):
        zl = (z_here + origin + away) & (NZL - 1)
        for half in range(2):
            y = (y_here + row + half) & (NY - 1)
            cols = pl.ds(pl.multiple_of((y * NZL + zl) * 128, 128), 128)
            back_ref[:, cols] = back[:, half * 128 : (half + 1) * 128]

    key_copy.wait()
    keys = key_ref[...]
    waited = 0
    for block, (group, away, row) in enumerate(blocks):
        if waited == group:
            copies[group].wait()
            waited += 1
        weight = weight_ref[2 * block : 2 * block + 2].reshape(256, K)
        back = lax.dot_general(keys, weight, (((1,), (1,)), ((), ())), preferred_element_type=F32)
        put(back, 4 * core, away, row)
    second[0].wait()
    second[1].wait()
    early = early_ref.shape[0]
    for block, (_, away, row) in enumerate(blocks):
        back = early_ref[block] if block < early else late_ref[block - early]
        put(back.astype(F32), 4 * (1 - core), away, row)
    for copy in second[2:]:
        copy.wait()

    step, parts, width = 16, 4, 512

    def rows_of(i, carry):
        rows = pl.ds(pl.multiple_of(i * step, step), step)
        inv = inv_ref[rows, 0:1]
        total = jnp.zeros((step, width), F32)
        for t in range(0, D, width):
            cols = slice(t, t + width)
            du = back_ref[rows, cols] * gain_ref[:, cols]
            total += du * hidden_ref[rows, cols].astype(F32)
        mean = inv * jnp.sum(total, axis=-1, keepdims=True) * (1.0 / D)
        factor = inv * inv * mean
        for t in range(0, D, width):
            cols = slice(t, t + width)
            du = back_ref[rows, cols] * gain_ref[:, cols]
            out = du * inv - hidden_ref[rows, cols].astype(F32) * factor
            out_ref[rows, cols] = out.astype(BF16)
        return carry

    rows_each = SEQ // parts
    copies = []
    for i in range(parts):
        lax.fori_loop(i * rows_each // step, (i + 1) * rows_each // step, rows_of, 0, unroll=4)
        rows = pl.ds(i * rows_each, rows_each)
        copies.append(start(out_ref.at[rows], out_hbm.at[rows], out_sems.at[i]))
    for copy in copies:
        copy.wait()


def body(hidden_in, key_grad, key_weight, norm_gain, head_order):
    gain = norm_gain.reshape(1, D)
    vmem, hbm, any_ = pltpu.VMEM, pltpu.HBM, pl.ANY
    dma = pltpu.SemaphoreType.DMA
    blocks = NX * NZH
    barrier = lax.optimization_barrier

    with jax.named_scope("weight_z4"):
        origin = lax.ppermute(key_weight, AXES, origins())
    with jax.named_scope("norm"):
        own, send, inv = call(
            norm_kernel,
            (shape((blocks, SEQ, COLS)), shape((blocks + 2, SEQ, COLS)), shape((SEQ, 128), F32)),
            (hidden_in, key_grad, gain),
            (any_,) * 3,
            (hbm, hbm, hbm),
            [
                pltpu.VMEM((SEQ, D), BF16),
                pltpu.VMEM((SEQ, K), BF16),
                pltpu.VMEM((1, D), F32),
                pltpu.VMEM((blocks, SEQ, COLS), BF16),
                pltpu.VMEM((blocks, SEQ, COLS), BF16),
                pltpu.VMEM((SEQ, 128), F32),
                dma((NORM_PARTS + 2,)),
                dma((2 * NORM_PARTS + 3,)),
            ],
            mib=None,
        )
        origin, send = barrier((origin, send))
        other = lax.ppermute(send, AXES, CORE_SWAP)
    with jax.named_scope("squares"):
        chunks = call(
            square_kernel,
            shape((NX * NY, 256, COLS)),
            (own, other, key_grad),
            (any_,) * 3,
            hbm,
            [
                pltpu.VMEM((blocks, SEQ, COLS), BF16),
                pltpu.VMEM((blocks + 2, SEQ, COLS), BF16),
                pltpu.VMEM((SEQ, K), BF16),
                pltpu.VMEM((blocks, NY, 128, COLS), BF16),
                dma((10,)),
                dma((blocks, NY)),
            ],
            mib=51,
        )
    with jax.named_scope("weight_y"):
        column = [origin] + [lax.ppermute(origin, AXES, from_y(ahead)) for ahead in (1, 2, 3)]
        chunks, *column = barrier((chunks, *column))
    with jax.named_scope("plane"):
        chunks = exchange(chunks, PLANES)
    with jax.named_scope("weight_y"):
        near = call(
            column_kernel, shape((NY, 128, K)), column, (any_,) * NY, hbm, [dma((NY,))], mib=52
        )
    with jax.named_scope("weight_z1"):
        up = lax.ppermute(near, AXES, from_z(1))
        down = lax.ppermute(near, AXES, from_z(-1))
        *now, up, down = barrier((near, up, down))
        far = lax.ppermute(now[0], AXES, two_away())
    with jax.named_scope("back_early"):
        early = lax.ppermute(partner(other, near, up, down), AXES, CORE_SWAP)
    with jax.named_scope("split"):
        parts = call(split_kernel, shape((NZH * NZL, 16, COLS)), (chunks,), (vmem,), vmem)
    with jax.named_scope("ring_z"):
        parts = exchange(parts, Z_RINGS)
    with jax.named_scope("back_late"):
        late = lax.ppermute(partner(other, far), AXES, CORE_SWAP)
    with jax.named_scope("input_grad"):
        weights = (near, up, down, far)
        input_grad = call(
            input_kernel,
            shape((SEQ, D)),
            (hidden_in, key_grad, gain, inv, *weights, early, late),
            (any_,) * 10,
            hbm,
            [
                pltpu.VMEM((SEQ, D), BF16),
                pltpu.VMEM((SEQ, K), BF16),
                pltpu.VMEM((1, D), F32),
                pltpu.VMEM((SEQ, 128), F32),
                pltpu.VMEM((16, 128, K), BF16),
                pltpu.VMEM((6, SEQ, COLS), BF16),
                pltpu.VMEM((2, SEQ, COLS), BF16),
                pltpu.VMEM((SEQ, D), F32),
                pltpu.VMEM((SEQ, D), BF16),
                dma((10,)),
                dma((4,)),
            ],
            mib=60,
        )
        parts, input_grad = barrier((parts, input_grad))
    with jax.named_scope("serve"):
        served = call(
            serve_kernel,
            shape((8, K)),
            (head_order.reshape(1, K), parts),
            (any_, vmem),
            vmem,
            [pltpu.VMEM((1, K), jnp.int32), dma],
        )
    return served, input_grad


def solution(mesh):
    in_specs = (P(AXES, None), P(AXES, None), P("fsdp", None), P(), P())
    out_specs = (P(AXES, None), P(AXES, None))
    return jax.shard_map(body, mesh=mesh, in_specs=in_specs, out_specs=out_specs, check_vma=False)
```

```python
import jax
import jax.numpy as jnp
from jax import lax
from jax.experimental import pallas as pl
from jax.experimental.pallas import tpu as pltpu
from jax.sharding import PartitionSpec as P

AXES = ("dp", "fsdp")
NX, NZH, NC, NY, NZL = 4, 2, 2, 4, 8
D, K = 4096, 512
SEQ = 256
TOKENS = SEQ * NX * NZH * NC * NY * NZL
COLS = 256
NORM_PARTS = 4
BF16, F32 = jnp.bfloat16, jnp.float32


def device(x, zh, c, y, zl):
    return (((x * NZH + zh) * NC + c) * NY + y) * NZL + zl


def places():
    return [
        (x, zh, c, y, zl)
        for x in range(NX)
        for zh in range(NZH)
        for c in range(NC)
        for y in range(NY)
        for zl in range(NZL)
    ]


def from_z(distance):
    pairs = []
    for x, zh, c, y, zl in places():
        z = (zh * NZL + zl + distance) % (NZH * NZL)
        pairs.append((device(x, z // NZL, c, y, z % NZL), device(x, zh, c, y, zl)))
    return pairs


def two_away():
    pairs = []
    for x, zh, c, y, zl in places():
        z = (zh * NZL + zl + (2 if zl % 2 == 0 else -2)) % (NZH * NZL)
        pairs.append((device(x, z // NZL, c, y, z % NZL), device(x, zh, c, y, zl)))
    return pairs


def from_y(ahead):
    return [
        (device(x, zh, c, (y + ahead) % NY, zl), device(x, zh, c, y, zl))
        for x, zh, c, y, zl in places()
    ]


def origins():
    pairs = []
    for x, zh, c, y, zl in places():
        z = (zh * NZL + zl + c * (4 if zl % 2 == 0 else -4)) % (NZH * NZL)
        pairs.append((device(x, z // NZL, c, y, z % NZL), device(x, zh, c, y, zl)))
    return pairs


PLANES = [
    [device(x, zh, c, y, zl) for x in range(NX) for y in range(NY)]
    for zh in range(NZH)
    for c in range(NC)
    for zl in range(NZL)
]
Z_RINGS = [
    [device(x, zh, c, y, zl) for zh in range(NZH) for zl in range(NZL)]
    for x in range(NX)
    for c in range(NC)
    for y in range(NY)
]
CORE_SWAP = [(device(x, zh, c, y, zl), device(x, zh, 1 - c, y, zl)) for x, zh, c, y, zl in places()]


def exchange(value, groups):
    return lax.all_to_all(
        value, AXES, split_axis=0, concat_axis=0, axis_index_groups=groups, tiled=True
    )


def call(kernel, outs, ins, in_spaces, out_spaces, scratch=(), mib=24, us=0.05):
    return pl.pallas_call(
        kernel,
        out_shape=outs,
        in_specs=[pl.BlockSpec(memory_space=space) for space in in_spaces],
        out_specs=jax.tree.map(lambda space: pl.BlockSpec(memory_space=space), out_spaces),
        scratch_shapes=list(scratch),
        compiler_params=pltpu.CompilerParams(vmem_limit_bytes=mib and mib * 2**20),
        cost_estimate=pl.CostEstimate(
            flops=0, bytes_accessed=int(us * 3.0e6), transcendentals=0
        ),
    )(*ins)


def my_core():
    return lax.rem(lax.axis_index("dp"), NC)


def shape(dims, dtype=BF16):
    return jax.ShapeDtypeStruct(dims, dtype)


def start(source, target, sem):
    copy = pltpu.make_async_copy(source, target, sem)
    copy.start()
    return copy


OVER_TOKENS = (((0,), (0,)), ((), ()))


def put_terms(k, term, ref, hbm, sems):
    x, zh = k // NZH, k % NZH
    copies = []
    for y in range(NY):
        rows = slice(y * 64, (y + 1) * 64)
        ref[k, y, 0:64, :] = term[rows, 0:COLS]
        ref[k, y, 64:128, :] = term[rows, COLS:K]
        target = hbm.at[x * NY + y, pl.ds(zh * 128, 128)]
        copies.append(start(ref.at[k, y], target, sems.at[k, y]))
    return copies


def norm_kernel(
    hidden_hbm, key_hbm, gain_hbm, term_hbm, send_hbm, inv_hbm,
    hidden_ref, key_ref, gain_ref, own_ref, send_ref, inv_ref, term_ref, in_sems, out_sems,
    term_sems,
):
    core = my_core()
    step, parts, blocks = 16, NORM_PARTS, NX * NZH
    rows_each = SEQ // parts
    pieces = [pl.ds(i * rows_each, rows_each) for i in range(parts)]
    gain_copy = start(gain_hbm, gain_ref, in_sems.at[parts])
    copies = [
        start(hidden_hbm.at[rows], hidden_ref.at[rows], in_sems.at[i])
        for i, rows in enumerate(pieces)
    ]
    key_copy = start(key_hbm, key_ref, in_sems.at[parts + 1])

    def rows_of(i, carry):
        rows = pl.ds(pl.multiple_of(i * step, step), step)
        squares = jnp.zeros((step, 512), F32)
        for t in range(0, D, 512):
            values = hidden_ref[rows, t : t + 512].astype(F32)
            squares += values * values
        inv = lax.rsqrt(jnp.sum(squares, axis=-1, keepdims=True) * (1.0 / D) + 1e-06)
        inv_ref[rows, :] = jnp.broadcast_to(inv, (step, 128))
        for ref, part in ((own_ref, core), (send_ref, 1 - core)):
            for k in range(blocks):
                cols = pl.ds(pl.multiple_of((2 * k + part) * COLS, COLS), COLS)
                unit = hidden_ref[rows, cols].astype(F32) * inv
                ref[k, rows, :] = (unit * gain_ref[:, cols]).astype(BF16)
        return carry

    gain_copy.wait()
    out_copies = []
    for i, rows in enumerate(pieces):
        copies[i].wait()
        lax.fori_loop(i * rows_each // step, (i + 1) * rows_each // step, rows_of, 0, unroll=4)
        target = send_hbm.at[pl.ds(0, blocks), rows]
        out_copies.append(start(send_ref.at[:, rows], target, out_sems.at[i]))
    key_copy.wait()
    for half in range(2):
        source = key_ref.at[:, pl.ds(half * COLS, COLS)]
        out_copies.append(start(source, send_hbm.at[blocks + half], out_sems.at[parts + half]))
    out_copies.append(start(inv_ref, inv_hbm, out_sems.at[parts + 2]))
    for k in range(blocks):
        grad = lax.dot_general(own_ref[k], key_ref[...], OVER_TOKENS, preferred_element_type=F32)
        term = (grad * grad * (1.0 / TOKENS)).astype(BF16)
        out_copies += put_terms(k, term, term_ref, term_hbm, term_sems)
    for copy in out_copies:
        copy.wait()


def column_kernel(*refs):
    *blocks, out_hbm, sems = refs
    copies = [start(block, out_hbm.at[j], sems.at[j]) for j, block in enumerate(blocks)]
    for copy in copies:
        copy.wait()


def partner_kernel(key_hbm, *refs):
    *sources, out_hbm, key_ref, weight_ref, out_ref, in_sems, out_sems = refs
    key_copy = start(key_hbm.at[pl.ds(NX * NZH, 2)], key_ref, in_sems.at[0])
    copies, place = [], 0
    for i, source in enumerate(sources):
        size = source.shape[0]
        target = weight_ref.at[pl.ds(place, size)]
        copies.append((start(source, target, in_sems.at[1 + i]), place // 2, size // 2))
        place += size
    key_copy.wait()
    keys = jnp.concatenate([key_ref[0], key_ref[1]], axis=1)
    out_copies = []
    for copy, first, size in copies:
        copy.wait()
        for block in range(first, first + size):
            weight = weight_ref[2 * block : 2 * block + 2].reshape(256, K)
            back = lax.dot_general(
                keys, weight, (((1,), (1,)), ((), ())), preferred_element_type=F32
            )
            out_ref[block] = back.astype(BF16)
            out_copies.append(start(out_ref.at[block], out_hbm.at[block], out_sems.at[block]))
    for copy in out_copies:
        copy.wait()


def partner(other, *sources):
    size = sum(source.shape[0] for source in sources)
    dma = pltpu.SemaphoreType.DMA
    return call(
        partner_kernel,
        shape((size // 2, SEQ, COLS)),
        (other, *sources),
        (pl.ANY,) * (1 + len(sources)),
        pltpu.HBM,
        [
            pltpu.VMEM((2, SEQ, COLS), BF16),
            pltpu.VMEM((size, 128, K), BF16),
            pltpu.VMEM((size // 2, SEQ, COLS), BF16),
            dma((1 + len(sources),)),
            dma((size // 2,)),
        ],
        mib=52,
    )


def square_kernel(
    own_hbm, other_hbm, out_hbm, own_ref, other_ref, out_ref, in_sems, out_sems
):
    blocks = NX * NZH
    keys = start(other_hbm.at[pl.ds(blocks, 2)], other_ref.at[pl.ds(blocks, 2)], in_sems.at[0])
    copies = []
    for x in range(NX):
        some, chunks = pl.ds(NZH * x, NZH), pl.ds(NY * x, NY)
        copies += [
            start(other_hbm.at[some], other_ref.at[some], in_sems.at[1 + 2 * x]),
            start(own_hbm.at[chunks], own_ref.at[chunks], in_sems.at[2 + 2 * x]),
        ]
    keys.wait()
    key_other = jnp.concatenate([other_ref[blocks], other_ref[blocks + 1]], axis=1)
    out_copies = []
    for k in range(blocks):
        x, zh = k // NZH, k % NZH
        if zh == 0:
            copies[2 * x].wait()
        grad = lax.dot_general(other_ref[k], key_other, OVER_TOKENS, preferred_element_type=F32)
        if zh == 0:
            copies[2 * x + 1].wait()
        own = [own_ref[x * NY + y, zh * 128 : (zh + 1) * 128, :] for y in range(NY)]
        own = jnp.concatenate(
            [jnp.concatenate([part[0:64], part[64:128]], axis=1) for part in own], axis=0
        )
        term = (grad * grad * (1.0 / TOKENS) + own.astype(F32)).astype(BF16)
        out_copies += put_terms(k, term, out_ref, out_hbm, out_sems)
    for copy in out_copies:
        copy.wait()


def split_kernel(in_ref, out_ref):
    for zh in range(NZH):
        rows = slice(zh * 128, (zh + 1) * 128)
        total = in_ref[0, rows, :].astype(F32)
        for j in range(1, NX * NY):
            total += in_ref[j, rows, :].astype(F32)
        total = total.reshape(2, NZL, 8, COLS)
        for zl in range(NZL):
            both = jnp.concatenate([total[0, zl], total[1, zl]], axis=0)
            out_ref[zh * NZL + zl] = both.astype(BF16)


def serve_kernel(order_hbm, in_ref, out_ref, order_ref, sem):
    copy = start(order_hbm, order_ref, sem)
    total = in_ref[0].astype(F32)
    for z in range(1, NZH * NZL):
        total += in_ref[z].astype(F32)
    fisher = jnp.concatenate([total[0:8], total[8:16]], axis=1).astype(BF16)
    copy.wait()
    column = lax.broadcasted_iota(jnp.int32, (K, K), 0)
    pick = jnp.where(column == order_ref[...], 1.0, 0.0).astype(BF16)
    out_ref[...] = jnp.dot(fisher, pick, preferred_element_type=F32).astype(BF16)


def input_kernel(
    hidden_hbm, key_hbm, gain_hbm, inv_hbm, weight_0, weight_1, weight_3, weight_2,
    early_hbm, late_hbm, out_hbm,
    hidden_ref, key_ref, gain_ref, inv_ref, weight_ref, early_ref, late_ref, back_ref, out_ref,
    in_sems, out_sems,
):
    key_copy = start(key_hbm, key_ref, in_sems.at[0])
    core = my_core()
    z_here = lax.rem(lax.axis_index("fsdp"), NZL)
    y_here = lax.div(lax.axis_index("fsdp"), NZL)
    groups = (
        (weight_0, 0),
        (weight_1, 1),
        (weight_3, 7),
        (weight_2, jnp.where((z_here & 1) == 0, 2, 6)),
    )
    copies, blocks = [], []
    for i, (source, away) in enumerate(groups):
        size = source.shape[0]
        target = weight_ref.at[pl.ds(2 * len(blocks), size)]
        copies.append(start(source, target, in_sems.at[1 + i]))
        blocks += [(i, away, row) for row in range(0, size, 2)]
    second = [
        start(early_hbm, early_ref, in_sems.at[5]),
        start(late_hbm, late_ref, in_sems.at[6]),
        start(gain_hbm, gain_ref, in_sems.at[7]),
        start(inv_hbm, inv_ref, in_sems.at[8]),
        start(hidden_hbm, hidden_ref, in_sems.at[9]),
    ]

    def put(back, origin, away, row):
        zl = (z_here + origin + away) & (NZL - 1)
        for half in range(2):
            y = (y_here + row + half) & (NY - 1)
            cols = pl.ds(pl.multiple_of((y * NZL + zl) * 128, 128), 128)
            back_ref[:, cols] = back[:, half * 128 : (half + 1) * 128]

    key_copy.wait()
    keys = key_ref[...]
    waited = 0
    for block, (group, away, row) in enumerate(blocks):
        if waited == group:
            copies[group].wait()
            waited += 1
        weight = weight_ref[2 * block : 2 * block + 2].reshape(256, K)
        back = lax.dot_general(keys, weight, (((1,), (1,)), ((), ())), preferred_element_type=F32)
        put(back, 4 * core, away, row)
    second[0].wait()
    second[1].wait()
    early = early_ref.shape[0]
    for block, (_, away, row) in enumerate(blocks):
        back = early_ref[block] if block < early else late_ref[block - early]
        put(back.astype(F32), 4 * (1 - core), away, row)
    for copy in second[2:]:
        copy.wait()

    step, parts, width = 16, 4, 512

    def rows_of(i, carry):
        rows = pl.ds(pl.multiple_of(i * step, step), step)
        inv = inv_ref[rows, 0:1]
        total = jnp.zeros((step, width), F32)
        for t in range(0, D, width):
            cols = slice(t, t + width)
            du = back_ref[rows, cols] * gain_ref[:, cols]
            total += du * hidden_ref[rows, cols].astype(F32)
        mean = inv * jnp.sum(total, axis=-1, keepdims=True) * (1.0 / D)
        factor = inv * inv * mean
        for t in range(0, D, width):
            cols = slice(t, t + width)
            du = back_ref[rows, cols] * gain_ref[:, cols]
            out = du * inv - hidden_ref[rows, cols].astype(F32) * factor
            out_ref[rows, cols] = out.astype(BF16)
        return carry

    rows_each = SEQ // parts
    copies = []
    for i in range(parts):
        lax.fori_loop(i * rows_each // step, (i + 1) * rows_each // step, rows_of, 0, unroll=4)
        rows = pl.ds(i * rows_each, rows_each)
        copies.append(start(out_ref.at[rows], out_hbm.at[rows], out_sems.at[i]))
    for copy in copies:
        copy.wait()


def body(hidden_in, key_grad, key_weight, norm_gain, head_order):
    gain = norm_gain.reshape(1, D)
    vmem, hbm, any_ = pltpu.VMEM, pltpu.HBM, pl.ANY
    dma = pltpu.SemaphoreType.DMA
    blocks = NX * NZH
    barrier = lax.optimization_barrier

    with jax.named_scope("weight_z4"):
        origin = lax.ppermute(key_weight, AXES, origins())
    with jax.named_scope("norm"):
        own, send, inv = call(
            norm_kernel,
            (
                shape((NX * NY, 256, COLS)),
                shape((blocks + 2, SEQ, COLS)),
                shape((SEQ, 128), F32),
            ),
            (hidden_in, key_grad, gain),
            (any_,) * 3,
            (hbm, hbm, hbm),
            [
                pltpu.VMEM((SEQ, D), BF16),
                pltpu.VMEM((SEQ, K), BF16),
                pltpu.VMEM((1, D), F32),
                pltpu.VMEM((blocks, SEQ, COLS), BF16),
                pltpu.VMEM((blocks, SEQ, COLS), BF16),
                pltpu.VMEM((SEQ, 128), F32),
                pltpu.VMEM((blocks, NY, 128, COLS), BF16),
                dma((NORM_PARTS + 2,)),
                dma((NORM_PARTS + 3,)),
                dma((blocks, NY)),
            ],
            mib=None,
        )
        origin, send = barrier((origin, send))
        other = lax.ppermute(send, AXES, CORE_SWAP)
    with jax.named_scope("squares"):
        chunks = call(
            square_kernel,
            shape((NX * NY, 256, COLS)),
            (own, other),
            (any_,) * 2,
            hbm,
            [
                pltpu.VMEM((NX * NY, 256, COLS), BF16),
                pltpu.VMEM((blocks + 2, SEQ, COLS), BF16),
                pltpu.VMEM((blocks, NY, 128, COLS), BF16),
                dma((9,)),
                dma((blocks, NY)),
            ],
            mib=51,
        )
    with jax.named_scope("weight_y"):
        column = [origin] + [lax.ppermute(origin, AXES, from_y(ahead)) for ahead in (1, 2, 3)]
        chunks, *column = barrier((chunks, *column))
    with jax.named_scope("plane"):
        chunks = exchange(chunks, PLANES)
    with jax.named_scope("weight_y"):
        near = call(
            column_kernel, shape((NY, 128, K)), column, (any_,) * NY, hbm, [dma((NY,))], mib=52
        )
    with jax.named_scope("weight_z1"):
        up = lax.ppermute(near, AXES, from_z(1))
        down = lax.ppermute(near, AXES, from_z(-1))
        *now, up, down = barrier((near, up, down))
        far = lax.ppermute(now[0], AXES, two_away())
    with jax.named_scope("back_early"):
        early = lax.ppermute(partner(other, near, up, down), AXES, CORE_SWAP)
    with jax.named_scope("split"):
        parts = call(split_kernel, shape((NZH * NZL, 16, COLS)), (chunks,), (vmem,), vmem)
    with jax.named_scope("ring_z"):
        parts = exchange(parts, Z_RINGS)
    with jax.named_scope("back_late"):
        late = lax.ppermute(partner(other, far), AXES, CORE_SWAP)
    with jax.named_scope("input_grad"):
        weights = (near, up, down, far)
        input_grad = call(
            input_kernel,
            shape((SEQ, D)),
            (hidden_in, key_grad, gain, inv, *weights, early, late),
            (any_,) * 10,
            hbm,
            [
                pltpu.VMEM((SEQ, D), BF16),
                pltpu.VMEM((SEQ, K), BF16),
                pltpu.VMEM((1, D), F32),
                pltpu.VMEM((SEQ, 128), F32),
                pltpu.VMEM((16, 128, K), BF16),
                pltpu.VMEM((6, SEQ, COLS), BF16),
                pltpu.VMEM((2, SEQ, COLS), BF16),
                pltpu.VMEM((SEQ, D), F32),
                pltpu.VMEM((SEQ, D), BF16),
                dma((10,)),
                dma((4,)),
            ],
            mib=60,
        )
        parts, input_grad = barrier((parts, input_grad))
    with jax.named_scope("serve"):
        served = call(
            serve_kernel,
            shape((8, K)),
            (head_order.reshape(1, K), parts),
            (any_, vmem),
            vmem,
            [pltpu.VMEM((1, K), jnp.int32), dma],
        )
    return served, input_grad


def solution(mesh):
    in_specs = (P(AXES, None), P(AXES, None), P("fsdp", None), P(), P())
    out_specs = (P(AXES, None), P(AXES, None))
    return jax.shard_map(body, mesh=mesh, in_specs=in_specs, out_specs=out_specs, check_vma=False)
```

```python
import jax
import jax.numpy as jnp
from jax import lax
from jax.experimental import pallas as pl
from jax.experimental.pallas import tpu as pltpu
from jax.sharding import PartitionSpec as P

AXES = ("dp", "fsdp")
NX, NZH, NC, NY, NZL = 4, 2, 2, 4, 8
D, K = 4096, 512
SEQ = 256
TOKENS = SEQ * NX * NZH * NC * NY * NZL
COLS = 256
NORM_PARTS = 4
BF16, F32 = jnp.bfloat16, jnp.float32


def device(x, zh, c, y, zl):
    return (((x * NZH + zh) * NC + c) * NY + y) * NZL + zl


def places():
    return [
        (x, zh, c, y, zl)
        for x in range(NX)
        for zh in range(NZH)
        for c in range(NC)
        for y in range(NY)
        for zl in range(NZL)
    ]


def from_z(distance):
    pairs = []
    for x, zh, c, y, zl in places():
        z = (zh * NZL + zl + distance) % (NZH * NZL)
        pairs.append((device(x, z // NZL, c, y, z % NZL), device(x, zh, c, y, zl)))
    return pairs


def two_away():
    pairs = []
    for x, zh, c, y, zl in places():
        z = (zh * NZL + zl + (2 if zl % 2 == 0 else -2)) % (NZH * NZL)
        pairs.append((device(x, z // NZL, c, y, z % NZL), device(x, zh, c, y, zl)))
    return pairs


def from_y(ahead):
    return [
        (device(x, zh, c, (y + ahead) % NY, zl), device(x, zh, c, y, zl))
        for x, zh, c, y, zl in places()
    ]


def origins():
    pairs = []
    for x, zh, c, y, zl in places():
        z = (zh * NZL + zl + c * (4 if zl % 2 == 0 else -4)) % (NZH * NZL)
        pairs.append((device(x, z // NZL, c, y, z % NZL), device(x, zh, c, y, zl)))
    return pairs


PLANES = [
    [device(x, zh, c, y, zl) for x in range(NX) for y in range(NY)]
    for zh in range(NZH)
    for c in range(NC)
    for zl in range(NZL)
]
Z_RINGS = [
    [device(x, zh, c, y, zl) for zh in range(NZH) for zl in range(NZL)]
    for x in range(NX)
    for c in range(NC)
    for y in range(NY)
]
CORE_SWAP = [(device(x, zh, c, y, zl), device(x, zh, 1 - c, y, zl)) for x, zh, c, y, zl in places()]


def exchange(value, groups):
    return lax.all_to_all(
        value, AXES, split_axis=0, concat_axis=0, axis_index_groups=groups, tiled=True
    )


def call(kernel, outs, ins, in_spaces, out_spaces, scratch=(), mib=24, us=0.05):
    return pl.pallas_call(
        kernel,
        out_shape=outs,
        in_specs=[pl.BlockSpec(memory_space=space) for space in in_spaces],
        out_specs=jax.tree.map(lambda space: pl.BlockSpec(memory_space=space), out_spaces),
        scratch_shapes=list(scratch),
        compiler_params=pltpu.CompilerParams(vmem_limit_bytes=mib and mib * 2**20),
        cost_estimate=pl.CostEstimate(
            flops=0, bytes_accessed=int(us * 3.0e6), transcendentals=0
        ),
    )(*ins)


def my_core():
    return lax.rem(lax.axis_index("dp"), NC)


def shape(dims, dtype=BF16):
    return jax.ShapeDtypeStruct(dims, dtype)


def start(source, target, sem):
    copy = pltpu.make_async_copy(source, target, sem)
    copy.start()
    return copy


OVER_TOKENS = (((0,), (0,)), ((), ()))


def put_terms(k, term, ref, hbm, sems):
    x, zh = k // NZH, k % NZH
    copies = []
    for y in range(NY):
        rows = slice(y * 64, (y + 1) * 64)
        ref[k, y, 0:64, :] = term[rows, 0:COLS]
        ref[k, y, 64:128, :] = term[rows, COLS:K]
        target = hbm.at[x * NY + y, pl.ds(zh * 128, 128)]
        copies.append(start(ref.at[k, y], target, sems.at[k, y]))
    return copies


def norm_kernel(
    hidden_hbm, key_hbm, gain_hbm, term_hbm, send_hbm, inv_hbm,
    hidden_ref, key_ref, gain_ref, own_ref, send_ref, inv_ref, term_ref, in_sems, out_sems,
    term_sems,
):
    core = my_core()
    step, parts, blocks = 16, NORM_PARTS, NX * NZH
    rows_each = SEQ // parts
    pieces = [pl.ds(i * rows_each, rows_each) for i in range(parts)]
    gain_copy = start(gain_hbm, gain_ref, in_sems.at[parts])
    copies = [
        start(hidden_hbm.at[rows], hidden_ref.at[rows], in_sems.at[i])
        for i, rows in enumerate(pieces)
    ]
    key_copy = start(key_hbm, key_ref, in_sems.at[parts + 1])

    def rows_of(i, carry):
        rows = pl.ds(pl.multiple_of(i * step, step), step)
        squares = jnp.zeros((step, 512), F32)
        for t in range(0, D, 512):
            values = hidden_ref[rows, t : t + 512].astype(F32)
            squares += values * values
        inv = lax.rsqrt(jnp.sum(squares, axis=-1, keepdims=True) * (1.0 / D) + 1e-06)
        inv_ref[rows, :] = jnp.broadcast_to(inv, (step, 128))
        for ref, part in ((own_ref, core), (send_ref, 1 - core)):
            for k in range(blocks):
                cols = pl.ds(pl.multiple_of((2 * k + part) * COLS, COLS), COLS)
                unit = hidden_ref[rows, cols].astype(F32) * inv
                ref[k, rows, :] = (unit * gain_ref[:, cols]).astype(BF16)
        return carry

    gain_copy.wait()
    out_copies = []
    for i, rows in enumerate(pieces):
        copies[i].wait()
        lax.fori_loop(i * rows_each // step, (i + 1) * rows_each // step, rows_of, 0, unroll=4)
        target = send_hbm.at[pl.ds(0, blocks), rows]
        out_copies.append(start(send_ref.at[:, rows], target, out_sems.at[i]))
    key_copy.wait()
    for half in range(2):
        source = key_ref.at[:, pl.ds(half * COLS, COLS)]
        out_copies.append(start(source, send_hbm.at[blocks + half], out_sems.at[parts + half]))
    out_copies.append(start(inv_ref, inv_hbm, out_sems.at[parts + 2]))
    for k in range(blocks):
        grad = lax.dot_general(own_ref[k], key_ref[...], OVER_TOKENS, preferred_element_type=F32)
        term = (grad * grad * (1.0 / TOKENS)).astype(BF16)
        out_copies += put_terms(k, term, term_ref, term_hbm, term_sems)
    for copy in out_copies:
        copy.wait()


def column_kernel(*refs):
    *blocks, out_hbm, sems = refs
    copies = [start(block, out_hbm.at[j], sems.at[j]) for j, block in enumerate(blocks)]
    for copy in copies:
        copy.wait()


def partner_kernel(key_hbm, *refs):
    *sources, out_hbm, key_ref, weight_ref, out_ref, in_sems, out_sems = refs
    key_copy = start(key_hbm.at[pl.ds(NX * NZH, 2)], key_ref, in_sems.at[0])
    copies, place = [], 0
    for i, source in enumerate(sources):
        size = source.shape[0]
        target = weight_ref.at[pl.ds(place, size)]
        copies.append((start(source, target, in_sems.at[1 + i]), place // 2, size // 2))
        place += size
    key_copy.wait()
    keys = jnp.concatenate([key_ref[0], key_ref[1]], axis=1)
    out_copies = []
    for copy, first, size in copies:
        copy.wait()
        for block in range(first, first + size):
            weight = weight_ref[2 * block : 2 * block + 2].reshape(256, K)
            back = lax.dot_general(
                keys, weight, (((1,), (1,)), ((), ())), preferred_element_type=F32
            )
            out_ref[block] = back.astype(BF16)
            out_copies.append(start(out_ref.at[block], out_hbm.at[block], out_sems.at[block]))
    for copy in out_copies:
        copy.wait()


def partner(other, *sources):
    size = sum(source.shape[0] for source in sources)
    dma = pltpu.SemaphoreType.DMA
    return call(
        partner_kernel,
        shape((size // 2, SEQ, COLS)),
        (other, *sources),
        (pl.ANY,) * (1 + len(sources)),
        pltpu.HBM,
        [
            pltpu.VMEM((2, SEQ, COLS), BF16),
            pltpu.VMEM((size, 128, K), BF16),
            pltpu.VMEM((size // 2, SEQ, COLS), BF16),
            dma((1 + len(sources),)),
            dma((size // 2,)),
        ],
        mib=52,
    )


def square_kernel(
    own_hbm, other_ref, out_hbm, own_ref, out_ref, in_sems, out_sems
):
    blocks = NX * NZH
    copies = []
    for x in range(NX):
        chunks = pl.ds(NY * x, NY)
        copies.append(start(own_hbm.at[chunks], own_ref.at[chunks], in_sems.at[x]))
    key_other = jnp.concatenate([other_ref[blocks], other_ref[blocks + 1]], axis=1)
    out_copies = []
    for k in range(blocks):
        x, zh = k // NZH, k % NZH
        grad = lax.dot_general(other_ref[k], key_other, OVER_TOKENS, preferred_element_type=F32)
        if zh == 0:
            copies[x].wait()
        own = [own_ref[x * NY + y, zh * 128 : (zh + 1) * 128, :] for y in range(NY)]
        own = jnp.concatenate(
            [jnp.concatenate([part[0:64], part[64:128]], axis=1) for part in own], axis=0
        )
        term = (grad * grad * (1.0 / TOKENS) + own.astype(F32)).astype(BF16)
        out_copies += put_terms(k, term, out_ref, out_hbm, out_sems)
    for copy in out_copies:
        copy.wait()


def split_kernel(in_ref, out_ref):
    for zh in range(NZH):
        rows = slice(zh * 128, (zh + 1) * 128)
        total = in_ref[0, rows, :].astype(F32)
        for j in range(1, NX * NY):
            total += in_ref[j, rows, :].astype(F32)
        total = total.reshape(2, NZL, 8, COLS)
        for zl in range(NZL):
            both = jnp.concatenate([total[0, zl], total[1, zl]], axis=0)
            out_ref[zh * NZL + zl] = both.astype(BF16)


def serve_kernel(order_hbm, in_ref, out_ref, order_ref, sem):
    copy = start(order_hbm, order_ref, sem)
    total = in_ref[0].astype(F32)
    for z in range(1, NZH * NZL):
        total += in_ref[z].astype(F32)
    fisher = jnp.concatenate([total[0:8], total[8:16]], axis=1).astype(BF16)
    copy.wait()
    column = lax.broadcasted_iota(jnp.int32, (K, K), 0)
    pick = jnp.where(column == order_ref[...], 1.0, 0.0).astype(BF16)
    out_ref[...] = jnp.dot(fisher, pick, preferred_element_type=F32).astype(BF16)


def input_kernel(
    hidden_hbm, key_hbm, gain_hbm, inv_hbm, weight_0, weight_1, weight_3, weight_2,
    early_hbm, late_hbm, out_hbm,
    hidden_ref, key_ref, gain_ref, inv_ref, weight_ref, early_ref, late_ref, back_ref, out_ref,
    in_sems, out_sems,
):
    key_copy = start(key_hbm, key_ref, in_sems.at[0])
    core = my_core()
    z_here = lax.rem(lax.axis_index("fsdp"), NZL)
    y_here = lax.div(lax.axis_index("fsdp"), NZL)
    groups = (
        (weight_0, 0),
        (weight_1, 1),
        (weight_3, 7),
        (weight_2, jnp.where((z_here & 1) == 0, 2, 6)),
    )
    copies, blocks = [], []
    for i, (source, away) in enumerate(groups):
        size = source.shape[0]
        target = weight_ref.at[pl.ds(2 * len(blocks), size)]
        copies.append(start(source, target, in_sems.at[1 + i]))
        blocks += [(i, away, row) for row in range(0, size, 2)]
    second = [
        start(early_hbm, early_ref, in_sems.at[5]),
        start(late_hbm, late_ref, in_sems.at[6]),
        start(gain_hbm, gain_ref, in_sems.at[7]),
        start(inv_hbm, inv_ref, in_sems.at[8]),
        start(hidden_hbm, hidden_ref, in_sems.at[9]),
    ]

    def put(back, origin, away, row):
        zl = (z_here + origin + away) & (NZL - 1)
        for half in range(2):
            y = (y_here + row + half) & (NY - 1)
            cols = pl.ds(pl.multiple_of((y * NZL + zl) * 128, 128), 128)
            back_ref[:, cols] = back[:, half * 128 : (half + 1) * 128]

    key_copy.wait()
    keys = key_ref[...]
    waited = 0
    for block, (group, away, row) in enumerate(blocks):
        if waited == group:
            copies[group].wait()
            waited += 1
        weight = weight_ref[2 * block : 2 * block + 2].reshape(256, K)
        back = lax.dot_general(keys, weight, (((1,), (1,)), ((), ())), preferred_element_type=F32)
        put(back, 4 * core, away, row)
    second[0].wait()
    second[1].wait()
    early = early_ref.shape[0]
    for block, (_, away, row) in enumerate(blocks):
        back = early_ref[block] if block < early else late_ref[block - early]
        put(back.astype(F32), 4 * (1 - core), away, row)
    for copy in second[2:]:
        copy.wait()

    step, parts, width = 16, 4, 512

    def rows_of(i, carry):
        rows = pl.ds(pl.multiple_of(i * step, step), step)
        inv = inv_ref[rows, 0:1]
        total = jnp.zeros((step, width), F32)
        for t in range(0, D, width):
            cols = slice(t, t + width)
            du = back_ref[rows, cols] * gain_ref[:, cols]
            total += du * hidden_ref[rows, cols].astype(F32)
        mean = inv * jnp.sum(total, axis=-1, keepdims=True) * (1.0 / D)
        factor = inv * inv * mean
        for t in range(0, D, width):
            cols = slice(t, t + width)
            du = back_ref[rows, cols] * gain_ref[:, cols]
            out = du * inv - hidden_ref[rows, cols].astype(F32) * factor
            out_ref[rows, cols] = out.astype(BF16)
        return carry

    rows_each = SEQ // parts
    copies = []
    for i in range(parts):
        lax.fori_loop(i * rows_each // step, (i + 1) * rows_each // step, rows_of, 0, unroll=4)
        rows = pl.ds(i * rows_each, rows_each)
        copies.append(start(out_ref.at[rows], out_hbm.at[rows], out_sems.at[i]))
    for copy in copies:
        copy.wait()


def body(hidden_in, key_grad, key_weight, norm_gain, head_order):
    gain = norm_gain.reshape(1, D)
    vmem, hbm, any_ = pltpu.VMEM, pltpu.HBM, pl.ANY
    dma = pltpu.SemaphoreType.DMA
    blocks = NX * NZH
    barrier = lax.optimization_barrier

    with jax.named_scope("weight_z4"):
        origin = lax.ppermute(key_weight, AXES, origins())
    with jax.named_scope("norm"):
        own, send, inv = call(
            norm_kernel,
            (
                shape((NX * NY, 256, COLS)),
                shape((blocks + 2, SEQ, COLS)),
                shape((SEQ, 128), F32),
            ),
            (hidden_in, key_grad, gain),
            (any_,) * 3,
            (hbm, hbm, hbm),
            [
                pltpu.VMEM((SEQ, D), BF16),
                pltpu.VMEM((SEQ, K), BF16),
                pltpu.VMEM((1, D), F32),
                pltpu.VMEM((blocks, SEQ, COLS), BF16),
                pltpu.VMEM((blocks, SEQ, COLS), BF16),
                pltpu.VMEM((SEQ, 128), F32),
                pltpu.VMEM((blocks, NY, 128, COLS), BF16),
                dma((NORM_PARTS + 2,)),
                dma((NORM_PARTS + 3,)),
                dma((blocks, NY)),
            ],
            mib=None,
        )
        origin, send = barrier((origin, send))
        other = lax.ppermute(send, AXES, CORE_SWAP)
    with jax.named_scope("squares"):
        chunks = call(
            square_kernel,
            shape((NX * NY, 256, COLS)),
            (own, other),
            (any_, vmem),
            hbm,
            [
                pltpu.VMEM((NX * NY, 256, COLS), BF16),
                pltpu.VMEM((blocks, NY, 128, COLS), BF16),
                dma((NX,)),
                dma((blocks, NY)),
            ],
            mib=51,
        )
    with jax.named_scope("weight_y"):
        column = [origin] + [lax.ppermute(origin, AXES, from_y(ahead)) for ahead in (1, 2, 3)]
        chunks, *column = barrier((chunks, *column))
    with jax.named_scope("plane"):
        chunks = exchange(chunks, PLANES)
    with jax.named_scope("weight_y"):
        near = call(
            column_kernel, shape((NY, 128, K)), column, (any_,) * NY, hbm, [dma((NY,))], mib=52
        )
    with jax.named_scope("weight_z1"):
        up = lax.ppermute(near, AXES, from_z(1))
        down = lax.ppermute(near, AXES, from_z(-1))
        *now, up, down = barrier((near, up, down))
        far = lax.ppermute(now[0], AXES, two_away())
    with jax.named_scope("back_early"):
        early = lax.ppermute(partner(other, near, up, down), AXES, CORE_SWAP)
    with jax.named_scope("split"):
        parts = call(split_kernel, shape((NZH * NZL, 16, COLS)), (chunks,), (vmem,), vmem)
    with jax.named_scope("ring_z"):
        parts = exchange(parts, Z_RINGS)
    with jax.named_scope("back_late"):
        late = lax.ppermute(partner(other, far), AXES, CORE_SWAP)
    with jax.named_scope("input_grad"):
        weights = (near, up, down, far)
        input_grad = call(
            input_kernel,
            shape((SEQ, D)),
            (hidden_in, key_grad, gain, inv, *weights, early, late),
            (any_,) * 10,
            hbm,
            [
                pltpu.VMEM((SEQ, D), BF16),
                pltpu.VMEM((SEQ, K), BF16),
                pltpu.VMEM((1, D), F32),
                pltpu.VMEM((SEQ, 128), F32),
                pltpu.VMEM((16, 128, K), BF16),
                pltpu.VMEM((6, SEQ, COLS), BF16),
                pltpu.VMEM((2, SEQ, COLS), BF16),
                pltpu.VMEM((SEQ, D), F32),
                pltpu.VMEM((SEQ, D), BF16),
                dma((10,)),
                dma((4,)),
            ],
            mib=60,
        )
        parts, input_grad = barrier((parts, input_grad))
    with jax.named_scope("serve"):
        served = call(
            serve_kernel,
            shape((8, K)),
            (head_order.reshape(1, K), parts),
            (any_, vmem),
            vmem,
            [pltpu.VMEM((1, K), jnp.int32), dma],
        )
    return served, input_grad


def solution(mesh):
    in_specs = (P(AXES, None), P(AXES, None), P("fsdp", None), P(), P())
    out_specs = (P(AXES, None), P(AXES, None))
    return jax.shard_map(body, mesh=mesh, in_specs=in_specs, out_specs=out_specs, check_vma=False)
```

```python
import jax
import jax.numpy as jnp
from jax import lax
from jax.experimental import pallas as pl
from jax.experimental.pallas import tpu as pltpu
from jax.sharding import PartitionSpec as P

AXES = ("dp", "fsdp")
NX, NZH, NC, NY, NZL = 4, 2, 2, 4, 8
D, K = 4096, 512
SEQ = 256
TOKENS = SEQ * NX * NZH * NC * NY * NZL
COLS = 256
NORM_PARTS = 4
BF16, F32 = jnp.bfloat16, jnp.float32


def device(x, zh, c, y, zl):
    return (((x * NZH + zh) * NC + c) * NY + y) * NZL + zl


def places():
    return [
        (x, zh, c, y, zl)
        for x in range(NX)
        for zh in range(NZH)
        for c in range(NC)
        for y in range(NY)
        for zl in range(NZL)
    ]


def from_z(distance):
    pairs = []
    for x, zh, c, y, zl in places():
        z = (zh * NZL + zl + distance) % (NZH * NZL)
        pairs.append((device(x, z // NZL, c, y, z % NZL), device(x, zh, c, y, zl)))
    return pairs


def two_away():
    pairs = []
    for x, zh, c, y, zl in places():
        z = (zh * NZL + zl + (2 if zl % 2 == 0 else -2)) % (NZH * NZL)
        pairs.append((device(x, z // NZL, c, y, z % NZL), device(x, zh, c, y, zl)))
    return pairs


def from_y(ahead):
    return [
        (device(x, zh, c, (y + ahead) % NY, zl), device(x, zh, c, y, zl))
        for x, zh, c, y, zl in places()
    ]


def origins():
    pairs = []
    for x, zh, c, y, zl in places():
        z = (zh * NZL + zl + c * (4 if zl % 2 == 0 else -4)) % (NZH * NZL)
        pairs.append((device(x, z // NZL, c, y, z % NZL), device(x, zh, c, y, zl)))
    return pairs


PLANES = [
    [device(x, zh, c, y, zl) for x in range(NX) for y in range(NY)]
    for zh in range(NZH)
    for c in range(NC)
    for zl in range(NZL)
]
Z_RINGS = [
    [device(x, zh, c, y, zl) for zh in range(NZH) for zl in range(NZL)]
    for x in range(NX)
    for c in range(NC)
    for y in range(NY)
]
CORE_SWAP = [(device(x, zh, c, y, zl), device(x, zh, 1 - c, y, zl)) for x, zh, c, y, zl in places()]


def exchange(value, groups):
    return lax.all_to_all(
        value, AXES, split_axis=0, concat_axis=0, axis_index_groups=groups, tiled=True
    )


def call(kernel, outs, ins, in_spaces, out_spaces, scratch=(), mib=24, us=0.05):
    return pl.pallas_call(
        kernel,
        out_shape=outs,
        in_specs=[pl.BlockSpec(memory_space=space) for space in in_spaces],
        out_specs=jax.tree.map(lambda space: pl.BlockSpec(memory_space=space), out_spaces),
        scratch_shapes=list(scratch),
        compiler_params=pltpu.CompilerParams(vmem_limit_bytes=mib and mib * 2**20),
        cost_estimate=pl.CostEstimate(
            flops=0, bytes_accessed=int(us * 3.0e6), transcendentals=0
        ),
    )(*ins)


def my_core():
    return lax.rem(lax.axis_index("dp"), NC)


def shape(dims, dtype=BF16):
    return jax.ShapeDtypeStruct(dims, dtype)


def start(source, target, sem):
    copy = pltpu.make_async_copy(source, target, sem)
    copy.start()
    return copy


OVER_TOKENS = (((0,), (0,)), ((), ()))


def put_terms(k, term, ref, hbm, sems):
    x, zh = k // NZH, k % NZH
    copies = []
    for y in range(NY):
        rows = slice(y * 64, (y + 1) * 64)
        ref[k, y, 0:64, :] = term[rows, 0:COLS]
        ref[k, y, 64:128, :] = term[rows, COLS:K]
        target = hbm.at[x * NY + y, pl.ds(zh * 128, 128)]
        copies.append(start(ref.at[k, y], target, sems.at[k, y]))
    return copies


def norm_kernel(
    hidden_hbm, key_hbm, gain_hbm, term_hbm, send_hbm, inv_hbm,
    hidden_ref, key_ref, gain_ref, own_ref, send_ref, inv_ref, term_ref, in_sems, out_sems,
    term_sems,
):
    core = my_core()
    step, parts, blocks = 16, NORM_PARTS, NX * NZH
    rows_each = SEQ // parts
    pieces = [pl.ds(i * rows_each, rows_each) for i in range(parts)]
    gain_copy = start(gain_hbm, gain_ref, in_sems.at[parts])
    copies = [
        start(hidden_hbm.at[rows], hidden_ref.at[rows], in_sems.at[i])
        for i, rows in enumerate(pieces)
    ]
    key_copy = start(key_hbm, key_ref, in_sems.at[parts + 1])

    def rows_of(i, carry):
        rows = pl.ds(pl.multiple_of(i * step, step), step)
        squares = jnp.zeros((step, 512), F32)
        for t in range(0, D, 512):
            values = hidden_ref[rows, t : t + 512].astype(F32)
            squares += values * values
        inv = lax.rsqrt(jnp.sum(squares, axis=-1, keepdims=True) * (1.0 / D) + 1e-06)
        inv_ref[rows, :] = jnp.broadcast_to(inv, (step, 128))
        for ref, part in ((own_ref, core), (send_ref, 1 - core)):
            for k in range(blocks):
                cols = pl.ds(pl.multiple_of((2 * k + part) * COLS, COLS), COLS)
                unit = hidden_ref[rows, cols].astype(F32) * inv
                ref[k, rows, :] = (unit * gain_ref[:, cols]).astype(BF16)
        return carry

    gain_copy.wait()
    out_copies = []
    for i, rows in enumerate(pieces):
        copies[i].wait()
        lax.fori_loop(i * rows_each // step, (i + 1) * rows_each // step, rows_of, 0, unroll=4)
        target = send_hbm.at[pl.ds(0, blocks), rows]
        out_copies.append(start(send_ref.at[:, rows], target, out_sems.at[i]))
    key_copy.wait()
    for half in range(2):
        source = key_ref.at[:, pl.ds(half * COLS, COLS)]
        out_copies.append(start(source, send_hbm.at[blocks + half], out_sems.at[parts + half]))
    out_copies.append(start(inv_ref, inv_hbm, out_sems.at[parts + 2]))
    for k in range(blocks):
        grad = lax.dot_general(own_ref[k], key_ref[...], OVER_TOKENS, preferred_element_type=F32)
        term = (grad * grad * (1.0 / TOKENS)).astype(BF16)
        out_copies += put_terms(k, term, term_ref, term_hbm, term_sems)
    for copy in out_copies:
        copy.wait()


def column_kernel(*refs):
    *blocks, out_hbm, sems = refs
    copies = [start(block, out_hbm.at[j], sems.at[j]) for j, block in enumerate(blocks)]
    for copy in copies:
        copy.wait()


def partner_kernel(key_hbm, *refs):
    *sources, out_hbm, key_ref, weight_ref, out_ref, in_sems, out_sems = refs
    key_copy = start(key_hbm.at[pl.ds(NX * NZH, 2)], key_ref, in_sems.at[0])
    copies, place = [], 0
    for i, source in enumerate(sources):
        size = source.shape[0]
        target = weight_ref.at[pl.ds(place, size)]
        copies.append((start(source, target, in_sems.at[1 + i]), place // 2, size // 2))
        place += size
    key_copy.wait()
    keys = jnp.concatenate([key_ref[0], key_ref[1]], axis=1)
    out_copies = []
    for copy, first, size in copies:
        copy.wait()
        for block in range(first, first + size):
            weight = weight_ref[2 * block : 2 * block + 2].reshape(256, K)
            back = lax.dot_general(
                keys, weight, (((1,), (1,)), ((), ())), preferred_element_type=F32
            )
            out_ref[block] = back.astype(BF16)
            out_copies.append(start(out_ref.at[block], out_hbm.at[block], out_sems.at[block]))
    for copy in out_copies:
        copy.wait()


def partner(other, *sources):
    size = sum(source.shape[0] for source in sources)
    dma = pltpu.SemaphoreType.DMA
    return call(
        partner_kernel,
        shape((size // 2, SEQ, COLS)),
        (other, *sources),
        (pl.ANY,) * (1 + len(sources)),
        pltpu.HBM,
        [
            pltpu.VMEM((2, SEQ, COLS), BF16),
            pltpu.VMEM((size, 128, K), BF16),
            pltpu.VMEM((size // 2, SEQ, COLS), BF16),
            dma((1 + len(sources),)),
            dma((size // 2,)),
        ],
        mib=52,
    )


def square_kernel(
    own_hbm, other_ref, out_hbm, own_ref, out_ref, in_sems, out_sems
):
    blocks = NX * NZH
    copies = []
    for x in range(NX):
        chunks = pl.ds(NY * x, NY)
        copies.append(start(own_hbm.at[chunks], own_ref.at[chunks], in_sems.at[x]))
    key_other = jnp.concatenate([other_ref[blocks], other_ref[blocks + 1]], axis=1)
    out_copies = []
    for k in range(blocks):
        x, zh = k // NZH, k % NZH
        grad = lax.dot_general(other_ref[k], key_other, OVER_TOKENS, preferred_element_type=F32)
        if zh == 0:
            copies[x].wait()
        own = [own_ref[x * NY + y, zh * 128 : (zh + 1) * 128, :] for y in range(NY)]
        own = jnp.concatenate(
            [jnp.concatenate([part[0:64], part[64:128]], axis=1) for part in own], axis=0
        )
        term = (grad * grad * (1.0 / TOKENS) + own.astype(F32)).astype(BF16)
        out_copies += put_terms(k, term, out_ref, out_hbm, out_sems)
    for copy in out_copies:
        copy.wait()


def split_kernel(in_ref, out_ref):
    for zh in range(NZH):
        rows = slice(zh * 128, (zh + 1) * 128)
        total = in_ref[0, rows, :].astype(F32)
        for j in range(1, NX * NY):
            total += in_ref[j, rows, :].astype(F32)
        total = total.reshape(2, NZL, 8, COLS)
        for zl in range(NZL):
            both = jnp.concatenate([total[0, zl], total[1, zl]], axis=0)
            out_ref[zh * NZL + zl] = both.astype(BF16)


def serve_kernel(order_hbm, in_ref, out_ref, order_ref, sem):
    copy = start(order_hbm, order_ref, sem)
    total = in_ref[0].astype(F32)
    for z in range(1, NZH * NZL):
        total += in_ref[z].astype(F32)
    fisher = jnp.concatenate([total[0:8], total[8:16]], axis=1).astype(BF16)
    copy.wait()
    column = lax.broadcasted_iota(jnp.int32, (K, K), 0)
    pick = jnp.where(column == order_ref[...], 1.0, 0.0).astype(BF16)
    out_ref[...] = jnp.dot(fisher, pick, preferred_element_type=F32).astype(BF16)


def input_kernel(
    hidden_hbm, key_hbm, gain_hbm, inv_hbm, weight_0, weight_1, weight_3, weight_2,
    early_hbm, late_hbm, out_hbm,
    hidden_ref, key_ref, gain_ref, inv_ref, weight_ref, early_ref, late_ref, back_ref, out_ref,
    in_sems, out_sems,
):
    key_copy = start(key_hbm, key_ref, in_sems.at[0])
    core = my_core()
    z_here = lax.rem(lax.axis_index("fsdp"), NZL)
    y_here = lax.div(lax.axis_index("fsdp"), NZL)
    groups = (
        (weight_0, 0),
        (weight_1, 1),
        (weight_3, 7),
        (weight_2, jnp.where((z_here & 1) == 0, 2, 6)),
    )
    copies, blocks = [], []
    for i, (source, away) in enumerate(groups):
        size = source.shape[0]
        target = weight_ref.at[pl.ds(2 * len(blocks), size)]
        copies.append(start(source, target, in_sems.at[1 + i]))
        blocks += [(i, away, row) for row in range(0, size, 2)]
    second = [
        start(early_hbm, early_ref, in_sems.at[5]),
        start(late_hbm, late_ref, in_sems.at[6]),
        start(gain_hbm, gain_ref, in_sems.at[7]),
        start(inv_hbm, inv_ref, in_sems.at[8]),
        start(hidden_hbm, hidden_ref, in_sems.at[9]),
    ]

    def put(back, origin, away, row):
        zl = (z_here + origin + away) & (NZL - 1)
        for half in range(2):
            y = (y_here + row + half) & (NY - 1)
            cols = pl.ds(pl.multiple_of((y * NZL + zl) * 128, 128), 128)
            back_ref[:, cols] = back[:, half * 128 : (half + 1) * 128]

    key_copy.wait()
    keys = key_ref[...]
    waited = 0
    for block, (group, away, row) in enumerate(blocks):
        if waited == group:
            copies[group].wait()
            waited += 1
        weight = weight_ref[2 * block : 2 * block + 2].reshape(256, K)
        back = lax.dot_general(keys, weight, (((1,), (1,)), ((), ())), preferred_element_type=F32)
        put(back, 4 * core, away, row)
    second[0].wait()
    second[1].wait()
    early = early_ref.shape[0]
    for block, (_, away, row) in enumerate(blocks):
        back = early_ref[block] if block < early else late_ref[block - early]
        put(back.astype(F32), 4 * (1 - core), away, row)
    for copy in second[2:]:
        copy.wait()

    step, parts, width = 16, 4, 512

    def rows_of(i, carry):
        rows = pl.ds(pl.multiple_of(i * step, step), step)
        inv = inv_ref[rows, 0:1]
        total = jnp.zeros((step, width), F32)
        for t in range(0, D, width):
            cols = slice(t, t + width)
            du = back_ref[rows, cols] * gain_ref[:, cols]
            total += du * hidden_ref[rows, cols].astype(F32)
        mean = inv * jnp.sum(total, axis=-1, keepdims=True) * (1.0 / D)
        factor = inv * inv * mean
        for t in range(0, D, width):
            cols = slice(t, t + width)
            du = back_ref[rows, cols] * gain_ref[:, cols]
            out = du * inv - hidden_ref[rows, cols].astype(F32) * factor
            out_ref[rows, cols] = out.astype(BF16)
        return carry

    rows_each = SEQ // parts
    copies = []
    for i in range(parts):
        lax.fori_loop(i * rows_each // step, (i + 1) * rows_each // step, rows_of, 0, unroll=4)
        rows = pl.ds(i * rows_each, rows_each)
        copies.append(start(out_ref.at[rows], out_hbm.at[rows], out_sems.at[i]))
    for copy in copies:
        copy.wait()


def body(hidden_in, key_grad, key_weight, norm_gain, head_order):
    gain = norm_gain.reshape(1, D)
    vmem, hbm, any_ = pltpu.VMEM, pltpu.HBM, pl.ANY
    dma = pltpu.SemaphoreType.DMA
    blocks = NX * NZH
    barrier = lax.optimization_barrier

    with jax.named_scope("weight_z4"):
        origin = lax.ppermute(key_weight, AXES, origins())
    with jax.named_scope("norm"):
        own, send, inv = call(
            norm_kernel,
            (
                shape((NX * NY, 256, COLS)),
                shape((blocks + 2, SEQ, COLS)),
                shape((SEQ, 128), F32),
            ),
            (hidden_in, key_grad, gain),
            (any_,) * 3,
            (hbm, hbm, hbm),
            [
                pltpu.VMEM((SEQ, D), BF16),
                pltpu.VMEM((SEQ, K), BF16),
                pltpu.VMEM((1, D), F32),
                pltpu.VMEM((blocks, SEQ, COLS), BF16),
                pltpu.VMEM((blocks, SEQ, COLS), BF16),
                pltpu.VMEM((SEQ, 128), F32),
                pltpu.VMEM((blocks, NY, 128, COLS), BF16),
                dma((NORM_PARTS + 2,)),
                dma((NORM_PARTS + 3,)),
                dma((blocks, NY)),
            ],
            mib=None,
        )
        origin, send = barrier((origin, send))
        other = lax.ppermute(send, AXES, CORE_SWAP)
    with jax.named_scope("squares"):
        chunks = call(
            square_kernel,
            shape((NX * NY, 256, COLS)),
            (own, other),
            (any_, vmem),
            hbm,
            [
                pltpu.VMEM((NX * NY, 256, COLS), BF16),
                pltpu.VMEM((blocks, NY, 128, COLS), BF16),
                dma((NX,)),
                dma((blocks, NY)),
            ],
            mib=51,
        )
    with jax.named_scope("weight_y"):
        column = [origin] + [lax.ppermute(origin, AXES, from_y(ahead)) for ahead in (1, 2, 3)]
        chunks, *column = barrier((chunks, *column))
    with jax.named_scope("plane"):
        chunks = exchange(chunks, PLANES)
    with jax.named_scope("weight_y"):
        near = call(
            column_kernel, shape((NY, 128, K)), column, (any_,) * NY, hbm, [dma((NY,))], mib=52
        )
    with jax.named_scope("weight_z1"):
        up = lax.ppermute(near, AXES, from_z(1))
        down = lax.ppermute(near, AXES, from_z(-1))
        products = partner(other, near, up, down)
        now, products = barrier((near, products))
        far = lax.ppermute(now, AXES, two_away())
    with jax.named_scope("back_early"):
        early = lax.ppermute(products, AXES, CORE_SWAP)
    with jax.named_scope("split"):
        parts = call(split_kernel, shape((NZH * NZL, 16, COLS)), (chunks,), (vmem,), vmem)
    with jax.named_scope("ring_z"):
        parts = exchange(parts, Z_RINGS)
    with jax.named_scope("back_late"):
        late = lax.ppermute(partner(other, far), AXES, CORE_SWAP)
    with jax.named_scope("input_grad"):
        weights = (near, up, down, far)
        input_grad = call(
            input_kernel,
            shape((SEQ, D)),
            (hidden_in, key_grad, gain, inv, *weights, early, late),
            (any_,) * 10,
            hbm,
            [
                pltpu.VMEM((SEQ, D), BF16),
                pltpu.VMEM((SEQ, K), BF16),
                pltpu.VMEM((1, D), F32),
                pltpu.VMEM((SEQ, 128), F32),
                pltpu.VMEM((16, 128, K), BF16),
                pltpu.VMEM((6, SEQ, COLS), BF16),
                pltpu.VMEM((2, SEQ, COLS), BF16),
                pltpu.VMEM((SEQ, D), F32),
                pltpu.VMEM((SEQ, D), BF16),
                dma((10,)),
                dma((4,)),
            ],
            mib=60,
        )
        parts, input_grad = barrier((parts, input_grad))
    with jax.named_scope("serve"):
        served = call(
            serve_kernel,
            shape((8, K)),
            (head_order.reshape(1, K), parts),
            (any_, vmem),
            vmem,
            [pltpu.VMEM((1, K), jnp.int32), dma],
        )
    return served, input_grad


def solution(mesh):
    in_specs = (P(AXES, None), P(AXES, None), P("fsdp", None), P(), P())
    out_specs = (P(AXES, None), P(AXES, None))
    return jax.shard_map(body, mesh=mesh, in_specs=in_specs, out_specs=out_specs, check_vma=False)
```
